32 devices in a mesh: seq: 8 (over y, x, core), wa: 4 (over z).
Axes of the slice: x: 2, y: 2, z: 4, core: 2. Of those that a mesh axis runs over, the one named last changes fastest.
Arguments:
- tokens: bfloat16 [4, 4096, 1024], P('wa', 'seq'), may hold values from -6 to 6
- in_weight: bfloat16 [2, 1024, 4384], P(None, 'wa'), may hold values from -0.1875 to 0.1875
- out_weight: bfloat16 [2, 2048, 1024], P(None, 'wa'), may hold values from -0.125 to 0.125
- conv_weight: bfloat16 [2, 4, 2304], P(None, None, 'wa'), may hold values from -3 to 3
- conv_bias: bfloat16 [2, 2304], P(None, 'wa'), may hold values from -4 to 4
- a_log: bfloat16 [2, 32], P(None, 'wa'), may hold values from -4.59375 to 2
- dt_bias: bfloat16 [2, 32], P(None, 'wa'), may hold values from -6 to -4
- skip_d: bfloat16 [2, 32], P(None, 'wa'), may hold values from 0.5 to 1.5
- norm_gain: bfloat16 [2, 1024], P(None, 'wa'), may hold values from 0.5 to 1.5
- gated_gain: bfloat16 [2, 2048], P(None, 'wa'), may hold values from 0.5 to 1.5
- doc_start: int32 [4, 4096], P('wa', 'seq'), may hold values from 0 to 4095, as said below
- cotangent: bfloat16 [4, 4096, 1024], P('wa', 'seq'), may hold values from -6 to 6
Outputs:
- mixed_out: bfloat16 [4, 4096, 1024], P('wa', 'seq')
- input_grad: float32 [4, 4096, 1024], P('wa', 'seq')
- in_weight_grad: float32 [2, 1024, 4384], P(None, 'wa')
- out_weight_grad: float32 [2, 2048, 1024], P(None, 'wa')
- conv_weight_grad: float32 [2, 4, 2304], P(None, None, 'wa')
- conv_bias_grad: float32 [2, 2304], P(None, 'wa')
- a_log_grad: float32 [2, 32], P(None, 'wa')
- dt_bias_grad: float32 [2, 32], P(None, 'wa')
- skip_grad: float32 [2, 32], P(None, 'wa')
- norm_gain_grad: float32 [2, 1024], P(None, 'wa')
- gated_gain_grad: float32 [2, 2048], P(None, 'wa')
The draws below stay inside these ranges and needn't reach their ends.
Inputs may be any that keep to these rules, and one draw needn't show every extreme that they name: doc_start[s, t] is the first position of the document that holds position t of sequence s: doc_start[s, t] <= t, constant on each document, and a document starts at position 0; in one sequence, which one drawn from the seed, one document begins within the first 512 positions and ends within the last 512; in the other sequences documents begin at scattered positions along the whole sequence; the last position of every sequence begins a document of its own.
All inputs are finite; a program needn't handle non-finite values.
Results may differ from the reference program's by a relative error of at most 0.02.
Values may be sent and summed in bfloat16 or wider, within the bound.
No kernel may reach another device: no remote copies, remote signals or barrier semaphores. Data moves between devices by JAX's collectives and lax.ppermute only.
A program may use at most 320 MiB of HBM per device.

```python
import jax
import jax.numpy as jnp
from jax import lax

D = 1024
HEADS = 32
HEADDIM = 64
STATE = 128
KCONV = 4
BLOCK = 256
LAYERS = 2
TOK_DEV = 512
INNER = 2048
CONVCH = 2304
PROJ = 4384
SEQS = 4
SEQ_LEN = 4096


def draw_doc_start(key, part):
    key = jax.random.fold_in(key, 11)
    chosen_key, first_key, last_key, extra_key = jax.random.split(key, 4)
    chosen = jax.random.randint(chosen_key, (), 0, SEQS)
    rows = jnp.arange(SEQS, dtype=jnp.int32)[:, None]
    spanning = rows == chosen
    opening = jax.random.randint(first_key, (SEQS, 1), 1, TOK_DEV)
    closing = jax.random.randint(last_key, (SEQS, 1), SEQ_LEN - TOK_DEV + 1, SEQ_LEN)
    position = jnp.arange(SEQ_LEN, dtype=jnp.int32)[None, :]
    extra = jax.random.randint(extra_key, (SEQS, SEQ_LEN), 0, 2 * TOK_DEV) == 0
    outside = (position < opening) | (position > closing)
    long_begins = (position == opening) | (position == closing) | extra & outside
    begins = jnp.where(spanning, long_begins, extra)
    begins = begins | (position == 0) | (position == SEQ_LEN - 1)
    marked = jnp.where(begins, position, 0).astype(jnp.int32)
    return lax.cummax(marked, axis=1)


def shard_levels(key, extent, cuts, least, high):
    def one(axis_at, shards_of):
        draws = jax.random.uniform(jax.random.fold_in(jax.random.fold_in(key, 6), axis_at), (shards_of,), jnp.float32, least / len(cuts), high / len(cuts))
        return jnp.repeat(jnp.exp(draws), extent[axis_at] // shards_of).reshape((-1,) + (1,) * (len(extent) - axis_at - 1))

    factor_of = one(*cuts[0])
    for cut in cuts[1:]:
        factor_of = factor_of * one(*cut)
    return factor_of


def bell_draw(own_key, extent, deviation, most, cuts=(), kind=jnp.bfloat16):
    factor_of = shard_levels(own_key, extent, cuts, -0.22, 0.18) if cuts else 1.0
    entries = jax.random.normal(own_key, extent, jnp.float32) * deviation * factor_of
    return jnp.minimum(jnp.maximum(entries, -most), most).astype(kind)


def setup_inputs(seed: int = 0) -> dict:
    seeds = jax.random.split(jax.random.key(seed), 13)
    return {
        "tokens": bell_draw(seeds[0], (SEQS, SEQ_LEN, D), 1.0, 6.0, ((0, 4), (1, 8))),
        "in_weight": bell_draw(seeds[1], (LAYERS, D, PROJ), D ** -0.5, 0.1875, ((1, 4),)),
        "out_weight": bell_draw(seeds[2], (LAYERS, INNER, D), INNER ** -0.5, 0.125, ((1, 4),)),
        "conv_weight": bell_draw(seeds[3], (LAYERS, KCONV, CONVCH), KCONV ** -0.5, 3.0, ((2, 4),)),
        "conv_bias": bell_draw(seeds[4], (LAYERS, CONVCH), 0.3, 4.0, ((1, 4),)),
        "a_log": jnp.clip(-4.59375 + 6.59375 * jax.random.uniform(seeds[5], (LAYERS, HEADS), jnp.float32) ** shard_levels(seeds[5], (LAYERS, HEADS), ((1, 4),), -0.2, 0.2), -4.59375, 2.0).astype(jnp.bfloat16),
        "dt_bias": jnp.clip(-6.0 + 2.0 * jax.random.uniform(seeds[6], (LAYERS, HEADS), jnp.float32) ** shard_levels(seeds[6], (LAYERS, HEADS), ((1, 4),), -0.2, 0.2), -6.0, -4.0).astype(jnp.bfloat16),
        "skip_d": jnp.clip(0.5 + 1.0 * jax.random.uniform(seeds[7], (LAYERS, HEADS), jnp.float32) ** shard_levels(seeds[7], (LAYERS, HEADS), ((1, 4),), -0.2, 0.2), 0.5, 1.5).astype(jnp.bfloat16),
        "norm_gain": jnp.clip(1.0 + 0.1 * jax.random.normal(seeds[8], (LAYERS, D), jnp.float32), 0.5, 1.5).astype(jnp.bfloat16),
        "gated_gain": jnp.clip(1.0 + 0.1 * jax.random.normal(seeds[9], (LAYERS, INNER), jnp.float32), 0.5, 1.5).astype(jnp.bfloat16),
        "doc_start": draw_doc_start(jax.random.fold_in(seeds[12], 71), 0),
        "cotangent": bell_draw(seeds[11], (SEQS, SEQ_LEN, D), 1.0, 6.0, ((0, 4), (1, 8))),
    }


EPSILON = 1e-05
PRECISE = lax.Precision.HIGHEST

@jax.custom_vjp
def low(v):
    return lax.optimization_barrier(v.astype(jnp.bfloat16)).astype(jnp.float32)

@jax.custom_vjp
def low_back(v):
    return v

def low_keep(v):
    return (low(v), None)

def low_pass(kept, grad):
    return (grad,)

def back_keep(v):
    return (v, None)

def back_low(kept, grad):
    return (low(grad),)
low.defvjp(low_keep, low_pass)
low_back.defvjp(back_keep, back_low)

def rms_scale(value, gain):
    mean_sq = lax.optimization_barrier(jnp.mean(value * value, axis=-1, keepdims=True))
    return value * lax.rsqrt(mean_sq + EPSILON) * gain

def block_mix(state, pieces, rate, skip):
    x_heads, b_proj, c_proj, step, starts, position = pieces
    begin = position[0]
    log_decay = jnp.cumsum(step * rate[None, :], axis=0)
    allowed = (position[None, :] <= position[:, None]) & (position[None, :] >= starts[:, None])
    allowed = allowed[None]
    decay_t = log_decay.T
    gaps = decay_t[:, :, None] - decay_t[:, None, :]
    weights = jnp.where(allowed, jnp.exp(jnp.where(allowed, gaps, 0.0)), 0.0)
    cross = jnp.dot(c_proj, b_proj.T, precision=PRECISE)
    scores = cross[None] * weights * step.T[:, None, :]
    intra = jnp.einsum('hij,jhp->ihp', scores, x_heads, precision=PRECISE)
    reach = (starts < begin).astype(jnp.float32)
    inter = jnp.exp(log_decay)[:, :, None] * reach[:, None, None] * jnp.einsum('in,hpn->ihp', c_proj, state, precision=PRECISE)
    mixed = intra + inter + skip[None, :, None] * x_heads
    decay = jnp.exp(log_decay[-1]) * reach[-1]
    keep_end = (position >= starts[-1]).astype(jnp.float32)[:, None]
    end_weight = keep_end * jnp.exp(log_decay[-1][None, :] - log_decay) * step
    fresh = jnp.einsum('jhp,jn->hpn', end_weight[:, :, None] * x_heads, b_proj, precision=PRECISE)
    return (decay[:, None, None] * state + fresh, mixed)

def sequence_mix(conv_in, step_raw, starts, conv_w, conv_b, rate, dt_bias, skip):
    length, heads = step_raw.shape
    taps = conv_w.shape[0]
    inner = heads * HEADDIM
    blocks = length // BLOCK
    position = jnp.arange(length, dtype=jnp.int32)
    padded = jnp.concatenate([jnp.zeros((taps - 1, conv_in.shape[1]), jnp.float32), conv_in], axis=0)
    conv = jnp.zeros((length, conv_in.shape[1]), jnp.float32) + conv_b[None, :]
    for tap in range(taps):
        keep = (position - (taps - 1) + tap >= starts).astype(jnp.float32)[:, None]
        conv = conv + conv_w[tap][None, :] * padded[tap:tap + length] * keep
    act = jax.nn.silu(conv)
    x_heads = act[:, :inner].reshape(blocks, BLOCK, heads, HEADDIM)
    b_proj = act[:, inner:inner + STATE].reshape(blocks, BLOCK, STATE)
    c_proj = act[:, inner + STATE:].reshape(blocks, BLOCK, STATE)
    step = jax.nn.softplus(step_raw + dt_bias[None, :]).reshape(blocks, BLOCK, heads)
    advance = jax.checkpoint(lambda state, pieces: block_mix(state, pieces, rate, skip))
    start_state = jnp.zeros((heads, HEADDIM, STATE), jnp.float32)
    pieces = (x_heads, b_proj, c_proj, step, starts.reshape(blocks, BLOCK), position.reshape(blocks, BLOCK))
    unused, mixed = lax.scan(advance, start_state, pieces)
    return mixed.reshape(length, inner)

def layer_pass(resid, doc_start, weight_in, weight_out, conv_w, conv_b, a_log, dt_bias, skip, norm_gain, gated_gain):
    normed = low(rms_scale(resid, norm_gain))
    proj = low_back(jnp.einsum('std,df->stf', normed, weight_in, precision=PRECISE))
    inner = weight_out.shape[0]
    channels = conv_w.shape[1]
    gate_in = proj[..., :inner]
    conv_in = proj[..., inner:inner + channels]
    step_raw = proj[..., inner + channels:]
    rate = -jnp.exp(a_log)
    mixer = jax.vmap(sequence_mix, in_axes=(0, 0, 0, None, None, None, None, None))
    mixed = mixer(conv_in, step_raw, doc_start, conv_w, conv_b, rate, dt_bias, skip)
    gated = low(rms_scale(mixed * jax.nn.silu(gate_in), gated_gain))
    branch = low_back(jnp.einsum('sti,id->std', gated, weight_out, precision=PRECISE))
    return resid + branch

def reference(tokens, in_weight, out_weight, conv_weight, conv_bias, a_log, dt_bias, skip_d, norm_gain, gated_gain, doc_start, cotangent):

    def forward(resid, weight_in, weight_out, conv_w, conv_b, log_rate, step_bias, skip, gain_in, gain_gated):
        for layer in range(LAYERS):
            resid = layer_pass(resid, doc_start, weight_in[layer], weight_out[layer], conv_w[layer], conv_b[layer], log_rate[layer], step_bias[layer], skip[layer], gain_in[layer], gain_gated[layer])
        return resid
    result, pullback = jax.vjp(forward, tokens.astype(jnp.float32), in_weight.astype(jnp.float32), out_weight.astype(jnp.float32), conv_weight.astype(jnp.float32), conv_bias.astype(jnp.float32), a_log.astype(jnp.float32), dt_bias.astype(jnp.float32), skip_d.astype(jnp.float32), norm_gain.astype(jnp.float32), gated_gain.astype(jnp.float32))
    grads = pullback(cotangent.astype(jnp.float32))
    return (result.astype(jnp.bfloat16), grads[0], grads[1], grads[2], grads[3], grads[4], grads[5], grads[6], grads[7], grads[8], grads[9])
```

```python
import functools

import jax
import jax.numpy as jnp
from jax import lax
from jax.experimental import pallas as pl
from jax.experimental.pallas import tpu as pltpu
from jax.sharding import PartitionSpec as P

HEADDIM = 64
STATE = 128
BLOCK = 256
TILE = 256
PER = TILE // HEADDIM
RIM = 16
EPSILON = 1e-05
PRECISE = lax.Precision.HIGHEST
f32 = jnp.float32
bf16 = jnp.bfloat16
FAR = -1e30


def dot(a, b, ca=1, cb=0, precision=None):
    return lax.dot_general(
        a, b, (((ca,), (cb,)), ((), ())), precision=precision, preferred_element_type=f32
    )


def iota(shape, axis):
    return lax.broadcasted_iota(jnp.int32, shape, axis)


def logistic(v):
    return 1.0 / (1.0 + jnp.exp(-v))


def silu(v):
    return v * logistic(v)


def dsilu(v):
    s = logistic(v)
    return s * (1.0 + v * (1.0 - s))


def split(q):
    high = q.astype(bf16)
    return jnp.concatenate([high, (q - high.astype(f32)).astype(bf16)], axis=1)


def spread(pair, group):
    rows = iota((2 * STATE, TILE), 0) % STATE
    cols = PER * group + iota((2 * STATE, TILE), 1) // HEADDIM
    return dot(pair, (rows == cols).astype(f32).astype(bf16))


def chooser(group):
    return iota((TILE, STATE), 1) == PER * group + iota((TILE, STATE), 0) // HEADDIM


def gather_heads(z, group):
    pick = chooser(group).astype(f32).astype(bf16)
    high = z.astype(bf16)
    low = (z - high.astype(f32)).astype(bf16)
    return dot(high, pick) + dot(low, pick)


def head_rows(row, group):
    return jnp.sum(jnp.where(chooser(group), row, 0.0), axis=1, keepdims=True)


def lower(n):
    return iota((n, n), 0) >= iota((n, n), 1)


def block_of(b):
    return slice(b * BLOCK, (b + 1) * BLOCK)


def end_weights(starts, lam, b):
    s = block_of(b)
    last = (b + 1) * BLOCK - 1
    place = b * BLOCK + iota((BLOCK, 1), 0)
    keep = place >= starts[last : last + 1]
    return jnp.where(keep, jnp.exp(lam[last : last + 1] - lam[s]), 0.0)


def reach_weights(starts, lam, b):
    s = block_of(b)
    return jnp.where(starts[s] < b * BLOCK, jnp.exp(lam[s]), 0.0)


def fill_mask(mask_ref, starts, blocks):
    for b in range(blocks):
        t = b * BLOCK + iota((BLOCK, BLOCK), 0)
        s = b * BLOCK + iota((BLOCK, BLOCK), 1)
        mask_ref[b] = jnp.where((s <= t) & (s >= starts[block_of(b)]), 0.0, FAR)


def first_kernel(
    nrm_ref, w_ref, cw_ref, cb_ref, dtb_ref, rate_ref, starts_ref,
    cin_ref, cv_ref, dt_ref, lam_ref, sig_ref, lamt_ref, state_ref, fresh_ref, dec_ref, nrmt_ref,
    b_sc, e_sc,
):
    step = pl.program_id(0)
    length = starts_ref.shape[0]
    blocks = length // BLOCK
    heads = lamt_ref.shape[0] * PER
    starts = starts_ref[...]

    def conv():
        pe = dot(nrm_ref[...], w_ref[...])
        cin_ref[...] = pe.astype(bf16)
        place = iota((length, 1), 0)
        taps = cw_ref.shape[0]
        acc = cb_ref[...] + cw_ref[taps - 1 : taps] * pe[RIM:]
        for k in range(taps - 1):
            back = taps - 1 - k
            keep = place - back >= starts
            acc = acc + jnp.where(keep, cw_ref[k : k + 1] * pltpu.roll(pe, back, 0)[RIM:], 0.0)
        cv = acc.astype(bf16)
        cv_ref[...] = cv
        return silu(cv.astype(f32))

    @pl.when(step == 0)
    def _():
        act = conv()
        b_sc[...] = act[:, :STATE].astype(bf16)
        nrmt_ref[...] = nrm_ref[...].T

    @pl.when(step == 1)
    def _():
        z = dot(nrm_ref[RIM:], w_ref[:, :STATE]) + dtb_ref[...]
        live = iota(z.shape, 1) < heads
        dt = jnp.where(live, jnp.maximum(z, 0.0) + jnp.log1p(jnp.exp(-jnp.abs(z))), 0.0)
        dt_ref[...] = dt
        sig_ref[...] = jnp.where(live, logistic(z), 0.0)
        change = dt * rate_ref[...]
        tri = lower(BLOCK).astype(f32)
        lam = jnp.concatenate(
            [dot(tri, change[block_of(b)], precision=PRECISE) for b in range(blocks)], axis=0
        )
        lam_ref[...] = lam
        across = lam.T
        for g in range(lamt_ref.shape[0]):
            lamt_ref[g] = across[PER * g : PER * (g + 1)]
        total = None
        rows = []
        for b in range(blocks):
            e_sc[block_of(b)] = split(end_weights(starts, lam, b) * dt[block_of(b)])
            last = (b + 1) * BLOCK - 1
            decay = jnp.where(
                starts[last : last + 1] < b * BLOCK, jnp.exp(lam[last : last + 1]), 0.0
            )
            decay = jnp.where(iota(decay.shape, 1) < heads, decay, 0.0)
            rows.append(decay)
            total = decay if total is None else total * decay
        rows.append(total)
        rows.append(jnp.zeros((8 - len(rows), STATE), f32))
        dec_ref[...] = jnp.concatenate(rows, axis=0)

    @pl.when(step >= 2)
    def _():
        group = step - 2
        xe = (conv() * spread(e_sc[...], group)).astype(bf16)
        total = None
        for b in range(blocks):
            fresh = dot(xe[block_of(b)], b_sc[block_of(b)], 0, 0)
            if b + 1 < blocks:
                fresh_ref[b] = fresh
            if total is None:
                total = fresh
            else:
                total = head_rows(dec_ref[b : b + 1], group) * total + fresh
        state_ref[...] = total.astype(state_ref.dtype)


def first(nrm, w_in, cw, cb, dtb, rate, starts, heads):
    ext, d = nrm.shape
    length = starts.shape[0]
    blocks = length // BLOCK
    inner = heads * HEADDIM
    groups = inner // TILE
    conv_at = inner // TILE
    bc = 2 * groups
    col = lambda s: jnp.where(s == 0, groups, jnp.maximum(s - 2, 0))
    wcol = lambda s: jnp.where(s < 2, bc + s, conv_at + s - 2)
    tile = lambda s: jnp.maximum(s - 2, 0)
    full = lambda *shape: pl.BlockSpec(shape, lambda s: (0,) * len(shape))
    return pl.pallas_call(
        first_kernel,
        grid=(groups + 2,),
        in_specs=[
            full(ext, d),
            pl.BlockSpec((d, TILE), lambda s: (0, wcol(s))),
            pl.BlockSpec((cw.shape[0], TILE), lambda s: (0, col(s))),
            pl.BlockSpec((1, TILE), lambda s: (0, col(s))),
            full(1, STATE),
            full(1, STATE),
            full(length, 1),
        ],
        out_specs=[
            pl.BlockSpec((ext, TILE), lambda s: (0, col(s))),
            pl.BlockSpec((length, TILE), lambda s: (0, col(s))),
            full(length, STATE),
            full(length, STATE),
            full(length, STATE),
            full(groups, PER, length),
            pl.BlockSpec((TILE, STATE), lambda s: (tile(s), 0)),
            pl.BlockSpec((blocks - 1, TILE, STATE), lambda s: (0, tile(s), 0)),
            full(8, STATE),
            full(d, ext),
        ],
        out_shape=[
            jax.ShapeDtypeStruct((ext, inner + 2 * STATE), bf16),
            jax.ShapeDtypeStruct((length, inner + 2 * STATE), bf16),
            jax.ShapeDtypeStruct((length, STATE), f32),
            jax.ShapeDtypeStruct((length, STATE), f32),
            jax.ShapeDtypeStruct((length, STATE), f32),
            jax.ShapeDtypeStruct((groups, PER, length), f32),
            jax.ShapeDtypeStruct((inner, STATE), bf16),
            jax.ShapeDtypeStruct((blocks - 1, inner, STATE), f32),
            jax.ShapeDtypeStruct((8, STATE), f32),
            jax.ShapeDtypeStruct((d, ext), bf16),
        ],
        scratch_shapes=[
            pltpu.VMEM((length, STATE), bf16),
            pltpu.VMEM((length, 2 * STATE), bf16),
        ],
        compiler_params=pltpu.CompilerParams(vmem_limit_bytes=32 * 2**20),
        cost_estimate=pl.CostEstimate(
            flops=2 * ext * d * (inner + 3 * STATE), bytes_accessed=12 * 2**20, transcendentals=0
        ),
        name="project",
    )(nrm, w_in, cw, cb, dtb, rate, starts)


def pair_of(width):
    return iota((1, width), 1) < HEADDIM


def within_kernel(
    nrm_ref, w_ref, x_ref, bc_ref, dt_ref, lam_ref, lamt_ref, starts_ref, skip_ref,
    gate_ref, y_ref,
    cross_sc, mask_sc, dt_sc,
):
    group = pl.program_id(0)
    length = starts_ref.shape[0]
    blocks = length // BLOCK

    @pl.when(group == 0)
    def _():
        act = silu(bc_ref[...].astype(f32)).astype(bf16)
        for b in range(blocks):
            s = block_of(b)
            cross_sc[b] = dot(act[s, STATE:], act[s, :STATE], 1, 1)
        fill_mask(mask_sc, starts_ref[...], blocks)
        dt_sc[...] = split(dt_ref[...])

    gate_ref[...] = dot(nrm_ref[RIM:], w_ref[...]).astype(bf16)
    x = silu(x_ref[...].astype(f32))
    xd = (x * spread(dt_sc[...], group)).astype(bf16)
    lam = pltpu.roll(lam_ref[...], lax.rem(STATE - PER * group, STATE), 1)
    lamt = lamt_ref[group]
    left = pair_of(2 * HEADDIM)
    for b in range(blocks):
        s = block_of(b)
        parts = []
        for p in range(PER // 2):
            c = slice(2 * HEADDIM * p, 2 * HEADDIM * (p + 1))
            two = []
            for h in (2 * p, 2 * p + 1):
                gap = (lam[s, h : h + 1] - lamt[h : h + 1, s]) + mask_sc[b]
                two.append(dot((jnp.exp(gap) * cross_sc[b]).astype(bf16), xd[s, c]))
            parts.append(jnp.where(left, two[0], two[1]))
        y = jnp.concatenate(parts, axis=1) + skip_ref[...] * x[s]
        y_ref[s] = y.astype(bf16)


def within(nrm, w_in, cv, dt, lam, lamt, starts, skip):
    ext, d = nrm.shape
    length = starts.shape[0]
    blocks = length // BLOCK
    groups = lamt.shape[0]
    inner = groups * TILE
    full = lambda *shape: pl.BlockSpec(shape, lambda s: (0,) * len(shape))
    tile = pl.BlockSpec((length, TILE), lambda s: (0, s))
    return pl.pallas_call(
        within_kernel,
        grid=(groups,),
        in_specs=[
            full(ext, d),
            pl.BlockSpec((d, TILE), lambda s: (0, s)),
            tile,
            pl.BlockSpec((length, TILE), lambda s: (0, groups)),
            full(length, STATE),
            full(length, STATE),
            full(groups, PER, length),
            full(length, 1),
            pl.BlockSpec((1, TILE), lambda s: (0, s)),
        ],
        out_specs=[tile, tile],
        out_shape=[
            jax.ShapeDtypeStruct((length, inner), bf16),
            jax.ShapeDtypeStruct((length, inner), bf16),
        ],
        scratch_shapes=[
            pltpu.VMEM((blocks, BLOCK, BLOCK), f32),
            pltpu.VMEM((blocks, BLOCK, BLOCK), f32),
            pltpu.VMEM((length, 2 * STATE), bf16),
        ],
        compiler_params=pltpu.CompilerParams(vmem_limit_bytes=32 * 2**20),
        cost_estimate=pl.CostEstimate(
            flops=2 * ext * d * inner * 4, bytes_accessed=12 * 2**20, transcendentals=0
        ),
        name="within",
    )(nrm, w_in, cv, cv, dt, lam, lamt, starts, skip)


def states_of(s0, fresh_ref, dec_ref, group, blocks):
    found = [s0]
    for b in range(blocks - 1):
        found.append(head_rows(dec_ref[b : b + 1], group) * found[-1] + fresh_ref[b])
    return found


def join_kernel(
    y_ref, bc_ref, lam_ref, starts_ref, gate_ref, s0_ref, fresh_ref, dec_ref, gain_ref, wo_ref,
    resid_ref, gain_next_ref,
    y_out_ref, gated_ref, scale_ref, next_ref, low_ref, nrm_ref,
    u_sc, c_sc, v_sc, sq_sc,
):
    group = pl.program_id(0)
    length = starts_ref.shape[0]
    blocks = length // BLOCK
    groups = v_sc.shape[0]
    inner = groups * TILE

    @pl.when(group == 0)
    def _():
        c_sc[...] = silu(bc_ref[:, STATE:].astype(f32)).astype(bf16)
        for b in range(blocks):
            u_sc[block_of(b)] = split(reach_weights(starts_ref[...], lam_ref[...], b))
        sq_sc[...] = jnp.zeros_like(sq_sc)

    u = spread(u_sc[...], group)
    before = states_of(s0_ref[...].astype(f32), fresh_ref, dec_ref, group, blocks)
    carried = jnp.concatenate(
        [dot(c_sc[block_of(b)], before[b].astype(bf16), 1, 1) for b in range(blocks)], axis=0
    )
    y = (y_ref[...].astype(f32) + u * carried).astype(bf16)
    y_out_ref[...] = y
    v = y.astype(f32) * silu(gate_ref[...].astype(f32))
    v_sc[group] = v
    sq = v * v
    sq_sc[...] += sq[:, :STATE] + sq[:, STATE:]

    @pl.when(group == groups - 1)
    def _():
        mean = jnp.sum(sq_sc[...], axis=1, keepdims=True) / inner
        scale = lax.rsqrt(mean + EPSILON)
        scale_ref[...] = scale
        acc = resid_ref[...]
        for g in range(groups):
            c = slice(g * TILE, (g + 1) * TILE)
            low = (v_sc[g] * scale * gain_ref[:, c]).astype(bf16)
            gated_ref[:, c] = low
            acc = acc + dot(low, wo_ref[c])
        next_ref[...] = acc
        low_ref[...] = acc.astype(bf16)
        norm = lax.rsqrt(jnp.mean(acc * acc, axis=1, keepdims=True) + EPSILON)
        nrm_ref[...] = (acc * norm * gain_next_ref[...]).astype(bf16)


def join(y, cv, lam, starts, gate, s0, fresh, dec, gain, w_out, resid, gain_next):
    length, inner = y.shape
    d = w_out.shape[1]
    blocks = length // BLOCK
    groups = inner // TILE
    full = lambda *shape: pl.BlockSpec(shape, lambda s: (0,) * len(shape))
    tile = pl.BlockSpec((length, TILE), lambda s: (0, s))
    return pl.pallas_call(
        join_kernel,
        grid=(groups,),
        in_specs=[
            tile,
            pl.BlockSpec((length, TILE), lambda s: (0, groups)),
            full(length, STATE),
            full(length, 1),
            tile,
            pl.BlockSpec((TILE, STATE), lambda s: (s, 0)),
            pl.BlockSpec((blocks - 1, TILE, STATE), lambda s: (0, s, 0)),
            full(8, STATE),
            full(1, inner),
            full(inner, d),
            full(length, d),
            full(1, d),
        ],
        out_specs=[
            tile,
            full(length, inner),
            full(length, 1),
            full(length, d),
            full(length, d),
            full(length, d),
        ],
        out_shape=[
            jax.ShapeDtypeStruct((length, inner), bf16),
            jax.ShapeDtypeStruct((length, inner), bf16),
            jax.ShapeDtypeStruct((length, 1), f32),
            jax.ShapeDtypeStruct((length, d), f32),
            jax.ShapeDtypeStruct((length, d), bf16),
            jax.ShapeDtypeStruct((length, d), bf16),
        ],
        scratch_shapes=[
            pltpu.VMEM((length, 2 * STATE), bf16),
            pltpu.VMEM((length, STATE), bf16),
            pltpu.VMEM((groups, length, TILE), f32),
            pltpu.VMEM((length, STATE), f32),
        ],
        compiler_params=pltpu.CompilerParams(vmem_limit_bytes=40 * 2**20),
        cost_estimate=pl.CostEstimate(
            flops=2 * length * inner * d, bytes_accessed=16 * 2**20, transcendentals=0
        ),
        name="join",
    )(y, cv, lam, starts, gate, s0, fresh, dec, gain, w_out, resid, gain_next)


def gate_back_kernel(
    grad_ref, wo_ref, y_ref, gate_ref, gated_ref, scale_ref, gain_ref, x_ref, bc_ref, lam_ref,
    starts_ref, dec_ref,
    gy_ref, ggate_ref, dwo_ref, ggain_ref, gskip_ref, later_ref, total_ref,
    gg_sc, u_sc, c_sc, dot_sc,
):
    phase, group = pl.program_id(0), pl.program_id(1)
    length = starts_ref.shape[0]
    blocks = length // BLOCK
    groups = gg_sc.shape[0]
    inner = groups * TILE

    @pl.when((phase == 0) & (group == 0))
    def _():
        c_sc[...] = silu(bc_ref[:, STATE:].astype(f32)).astype(bf16)
        for b in range(blocks):
            u_sc[block_of(b)] = split(reach_weights(starts_ref[...], lam_ref[...], b))
        dot_sc[...] = jnp.zeros_like(dot_sc)

    y = y_ref[...].astype(f32)
    gate = gate_ref[...].astype(f32)
    sig = logistic(gate)
    act = gate * sig
    v = y * act
    scale = scale_ref[...]

    @pl.when(phase == 0)
    def _():
        gg = dot(grad_ref[...], wo_ref[...], 1, 1)
        gv = gg * v
        ggain_ref[...] = jnp.sum(gv * scale, axis=0, keepdims=True)
        gv = gv * gain_ref[...]
        dot_sc[...] += gv[:, :STATE] + gv[:, STATE:]
        gg_sc[group] = gg * gain_ref[...]
        dwo_ref[...] = dot(gated_ref[...], grad_ref[...], 0, 0).astype(bf16)

    @pl.when(phase == 1)
    def _():
        @pl.when(group == 0)
        def _():
            total = jnp.sum(dot_sc[...], axis=1, keepdims=True)
            dot_sc[...] = jnp.broadcast_to(
                total * scale * scale * scale * (1.0 / inner), dot_sc.shape
            )

        gv = scale * gg_sc[group] - v * dot_sc[:, :1]
        gy = gv * act
        ggate_ref[...] = (gv * y * (sig + act * (1.0 - sig))).astype(bf16)
        low = gy.astype(bf16)
        gy_ref[...] = low
        x = silu(x_ref[...].astype(f32))
        gskip_ref[...] = jnp.sum(low.astype(f32) * x, axis=0, keepdims=True)
        ug = (gy * spread(u_sc[...], group)).astype(bf16)
        total = None
        for b in reversed(range(blocks)):
            direct = dot(ug[block_of(b)], c_sc[block_of(b)], 0, 0)
            if total is None:
                total = direct
            else:
                total = head_rows(dec_ref[b : b + 1], group) * total + direct
            if b > 0:
                later_ref[b - 1] = direct
        total_ref[...] = total.astype(total_ref.dtype)


def gate_back(grad_low, w_out, y, gate, gated, scale, gain, cv, lam, starts, dec):
    length, inner = y.shape
    d = w_out.shape[1]
    blocks = length // BLOCK
    groups = inner // TILE
    full = lambda *shape: pl.BlockSpec(shape, lambda p, s: (0,) * len(shape))
    early = lambda p, s: jnp.where(p == 0, s, groups - 1)
    late = lambda p, s: s * p
    tile = pl.BlockSpec((length, TILE), lambda p, s: (0, s))
    late_tile = pl.BlockSpec((length, TILE), lambda p, s: (0, late(p, s)))
    return pl.pallas_call(
        gate_back_kernel,
        grid=(2, groups),
        in_specs=[
            full(length, d),
            pl.BlockSpec((TILE, d), lambda p, s: (early(p, s), 0)),
            tile,
            tile,
            pl.BlockSpec((length, TILE), lambda p, s: (0, early(p, s))),
            full(length, 1),
            pl.BlockSpec((1, TILE), lambda p, s: (0, s)),
            late_tile,
            pl.BlockSpec((length, TILE), lambda p, s: (0, groups)),
            full(length, STATE),
            full(length, 1),
            full(8, STATE),
        ],
        out_specs=[
            late_tile,
            late_tile,
            pl.BlockSpec((TILE, d), lambda p, s: (early(p, s), 0)),
            pl.BlockSpec((1, TILE), lambda p, s: (0, early(p, s))),
            pl.BlockSpec((1, TILE), lambda p, s: (0, late(p, s))),
            pl.BlockSpec((blocks - 1, TILE, STATE), lambda p, s: (0, late(p, s), 0)),
            pl.BlockSpec((TILE, STATE), lambda p, s: (late(p, s), 0)),
        ],
        out_shape=[
            jax.ShapeDtypeStruct((length, inner), bf16),
            jax.ShapeDtypeStruct((length, inner), bf16),
            jax.ShapeDtypeStruct((inner, d), bf16),
            jax.ShapeDtypeStruct((1, inner), f32),
            jax.ShapeDtypeStruct((1, inner), f32),
            jax.ShapeDtypeStruct((blocks - 1, inner, STATE), f32),
            jax.ShapeDtypeStruct((inner, STATE), bf16),
        ],
        scratch_shapes=[
            pltpu.VMEM((groups, length, TILE), f32),
            pltpu.VMEM((length, 2 * STATE), bf16),
            pltpu.VMEM((length, STATE), bf16),
            pltpu.VMEM((length, STATE), f32),
        ],
        compiler_params=pltpu.CompilerParams(vmem_limit_bytes=40 * 2**20),
        cost_estimate=pl.CostEstimate(
            flops=4 * length * inner * d, bytes_accessed=24 * 2**20, transcendentals=0
        ),
        name="gate_back",
    )(grad_low, w_out, y, gate, gated, scale, gain, cv, cv, lam, starts, dec)


def within_back_kernel(
    gy_ref, x_ref, bc_ref, dt_ref, lam_ref, lamt_ref, starts_ref, s0_ref, fresh_ref, dec_ref,
    ggate_ref, w_ref, nrmt_ref,
    gxd_ref, glam_ref, gbc_ref, dw_ref, gnrm_ref,
    cross_sc, gcross_sc, mask_sc, dt_sc, u_sc, act_sc,
):
    group = pl.program_id(0)
    length = starts_ref.shape[0]
    blocks = length // BLOCK
    groups = lamt_ref.shape[0]

    @pl.when(group == 0)
    def _():
        act = silu(bc_ref[...].astype(f32)).astype(bf16)
        act_sc[...] = act
        for b in range(blocks):
            s = block_of(b)
            cross_sc[b] = dot(act[s, STATE:], act[s, :STATE], 1, 1)
            u_sc[s] = split(reach_weights(starts_ref[...], lam_ref[...], b))
        fill_mask(mask_sc, starts_ref[...], blocks)
        dt_sc[...] = split(dt_ref[...])
        gcross_sc[...] = jnp.zeros_like(gcross_sc)
        glam_ref[...] = jnp.zeros_like(glam_ref)
        gbc_ref[...] = jnp.zeros_like(gbc_ref)
        gnrm_ref[...] = jnp.zeros_like(gnrm_ref)

    ggate = ggate_ref[...]
    gnrm_ref[...] += dot(ggate, w_ref[...], 1, 1)
    dw_ref[...] = dot(nrmt_ref[:, RIM:], ggate).astype(bf16)

    x = silu(x_ref[...].astype(f32))
    xd = (x * spread(dt_sc[...], group)).astype(bf16)
    gy = gy_ref[...]
    u = spread(u_sc[...], group)
    before = states_of(s0_ref[...].astype(f32), fresh_ref, dec_ref, group, blocks)
    lam = pltpu.roll(lam_ref[...], lax.rem(STATE - PER * group, STATE), 1)
    lamt = lamt_ref[group]
    left = pair_of(2 * HEADDIM)
    for b in range(blocks):
        s = block_of(b)
        gcross = gcross_sc[b]
        ys, gxds = [], []
        for p in range(PER // 2):
            c = slice(2 * HEADDIM * p, 2 * HEADDIM * (p + 1))
            y2, g2 = [], []
            for h in (2 * p, 2 * p + 1):
                decay = jnp.exp((lam[s, h : h + 1] - lamt[h : h + 1, s]) + mask_sc[b])
                weight = (decay * cross_sc[b]).astype(bf16)
                y2.append(dot(weight, xd[s, c]))
                g2.append(dot(weight, gy[s, c], 0, 0))
                own = left if h % 2 == 0 else ~left
                mine = jnp.where(own, gy[s, c], jnp.zeros((), bf16))
                gcross = gcross + dot(mine, xd[s, c], 1, 1) * decay
            ys.append(jnp.where(left, y2[0], y2[1]))
            gxds.append(jnp.where(left, g2[0], g2[1]))
        gcross_sc[b] = gcross
        state = before[b].astype(bf16)
        y = jnp.concatenate(ys, axis=1) + u[s] * dot(act_sc[s, STATE:], state, 1, 1)
        gxd = jnp.concatenate(gxds, axis=1)
        gxd_ref[s] = gxd
        gyf = gy[s].astype(f32)
        glam_ref[s] += gather_heads(gyf * y - xd[s].astype(f32) * gxd, group)
        gbc_ref[s, STATE:] += dot((u[s] * gyf).astype(bf16), state)

    @pl.when(group == groups - 1)
    def _():
        for b in range(blocks):
            s = block_of(b)
            low = gcross_sc[b].astype(bf16)
            gbc_ref[s, :STATE] += dot(low, act_sc[s, STATE:], 0, 0)
            gbc_ref[s, STATE:] += dot(low, act_sc[s, :STATE])


def within_back(gy, cv, dt, lam, lamt, starts, s0, fresh, dec, ggate, w_in, nrmt):
    length, inner = gy.shape
    d, ext = nrmt.shape
    blocks = length // BLOCK
    groups = inner // TILE
    full = lambda *shape: pl.BlockSpec(shape, lambda s: (0,) * len(shape))
    tile = pl.BlockSpec((length, TILE), lambda s: (0, s))
    wide = pl.BlockSpec((d, TILE), lambda s: (0, s))
    return pl.pallas_call(
        within_back_kernel,
        grid=(groups,),
        in_specs=[
            tile,
            tile,
            pl.BlockSpec((length, TILE), lambda s: (0, groups)),
            full(length, STATE),
            full(length, STATE),
            full(groups, PER, length),
            full(length, 1),
            pl.BlockSpec((TILE, STATE), lambda s: (s, 0)),
            pl.BlockSpec((blocks - 1, TILE, STATE), lambda s: (0, s, 0)),
            full(8, STATE),
            tile,
            wide,
            full(d, ext),
        ],
        out_specs=[tile, full(length, STATE), full(length, 2 * STATE), wide, full(length, d)],
        out_shape=[
            jax.ShapeDtypeStruct((length, inner), f32),
            jax.ShapeDtypeStruct((length, STATE), f32),
            jax.ShapeDtypeStruct((length, 2 * STATE), f32),
            jax.ShapeDtypeStruct((d, inner), bf16),
            jax.ShapeDtypeStruct((length, d), f32),
        ],
        scratch_shapes=[
            pltpu.VMEM((blocks, BLOCK, BLOCK), f32),
            pltpu.VMEM((blocks, BLOCK, BLOCK), f32),
            pltpu.VMEM((blocks, BLOCK, BLOCK), f32),
            pltpu.VMEM((length, 2 * STATE), bf16),
            pltpu.VMEM((length, 2 * STATE), bf16),
            pltpu.VMEM((length, 2 * STATE), bf16),
        ],
        compiler_params=pltpu.CompilerParams(vmem_limit_bytes=40 * 2**20),
        cost_estimate=pl.CostEstimate(
            flops=12 * length * inner * d, bytes_accessed=24 * 2**20, transcendentals=0
        ),
        name="within_back",
    )(gy, cv, cv, dt, lam, lamt, starts, s0, fresh, dec, ggate, w_in, nrmt)


def last_kernel(
    gxd_ref, cv_ref, cin_ref, gy_ref, bc_ref, dt_ref, lam_ref, sig_ref, starts_ref, gend_ref,
    later_ref, s0_ref, fresh_ref, dec_ref, w_ref, nrmt_ref, glam_ref, gbc_ref, gin_ref, skip_ref,
    rate_ref, cw_ref,
    dw_ref, gnrm_ref, gcw_ref, gcb_ref, gsmall_ref,
    b_sc, gb_sc, dt_sc, e_sc, glam_sc, gdt_sc, zs_sc, over_sc, gp_sc,
):
    step = pl.program_id(0)
    length = starts_ref.shape[0]
    blocks = length // BLOCK
    groups = pl.num_programs(0) - 2
    starts = starts_ref[...]
    ext = gnrm_ref.shape[0]

    @pl.when(step == 0)
    def _():
        b_sc[...] = silu(bc_ref[:, :STATE].astype(f32)).astype(bf16)
        gb_sc[...] = gbc_ref[:, :STATE]
        dt_sc[...] = split(dt_ref[...])
        for b in range(blocks):
            e_sc[block_of(b)] = split(end_weights(starts, lam_ref[...], b))
        gdt_sc[...] = jnp.zeros_like(gdt_sc)
        zs_sc[...] = jnp.zeros_like(zs_sc)
        over_sc[...] = jnp.zeros_like(over_sc)
        gnrm_ref[:RIM] = jnp.zeros((RIM, gnrm_ref.shape[1]), f32)
        gnrm_ref[RIM:] = gin_ref[...]

    def conv_back(gact):
        gcv = gact * dsilu(cv_ref[...].astype(f32))
        gcb_ref[...] = jnp.sum(gcv, axis=0, keepdims=True)
        place = iota((length, 1), 0)
        taps = cw_ref.shape[0]
        cin = cin_ref[...].astype(f32)
        zeros = jnp.zeros((RIM, TILE), f32)
        acc = None
        rows = []
        for k in range(taps):
            back = taps - 1 - k
            term = gcv if back == 0 else jnp.where(place - back >= starts, gcv, 0.0)
            moved = jnp.concatenate([zeros, term], axis=0)
            if back:
                moved = pltpu.roll(moved, ext - back, 0)
            rows.append(jnp.sum(moved * cin, axis=0, keepdims=True))
            part = cw_ref[k : k + 1] * moved
            acc = part if acc is None else acc + part
        gcw_ref[...] = jnp.concatenate(rows, axis=0)
        gp_sc[...] = acc.astype(bf16)

    @pl.when(step < groups)
    def _():
        group = step
        x = silu(cv_ref[...].astype(f32))
        dt = spread(dt_sc[...], group)
        e = spread(e_sc[...], group)
        xd = x * dt
        gend = gend_ref[...].astype(f32)
        grads = [None] * blocks
        for b in reversed(range(blocks)):
            grads[b] = gend
            if b > 0:
                gend = head_rows(dec_ref[b : b + 1], group) * gend + later_ref[b - 1]
        before = states_of(s0_ref[...].astype(f32), fresh_ref, dec_ref, group, blocks)
        parts = []
        for b in range(blocks):
            s = block_of(b)
            low = grads[b].astype(bf16)
            parts.append(e[s] * dot(b_sc[s], low, 1, 1))
            gb_sc[s] += dot((e[s] * xd[s]).astype(bf16), low)
            over = jnp.sum(grads[b] * before[b], axis=1, keepdims=True)
            over_sc[b : b + 1] += dec_ref[b : b + 1] * jnp.sum(
                jnp.where(chooser(group), over, 0.0), axis=0, keepdims=True
            )
        more = jnp.concatenate(parts, axis=0)
        gxd = gxd_ref[...] + more
        zs_sc[...] += gather_heads(xd * more, group)
        gdt_sc[...] += gather_heads(x * gxd, group)
        conv_back(dt * gxd + skip_ref[...] * gy_ref[...].astype(f32))

    @pl.when(step == groups)
    def _():
        conv_back(jnp.concatenate([gb_sc[...], gbc_ref[:, STATE:]], axis=1))

    @pl.when(step <= groups)
    def _():
        gp = gp_sc[...]
        gnrm_ref[...] += dot(gp, w_ref[...], 1, 1)
        dw_ref[...] = dot(nrmt_ref[...], gp).astype(bf16)

    @pl.when(step == groups + 1)
    def _():
        tri = lower(BLOCK).astype(f32)
        glam = glam_ref[...] - zs_sc[...]
        rows = []
        for b in range(blocks):
            s = block_of(b)
            end = jnp.sum(zs_sc[s], axis=0, keepdims=True) + over_sc[b : b + 1]
            rows.append(dot(tri, glam[s], 0, 0, precision=PRECISE) + end)
        back = jnp.concatenate(rows, axis=0)
        dt = dt_ref[...]
        gz = (gdt_sc[...] + rate_ref[...] * back) * sig_ref[...]
        gsmall_ref[0:1] = jnp.sum(gz, axis=0, keepdims=True)
        gsmall_ref[1:2] = rate_ref[...] * jnp.sum(dt * back, axis=0, keepdims=True)
        gsmall_ref[2:8] = jnp.zeros((6, STATE), f32)
        low = gz.astype(bf16)
        heads = groups * PER
        w = jnp.where(iota((w_ref.shape[0], STATE), 1) < heads, w_ref[:, :STATE], jnp.zeros((), bf16))
        gnrm_ref[RIM:] += dot(low, w, 1, 1)
        dw_ref[:, :STATE] = dot(nrmt_ref[:, RIM:], low).astype(bf16)


def last(
    gxd, cv, cin, gy, dt, lam, sig, starts, gend, later, s0, fresh, dec, w_in, nrmt, glam, gbc,
    gin, skip, rate, cw,
):
    length, inner = gy.shape
    d, ext = nrmt.shape
    blocks = length // BLOCK
    groups = inner // TILE
    heads = inner // HEADDIM
    taps = cw.shape[0]
    full = lambda *shape: pl.BlockSpec(shape, lambda s: (0,) * len(shape))
    own = lambda s: jnp.minimum(s, groups - 1)
    col = lambda s: jnp.minimum(s, groups)
    tile = pl.BlockSpec((length, TILE), lambda s: (0, own(s)))
    state = pl.BlockSpec((TILE, STATE), lambda s: (own(s), 0))
    states = pl.BlockSpec((blocks - 1, TILE, STATE), lambda s: (0, own(s), 0))
    return pl.pallas_call(
        last_kernel,
        grid=(groups + 2,),
        in_specs=[
            tile,
            pl.BlockSpec((length, TILE), lambda s: (0, col(s))),
            pl.BlockSpec((ext, TILE), lambda s: (0, col(s))),
            tile,
            pl.BlockSpec((length, TILE), lambda s: (0, groups)),
            full(length, STATE),
            full(length, STATE),
            full(length, STATE),
            full(length, 1),
            state,
            states,
            state,
            states,
            full(8, STATE),
            pl.BlockSpec((d, TILE), lambda s: (0, groups + s)),
            full(d, ext),
            full(length, STATE),
            full(length, 2 * STATE),
            full(length, d),
            pl.BlockSpec((1, TILE), lambda s: (0, own(s))),
            full(1, STATE),
            pl.BlockSpec((taps, TILE), lambda s: (0, col(s))),
        ],
        out_specs=[
            pl.BlockSpec((d, TILE), lambda s: (0, s)),
            full(ext, d),
            pl.BlockSpec((taps, TILE), lambda s: (0, col(s))),
            pl.BlockSpec((1, TILE), lambda s: (0, col(s))),
            full(8, STATE),
        ],
        out_shape=[
            jax.ShapeDtypeStruct((d, inner + 2 * STATE + heads), bf16),
            jax.ShapeDtypeStruct((ext, d), f32),
            jax.ShapeDtypeStruct((taps, inner + 2 * STATE), f32),
            jax.ShapeDtypeStruct((1, inner + 2 * STATE), f32),
            jax.ShapeDtypeStruct((8, STATE), f32),
        ],
        scratch_shapes=[
            pltpu.VMEM((length, STATE), bf16),
            pltpu.VMEM((length, STATE), f32),
            pltpu.VMEM((length, 2 * STATE), bf16),
            pltpu.VMEM((length, 2 * STATE), bf16),
            pltpu.VMEM((length, STATE), f32),
            pltpu.VMEM((length, STATE), f32),
            pltpu.VMEM((length, STATE), f32),
            pltpu.VMEM((8, STATE), f32),
            pltpu.VMEM((ext, TILE), bf16),
        ],
        compiler_params=pltpu.CompilerParams(vmem_limit_bytes=40 * 2**20),
        cost_estimate=pl.CostEstimate(
            flops=12 * length * inner * d, bytes_accessed=24 * 2**20, transcendentals=0
        ),
        name="last",
    )(
        gxd, cv, cin, gy, cv, dt, lam, sig, starts, gend, later, s0, fresh, dec, w_in, nrmt, glam,
        gbc, gin, skip, rate, cw,
    )


def rms_back(resid, gain, grad_normed):
    width = resid.shape[1]
    scale = lax.rsqrt(jnp.mean(resid * resid, axis=1, keepdims=True) + EPSILON)
    scaled = grad_normed * gain
    inner = jnp.sum(scaled * resid, axis=1, keepdims=True)
    grad = scale * scaled - resid * (inner * scale * scale * scale / width)
    return grad, jnp.sum(grad_normed * resid * scale, axis=0)


def passed_along(shard, axis, by):
    devices = lax.axis_size(axis)
    pairs = [(i, i + by) for i in range(devices) if 0 <= i + by < devices]
    return lax.ppermute(shard, axis, pairs)


def carried_over(state, decay, reverse):
    devices, here = lax.axis_size("seq"), lax.axis_index("seq")
    states = lax.all_gather(state, "seq", axis=0)
    decays = lax.all_gather(decay, "seq", axis=0)[:, 0]
    source = jnp.arange(devices)[:, None]
    between = jnp.arange(devices)[None, :]
    if reverse:
        inside = (between < source) & (between > here)
        counted = jnp.arange(devices) > here
    else:
        inside = (between > source) & (between < here)
        counted = jnp.arange(devices) < here
    share = jnp.prod(jnp.where(inside[:, :, None], decays[None], 1.0), axis=1)
    share = jnp.where(counted[:, None], share, 0.0)
    heads = state.shape[0] // HEADDIM
    share = jnp.repeat(share[:, :heads], HEADDIM, axis=1)
    return jnp.sum(share[:, :, None] * states.astype(f32), axis=0)


def lanes(row):
    return jnp.pad(row, (0, STATE - row.shape[0]))[None]


def local(
    tokens,
    in_weight,
    out_weight,
    conv_weight,
    conv_bias,
    a_log,
    dt_bias,
    skip_d,
    norm_gain,
    gated_gain,
    doc_start,
    cotangent,
):
    layers = in_weight.shape[0]
    length, width = tokens.shape[1:]
    taps, channels = conv_weight.shape[1:]
    owners = lax.axis_size("wa")
    heads = a_log.shape[1] * owners
    inner = heads * HEADDIM
    starts = (doc_start[0] - lax.axis_index("seq") * length)[:, None]

    own_small = [
        conv_weight.reshape(layers, taps * channels), conv_bias, a_log, dt_bias, skip_d,
        norm_gain, gated_gain,
    ]
    small = lax.all_gather(jnp.concatenate(own_small, axis=1), "wa", axis=0).astype(f32)
    sizes = [a.shape[1] for a in own_small]
    params = []
    for layer in range(layers):
        found, at = [], 0
        for i, size in enumerate(sizes):
            part = small[:, layer, at : at + size]
            at += size
            if i == 0:
                part = part.reshape(owners, taps, channels).swapaxes(0, 1)
                found.append(part.reshape(taps, owners * channels))
            else:
                found.append(part.reshape(owners * size))
        params.append(found)

    weights = [
        (
            lax.all_gather(in_weight[layer], "wa", axis=0, tiled=True),
            lax.all_gather(out_weight[layer], "wa", axis=0, tiled=True),
        )
        for layer in range(layers)
    ]
    resid = tokens[0].astype(f32)
    normed = (
        resid
        * lax.rsqrt(jnp.mean(resid * resid, axis=1, keepdims=True) + EPSILON)
        * params[0][5]
    ).astype(bf16)
    records = []
    for layer in range(layers):
        cw, cb, alog, dtb, skip, ngain, ggain = params[layer]
        rate = lanes(-jnp.exp(alog))
        skip_row = jnp.repeat(skip, HEADDIM)[None]
        w_in, w_out = weights[layer]
        rim = passed_along(normed[length - RIM :], "seq", 1)
        nrm = jnp.concatenate([rim, normed], axis=0)
        cin, cv, dt, lam, sig, lamt, state, fresh, dec, nrmt = first(
            nrm, w_in, cw, cb[None], lanes(dtb), rate, starts, heads
        )
        blocks = length // BLOCK
        decay = dec[blocks : blocks + 1]
        s0 = carried_over(state, decay, False)
        gate, y = within(nrm, w_in, cv, dt, lam, lamt, starts, skip_row)
        gain_next = params[min(layer + 1, layers - 1)][5][None]
        y, gated, scale, resid_next, low, normed = join(
            y, cv, lam, starts, gate, s0, fresh, dec, ggain[None], w_out, resid, gain_next
        )
        records.append(
            (resid, cin, cv, dt, lam, sig, lamt, fresh, dec, nrmt, s0, gate, y, gated, scale,
             rate, skip_row, decay)
        )
        resid = resid_next
    result = low[None]
    grad = cotangent[0].astype(f32)
    big = [None] * layers
    little = [None] * layers
    for layer in reversed(range(layers)):
        cw, cb, alog, dtb, skip, ngain, ggain = params[layer]
        w_in, w_out = weights[layer]
        (resid, cin, cv, dt, lam, sig, lamt, fresh, dec, nrmt, s0, gate, y, gated, scale,
         rate, skip_row, decay) = records[layer]
        gy, ggate, dwo, gggain, gskip, later, total = gate_back(
            grad.astype(bf16), w_out, y, gate, gated, scale, ggain[None], cv, lam, starts, dec
        )
        gend = carried_over(total, decay, True)
        gxd, glam, gbc, dw_gate, gnrm_gate = within_back(
            gy, cv, dt, lam, lamt, starts, s0, fresh, dec, ggate, w_in, nrmt
        )
        dw_rest, gnrm, gcw, gcb, gsmall = last(
            gxd, cv, cin, gy, dt, lam, sig, starts, gend, later, s0, fresh, dec, w_in, nrmt, glam,
            gbc, gnrm_gate, skip_row, rate, cw,
        )
        rim = passed_along(gnrm[:RIM], "seq", -1)
        gnormed = gnrm[RIM:]
        gnormed = jnp.concatenate([gnormed[: length - RIM], gnormed[length - RIM :] + rim], axis=0)
        grad_resid, gngain = rms_back(resid, ngain, gnormed)
        grad = grad + grad_resid
        big[layer] = (jnp.concatenate([dw_gate, dw_rest], axis=1), dwo)
        little[layer] = (
            gcw, gcb[0], gsmall[1, :heads], gsmall[0, :heads],
            jnp.sum(gskip.reshape(heads, HEADDIM), axis=1), gngain, gggain[0],
        )

    def owned(part):
        part = lax.psum_scatter(part, "wa", scatter_dimension=0, tiled=True)
        return lax.psum(part, "seq").astype(f32)

    in_grad = jnp.stack([owned(big[layer][0]) for layer in range(layers)])
    out_grad = jnp.stack([owned(big[layer][1]) for layer in range(layers)])
    rows = []
    for layer in range(layers):
        gcw = little[layer][0].reshape(taps, owners, channels).swapaxes(0, 1)
        parts = [gcw.reshape(owners, taps * channels)]
        parts += [a.reshape(owners, -1) for a in little[layer][1:]]
        rows.append(jnp.concatenate(parts, axis=1))
    packed = jnp.stack(rows, axis=1)
    mine = lax.dynamic_index_in_dim(
        lax.psum(packed, ("wa", "seq")), lax.axis_index("wa"), 0, keepdims=False
    )
    found, at = [], 0
    for i, size in enumerate(sizes):
        part = mine[:, at : at + size]
        at += size
        found.append(part.reshape(layers, taps, channels) if i == 0 else part)
    return (result, grad[None], in_grad, out_grad, *found)


def solution(mesh):
    in_specs = (
        P("wa", "seq", None),
        P(None, "wa", None),
        P(None, "wa", None),
        P(None, None, "wa"),
        P(None, "wa"),
        P(None, "wa"),
        P(None, "wa"),
        P(None, "wa"),
        P(None, "wa"),
        P(None, "wa"),
        P("wa", "seq"),
        P("wa", "seq", None),
    )
    out_specs = (
        P("wa", "seq", None),
        P("wa", "seq", None),
        P(None, "wa", None),
        P(None, "wa", None),
        P(None, None, "wa"),
        P(None, "wa"),
        P(None, "wa"),
        P(None, "wa"),
        P(None, "wa"),
        P(None, "wa"),
        P(None, "wa"),
    )
    return jax.shard_map(local, mesh=mesh, in_specs=in_specs, out_specs=out_specs, check_vma=False)
```

```python
import functools

import jax
import jax.numpy as jnp
from jax import lax
from jax.experimental import pallas as pl
from jax.experimental.pallas import tpu as pltpu
from jax.sharding import PartitionSpec as P

HEADDIM = 64
STATE = 128
BLOCK = 256
TILE = 256
PER = TILE // HEADDIM
RIM = 16
EPSILON = 1e-05
PRECISE = lax.Precision.HIGHEST
f32 = jnp.float32
bf16 = jnp.bfloat16
FAR = -1e30
VMEM = 60 * 2**20
NO_COST = pl.CostEstimate(flops=0, bytes_accessed=0, transcendentals=0)


def dot(a, b, ca=1, cb=0, precision=None):
    return lax.dot_general(
        a, b, (((ca,), (cb,)), ((), ())), precision=precision, preferred_element_type=f32
    )


def iota(shape, axis):
    return lax.broadcasted_iota(jnp.int32, shape, axis)


def logistic(v):
    return 1.0 / (1.0 + jnp.exp(-v))


def silu(v):
    return v * logistic(v)


def dsilu(v):
    s = logistic(v)
    return s * (1.0 + v * (1.0 - s))


def split(q):
    high = q.astype(bf16)
    return jnp.concatenate([high, (q - high.astype(f32)).astype(bf16)], axis=1)


def spread(pair, group):
    rows = iota((2 * STATE, TILE), 0) % STATE
    cols = PER * group + iota((2 * STATE, TILE), 1) // HEADDIM
    return dot(pair, (rows == cols).astype(f32).astype(bf16))


def chooser(group):
    return iota((TILE, STATE), 1) == PER * group + iota((TILE, STATE), 0) // HEADDIM


def gather_heads(z, group):
    pick = chooser(group).astype(f32).astype(bf16)
    high = z.astype(bf16)
    low = (z - high.astype(f32)).astype(bf16)
    return dot(high, pick) + dot(low, pick)


def head_rows(row, group):
    return jnp.sum(jnp.where(chooser(group), row, 0.0), axis=1, keepdims=True)


def lower(n):
    return iota((n, n), 0) >= iota((n, n), 1)


def decay_rows(decay):
    high = decay.astype(bf16).astype(f32)
    zeros = jnp.zeros((RIM - 2, STATE), f32)
    return jnp.concatenate([high, decay - high, zeros], axis=0).astype(bf16)


def block_of(b):
    return slice(b * BLOCK, (b + 1) * BLOCK)


def end_weights(starts, lam, b):
    s = block_of(b)
    last = (b + 1) * BLOCK - 1
    place = b * BLOCK + iota((BLOCK, 1), 0)
    keep = place >= starts[last : last + 1]
    return jnp.where(keep, jnp.exp(lam[last : last + 1] - lam[s]), 0.0)


def reach_weights(starts, lam, b):
    s = block_of(b)
    return jnp.where(starts[s] < b * BLOCK, jnp.exp(lam[s]), 0.0)


def fill_mask(mask_ref, starts, blocks):
    for b in range(blocks):
        t = b * BLOCK + iota((BLOCK, BLOCK), 0)
        s = b * BLOCK + iota((BLOCK, BLOCK), 1)
        mask_ref[b] = jnp.where((s <= t) & (s >= starts[block_of(b)]), 0.0, FAR)


def assemble(w_refs, w_sc, at_ref, plan):
    for w_ref, (places, first_owner) in zip(w_refs, plan):
        for i, r in enumerate(places):
            for q in range(w_ref.shape[1]):
                w_sc[at_ref[0] ^ (first_owner + q), at_ref[1] ^ r] = w_ref[i, q]
    return w_sc[...].reshape(-1, w_sc.shape[-1])


def deal(value, keep_ref, send_ref, d_sc, at_ref):
    owners, places = d_sc.shape[:2]
    d_sc[...] = value.astype(bf16).reshape(d_sc.shape)
    for r in range(places):
        target = send_ref if r % 2 else keep_ref
        for q in range(owners):
            target[r // 2, q] = d_sc[at_ref[2] ^ q, at_ref[3] ^ r]


class Layout:
    def __init__(self, owners, places, rows):
        self.owners, self.places, self.rows = owners, places, rows

    def scratch(self, width):
        return pltpu.VMEM((self.owners, self.places, self.rows, width), bf16)

    def dealt(self, col):
        block = (max(self.places // 2, 1), self.owners, self.rows, TILE)
        return [pl.BlockSpec(block, lambda *s: (0, 0, 0, col(*s)))] * (1 if self.places == 1 else 2)

    def dealt_shape(self, rows, width):
        shape = (max(self.places // 2, 1), self.owners, rows, width)
        return [jax.ShapeDtypeStruct(shape, bf16)] * (1 if self.places == 1 else 2)


class Slots:
    def __init__(self, near, arrays, plan):
        self.near, self.arrays, self.plan = near, tuple(arrays), tuple(plan)

    def tiles(self, col):
        return [
            pl.BlockSpec((*a.shape[:3], TILE), lambda *s: (0, 0, 0, col(*s))) for a in self.arrays
        ]

    def whole(self, width, at):
        return [pl.BlockSpec((*a.shape[:3], width), lambda *s: (0, 0, 0, at)) for a in self.arrays]


SMEM = pl.BlockSpec(memory_space=pltpu.SMEM)


def first_kernel(
    plan, at_ref, nrm_ref, *refs
):
    w_refs, rest = refs[: len(plan)], refs[len(plan) :]
    first_body(plan, at_ref, nrm_ref, w_refs, *rest)


def first_body(
    plan, at_ref, nrm_ref, w_refs, cw_ref, cb_ref, dtb_ref, rate_ref, starts_ref,
    cin_ref, cv_ref, dt_ref, lam_ref, sig_ref, lamt_ref, state_ref, fresh_ref, dec_ref, nrmt_ref,
    b_sc, e_sc, w_sc,
):
    step = pl.program_id(0)
    length = starts_ref.shape[0]
    blocks = length // BLOCK
    heads = lamt_ref.shape[0] * PER
    starts = starts_ref[...]
    w = assemble(w_refs, w_sc, at_ref, plan)

    def conv():
        pe = dot(nrm_ref[...], w)
        cin_ref[...] = pe.astype(bf16)
        place = iota((length, 1), 0)
        taps = cw_ref.shape[0]
        acc = cb_ref[...] + cw_ref[taps - 1 : taps] * pe[RIM:]
        for k in range(taps - 1):
            back = taps - 1 - k
            keep = place - back >= starts
            acc = acc + jnp.where(keep, cw_ref[k : k + 1] * pltpu.roll(pe, back, 0)[RIM:], 0.0)
        cv = acc.astype(bf16)
        cv_ref[...] = cv
        return silu(cv.astype(f32))

    @pl.when(step == 0)
    def _():
        act = conv()
        b_sc[...] = act[:, :STATE].astype(bf16)
        nrmt_ref[...] = nrm_ref[...].T

    @pl.when(step == 1)
    def _():
        z = dot(nrm_ref[RIM:], w[:, :STATE]) + dtb_ref[...]
        live = iota(z.shape, 1) < heads
        dt = jnp.where(live, jnp.maximum(z, 0.0) + jnp.log1p(jnp.exp(-jnp.abs(z))), 0.0)
        dt_ref[...] = dt
        sig_ref[...] = jnp.where(live, logistic(z), 0.0)
        change = dt * rate_ref[...]
        tri = lower(BLOCK).astype(f32)
        lam = jnp.concatenate(
            [dot(tri, change[block_of(b)], precision=PRECISE) for b in range(blocks)], axis=0
        )
        lam_ref[...] = lam
        across = lam.T
        for g in range(lamt_ref.shape[0]):
            lamt_ref[g] = across[PER * g : PER * (g + 1)]
        total = None
        rows = []
        for b in range(blocks):
            e_sc[block_of(b)] = split(end_weights(starts, lam, b) * dt[block_of(b)])
            last = (b + 1) * BLOCK - 1
            decay = jnp.where(
                starts[last : last + 1] < b * BLOCK, jnp.exp(lam[last : last + 1]), 0.0
            )
            decay = jnp.where(iota(decay.shape, 1) < heads, decay, 0.0)
            rows.append(decay)
            total = decay if total is None else total * decay
        rows.append(total)
        rows.append(jnp.zeros((8 - len(rows), STATE), f32))
        dec_ref[...] = jnp.concatenate(rows, axis=0)
        state_ref[:RIM] = decay_rows(total)

    @pl.when(step >= 2)
    def _():
        group = step - 2
        xe = (conv() * spread(e_sc[...], group)).astype(bf16)
        total = None
        for b in range(blocks):
            fresh = dot(xe[block_of(b)], b_sc[block_of(b)], 0, 0)
            if b + 1 < blocks:
                fresh_ref[b] = fresh
            if total is None:
                total = fresh
            else:
                total = head_rows(dec_ref[b : b + 1], group) * total + fresh
        state_ref[...] = total.astype(state_ref.dtype)


def first(layout, nrm, slots, rest_at, cw, cb, dtb, rate, starts, heads):
    ext, d = nrm.shape
    length = starts.shape[0]
    blocks = length // BLOCK
    inner = heads * HEADDIM
    groups = inner // TILE
    col = lambda s: jnp.where(s == 0, groups, jnp.maximum(s - 2, 0))
    wcol = lambda s: rest_at + jnp.where(s < 2, groups + s, s - 2)
    tile = lambda s: jnp.maximum(s - 2, 0)
    full = lambda *shape: pl.BlockSpec(shape, lambda s: (0,) * len(shape))
    state = lambda s: jnp.where(s < 2, groups, s - 2)
    return pl.pallas_call(
        functools.partial(first_kernel, slots.plan),
        grid=(groups + 2,),
        in_specs=[
            SMEM,
            full(ext, d),
            *slots.tiles(wcol),
            pl.BlockSpec((cw.shape[0], TILE), lambda s: (0, col(s))),
            pl.BlockSpec((1, TILE), lambda s: (0, col(s))),
            full(1, STATE),
            full(1, STATE),
            full(length, 1),
        ],
        out_specs=[
            pl.BlockSpec((ext, TILE), lambda s: (0, col(s))),
            pl.BlockSpec((length, TILE), lambda s: (0, col(s))),
            full(length, STATE),
            full(length, STATE),
            full(length, STATE),
            full(groups, PER, length),
            pl.BlockSpec((TILE, STATE), lambda s: (state(s), 0)),
            pl.BlockSpec((blocks - 1, TILE, STATE), lambda s: (0, tile(s), 0)),
            full(8, STATE),
            full(d, ext),
        ],
        out_shape=[
            jax.ShapeDtypeStruct((ext, inner + 2 * STATE), bf16),
            jax.ShapeDtypeStruct((length, inner + 2 * STATE), bf16),
            jax.ShapeDtypeStruct((length, STATE), f32),
            jax.ShapeDtypeStruct((length, STATE), f32),
            jax.ShapeDtypeStruct((length, STATE), f32),
            jax.ShapeDtypeStruct((groups, PER, length), f32),
            jax.ShapeDtypeStruct((inner + RIM, STATE), bf16),
            jax.ShapeDtypeStruct((blocks - 1, inner, STATE), f32),
            jax.ShapeDtypeStruct((8, STATE), f32),
            jax.ShapeDtypeStruct((d, ext), bf16),
        ],
        scratch_shapes=[
            pltpu.VMEM((length, STATE), bf16),
            pltpu.VMEM((length, 2 * STATE), bf16),
            layout.scratch(TILE),
        ],
        compiler_params=pltpu.CompilerParams(vmem_limit_bytes=VMEM),
        cost_estimate=pl.CostEstimate(
            flops=2 * ext * d * (inner + 3 * STATE), bytes_accessed=12 * 2**20, transcendentals=0
        ),
        name="project",
    )(slots.near, nrm, *slots.arrays, cw, cb, dtb, rate, starts)


def pair_of(width):
    return iota((1, width), 1) < HEADDIM


def within_kernel(
    plan, at_ref, nrm_ref, *refs
):
    w_refs, rest = refs[: len(plan)], refs[len(plan) :]
    within_body(plan, at_ref, nrm_ref, w_refs, *rest)


def within_body(
    plan, at_ref, nrm_ref, w_refs, x_ref, bc_ref, dt_ref, lam_ref, lamt_ref, starts_ref, skip_ref,
    gate_ref, y_ref,
    cross_sc, mask_sc, dt_sc, w_sc,
):
    group = pl.program_id(0)
    length = starts_ref.shape[0]
    blocks = length // BLOCK

    @pl.when(group == 0)
    def _():
        act = silu(bc_ref[...].astype(f32)).astype(bf16)
        for b in range(blocks):
            s = block_of(b)
            cross_sc[b] = dot(act[s, STATE:], act[s, :STATE], 1, 1)
        fill_mask(mask_sc, starts_ref[...], blocks)
        dt_sc[...] = split(dt_ref[...])

    gate_ref[...] = dot(nrm_ref[RIM:], assemble(w_refs, w_sc, at_ref, plan)).astype(bf16)
    x = silu(x_ref[...].astype(f32))
    xd = (x * spread(dt_sc[...], group)).astype(bf16)
    lam = pltpu.roll(lam_ref[...], lax.rem(STATE - PER * group, STATE), 1)
    lamt = lamt_ref[group]
    left = pair_of(2 * HEADDIM)
    for b in range(blocks):
        s = block_of(b)
        parts = []
        for p in range(PER // 2):
            c = slice(2 * HEADDIM * p, 2 * HEADDIM * (p + 1))
            two = []
            for h in (2 * p, 2 * p + 1):
                gap = (lam[s, h : h + 1] - lamt[h : h + 1, s]) + mask_sc[b]
                two.append(dot((jnp.exp(gap) * cross_sc[b]).astype(bf16), xd[s, c]))
            parts.append(jnp.where(left, two[0], two[1]))
        y = jnp.concatenate(parts, axis=1) + skip_ref[...] * x[s]
        y_ref[s] = y.astype(bf16)


def within(layout, nrm, slots, gate_at, cv, dt, lam, lamt, starts, skip):
    ext, d = nrm.shape
    length = starts.shape[0]
    blocks = length // BLOCK
    groups = lamt.shape[0]
    inner = groups * TILE
    full = lambda *shape: pl.BlockSpec(shape, lambda s: (0,) * len(shape))
    tile = pl.BlockSpec((length, TILE), lambda s: (0, s))
    return pl.pallas_call(
        functools.partial(within_kernel, slots.plan),
        grid=(groups,),
        in_specs=[
            SMEM,
            full(ext, d),
            *slots.tiles(lambda s: gate_at + s),
            tile,
            pl.BlockSpec((length, TILE), lambda s: (0, groups)),
            full(length, STATE),
            full(length, STATE),
            full(groups, PER, length),
            full(length, 1),
            pl.BlockSpec((1, TILE), lambda s: (0, s)),
        ],
        out_specs=[tile, tile],
        out_shape=[
            jax.ShapeDtypeStruct((length, inner), bf16),
            jax.ShapeDtypeStruct((length, inner), bf16),
        ],
        scratch_shapes=[
            pltpu.VMEM((blocks, BLOCK, BLOCK), f32),
            pltpu.VMEM((blocks, BLOCK, BLOCK), f32),
            pltpu.VMEM((length, 2 * STATE), bf16),
            layout.scratch(TILE),
        ],
        compiler_params=pltpu.CompilerParams(vmem_limit_bytes=VMEM),
        cost_estimate=NO_COST,
        name="within",
    )(slots.near, nrm, *slots.arrays, cv, cv, dt, lam, lamt, starts, skip)


def states_of(s0, fresh_ref, dec_ref, group, blocks):
    found = [s0]
    for b in range(blocks - 1):
        found.append(head_rows(dec_ref[b : b + 1], group) * found[-1] + fresh_ref[b])
    return found


def unfold(wo_refs, wo_sc, at_ref, plan):
    rows, width = wo_sc.shape[-2:]
    short = wo_refs[0].shape[2]
    for wo_ref, (places, first_owner) in zip(wo_refs, plan):
        for i, r in enumerate(places):
            for q in range(wo_ref.shape[1]):
                for f in range(rows // short):
                    part = wo_ref[i, q, :, f * width : (f + 1) * width]
                    owner = at_ref[0] ^ (first_owner + q)
                    wo_sc[owner, at_ref[1] ^ r, f * short : (f + 1) * short] = part


def pieces_of(shape, group):
    share = shape[1] * shape[2]
    parts = share // TILE
    if parts == 1:
        return group, slice(None)
    many = TILE // shape[2]
    return group // parts, pl.ds(many * (group % parts), many)


def join_kernel(
    plan, at_ref, *refs
):
    wo_refs, rest = refs[: len(plan)], refs[len(plan) :]
    join_body(plan, at_ref, wo_refs, *rest)


def join_body(
    plan, at_ref, wo_refs, y_ref, bc_ref, lam_ref, starts_ref, gate_ref, s0_ref, fresh_ref, dec_ref, gain_ref,
    resid_ref, gain_next_ref,
    y_out_ref, gated_ref, scale_ref, next_ref, low_ref, nrm_ref,
    u_sc, c_sc, v_sc, sq_sc, wo_sc,
):
    group = pl.program_id(0)
    length = starts_ref.shape[0]
    blocks = length // BLOCK
    groups = v_sc.shape[0]
    inner = groups * TILE

    @pl.when(group == 0)
    def _():
        c_sc[...] = silu(bc_ref[:, STATE:].astype(f32)).astype(bf16)
        for b in range(blocks):
            u_sc[block_of(b)] = split(reach_weights(starts_ref[...], lam_ref[...], b))
        sq_sc[...] = jnp.zeros_like(sq_sc)

    u = spread(u_sc[...], group)
    before = states_of(s0_ref[...].astype(f32), fresh_ref, dec_ref, group, blocks)
    carried = jnp.concatenate(
        [dot(c_sc[block_of(b)], before[b].astype(bf16), 1, 1) for b in range(blocks)], axis=0
    )
    y = (y_ref[...].astype(f32) + u * carried).astype(bf16)
    y_out_ref[...] = y
    v = y.astype(f32) * silu(gate_ref[...].astype(f32))
    v_sc[group] = v
    sq = v * v
    sq_sc[...] += sq[:, :STATE] + sq[:, STATE:]

    @pl.when(group == groups - 1)
    def _():
        mean = jnp.sum(sq_sc[...], axis=1, keepdims=True) / inner
        scale = lax.rsqrt(mean + EPSILON)
        scale_ref[...] = scale
        acc = resid_ref[...]
        unfold(wo_refs, wo_sc, at_ref, plan)
        for g in range(groups):
            c = slice(g * TILE, (g + 1) * TILE)
            low = (v_sc[g] * scale * gain_ref[:, c]).astype(bf16)
            gated_ref[:, c] = low
            owner, piece = pieces_of(wo_sc.shape, g)
            acc = acc + dot(low, wo_sc[owner, piece].reshape(TILE, -1))
        next_ref[...] = acc
        low_ref[...] = acc.astype(bf16)
        norm = lax.rsqrt(jnp.mean(acc * acc, axis=1, keepdims=True) + EPSILON)
        nrm_ref[...] = (acc * norm * gain_next_ref[...]).astype(bf16)


def join(layout, slots, out_at, y, cv, lam, starts, gate, s0, fresh, dec, gain, resid, gain_next):
    length, inner = y.shape
    d = resid.shape[1]
    fold = inner // d
    blocks = length // BLOCK
    groups = inner // TILE
    full = lambda *shape: pl.BlockSpec(shape, lambda s: (0,) * len(shape))
    tile = pl.BlockSpec((length, TILE), lambda s: (0, s))
    return pl.pallas_call(
        functools.partial(join_kernel, slots.plan),
        grid=(groups,),
        in_specs=[
            SMEM,
            *slots.whole(inner, out_at),
            tile,
            pl.BlockSpec((length, TILE), lambda s: (0, groups)),
            full(length, STATE),
            full(length, 1),
            tile,
            pl.BlockSpec((TILE, STATE), lambda s: (s, 0)),
            pl.BlockSpec((blocks - 1, TILE, STATE), lambda s: (0, s, 0)),
            full(8, STATE),
            full(1, inner),
            full(length, d),
            full(1, d),
        ],
        out_specs=[
            tile,
            full(length, inner),
            full(length, 1),
            full(length, d),
            full(length, d),
            full(length, d),
        ],
        out_shape=[
            jax.ShapeDtypeStruct((length, inner), bf16),
            jax.ShapeDtypeStruct((length, inner), bf16),
            jax.ShapeDtypeStruct((length, 1), f32),
            jax.ShapeDtypeStruct((length, d), f32),
            jax.ShapeDtypeStruct((length, d), bf16),
            jax.ShapeDtypeStruct((length, d), bf16),
        ],
        scratch_shapes=[
            pltpu.VMEM((length, 2 * STATE), bf16),
            pltpu.VMEM((length, STATE), bf16),
            pltpu.VMEM((groups, length, TILE), f32),
            pltpu.VMEM((length, STATE), f32),
            pltpu.VMEM((layout.owners, layout.places, fold * layout.rows, d), bf16),
        ],
        compiler_params=pltpu.CompilerParams(vmem_limit_bytes=VMEM),
        cost_estimate=NO_COST,
        name="join",
    )(slots.near, *slots.arrays, y, cv, lam, starts, gate, s0, fresh, dec, gain, resid, gain_next)


def gate_back_kernel(
    plan, skip, at_ref, *refs
):
    refs = refs[skip:]
    wo_refs, rest = refs[: len(plan)], refs[len(plan) :]
    gate_back_body(plan, at_ref, wo_refs, *rest)


def gate_back_body(
    plan, at_ref, wo_refs, grad_ref, y_ref, gate_ref, gated_ref, scale_ref, gain_ref, x_ref, bc_ref, lam_ref,
    starts_ref, dec_ref,
    gy_ref, ggate_ref, ggain_ref, gskip_ref, later_ref, total_ref, *more
):
    gg_sc, u_sc, c_sc, dot_sc, wo_sc, dwo_sc = more[-6:]
    keep_ref, send_ref = more[0], more[-7]
    phase, group = pl.program_id(0), pl.program_id(1)
    length = starts_ref.shape[0]
    blocks = length // BLOCK
    groups = gg_sc.shape[0]
    inner = groups * TILE

    @pl.when((phase == 0) & (group == 0))
    def _():
        c_sc[...] = silu(bc_ref[:, STATE:].astype(f32)).astype(bf16)
        for b in range(blocks):
            u_sc[block_of(b)] = split(reach_weights(starts_ref[...], lam_ref[...], b))
        dot_sc[...] = jnp.zeros_like(dot_sc)
        unfold(wo_refs, wo_sc, at_ref, plan)

    y = y_ref[...].astype(f32)
    gate = gate_ref[...].astype(f32)
    sig = logistic(gate)
    act = gate * sig
    v = y * act
    scale = scale_ref[...]

    @pl.when(phase == 0)
    def _():
        owners, places, rows, width = wo_sc.shape
        owner, piece = pieces_of(wo_sc.shape, group)
        gg = dot(grad_ref[...], wo_sc[owner, piece].reshape(TILE, width), 1, 1)
        gv = gg * v
        ggain_ref[...] = jnp.sum(gv * scale, axis=0, keepdims=True)
        total_ref[:RIM] = decay_rows(dec_ref[blocks : blocks + 1])
        gv = gv * gain_ref[...]
        dot_sc[...] += gv[:, :STATE] + gv[:, STATE:]
        gg_sc[group] = gg * gain_ref[...]
        dwo = dot(gated_ref[...], grad_ref[...], 0, 0).astype(bf16)
        dwo_sc[owner, piece] = dwo.reshape(-1, rows, width)

        @pl.when(group == groups - 1)
        def _():
            for r in range(places):
                target = send_ref if r % 2 else keep_ref
                for q in range(owners):
                    target[r // 2, q] = dwo_sc[at_ref[2] ^ q, at_ref[3] ^ r]

    @pl.when(phase == 1)
    def _():
        @pl.when(group == 0)
        def _():
            total = jnp.sum(dot_sc[...], axis=1, keepdims=True)
            dot_sc[...] = jnp.broadcast_to(
                total * scale * scale * scale * (1.0 / inner), dot_sc.shape
            )

        gv = scale * gg_sc[group] - v * dot_sc[:, :1]
        gy = gv * act
        ggate_ref[...] = (gv * y * (sig + act * (1.0 - sig))).astype(bf16)
        low = gy.astype(bf16)
        gy_ref[...] = low
        x = silu(x_ref[...].astype(f32))
        gskip_ref[...] = jnp.sum(low.astype(f32) * x, axis=0, keepdims=True)
        ug = (gy * spread(u_sc[...], group)).astype(bf16)
        total = None
        for b in reversed(range(blocks)):
            direct = dot(ug[block_of(b)], c_sc[block_of(b)], 0, 0)
            if total is None:
                total = direct
            else:
                total = head_rows(dec_ref[b : b + 1], group) * total + direct
            if b > 0:
                later_ref[b - 1] = direct
        total_ref[...] = total.astype(total_ref.dtype)


def gate_back(after, at, layout, slots, out_at, grad_low, y, gate, gated, scale, gain, cv, lam, starts, dec):
    length, inner = y.shape
    d = grad_low.shape[1]
    rows = inner // d * layout.rows
    blocks = length // BLOCK
    groups = inner // TILE
    full = lambda *shape: pl.BlockSpec(shape, lambda p, s: (0,) * len(shape))
    early = lambda p, s: jnp.where(p == 0, s, groups - 1)
    late = lambda p, s: s * p
    tile = pl.BlockSpec((length, TILE), lambda p, s: (0, s))
    late_tile = pl.BlockSpec((length, TILE), lambda p, s: (0, late(p, s)))
    return pl.pallas_call(
        functools.partial(gate_back_kernel, slots.plan, len(after)),
        grid=(2, groups),
        in_specs=[
            SMEM,
            *[pl.BlockSpec(memory_space=pl.ANY)] * len(after),
            *slots.whole(inner, out_at),
            full(length, d),
            tile,
            tile,
            pl.BlockSpec((length, TILE), lambda p, s: (0, early(p, s))),
            full(length, 1),
            pl.BlockSpec((1, TILE), lambda p, s: (0, s)),
            late_tile,
            pl.BlockSpec((length, TILE), lambda p, s: (0, groups)),
            full(length, STATE),
            full(length, 1),
            full(8, STATE),
        ],
        out_specs=[
            late_tile,
            late_tile,
            pl.BlockSpec((1, TILE), lambda p, s: (0, early(p, s))),
            pl.BlockSpec((1, TILE), lambda p, s: (0, late(p, s))),
            pl.BlockSpec((blocks - 1, TILE, STATE), lambda p, s: (0, late(p, s), 0)),
            pl.BlockSpec((TILE, STATE), lambda p, s: (jnp.where(p == 0, groups, s), 0)),
            *[full(*a.shape) for a in layout.dealt_shape(rows, d)],
        ],
        out_shape=[
            jax.ShapeDtypeStruct((length, inner), bf16),
            jax.ShapeDtypeStruct((length, inner), bf16),
            jax.ShapeDtypeStruct((1, inner), f32),
            jax.ShapeDtypeStruct((1, inner), f32),
            jax.ShapeDtypeStruct((blocks - 1, inner, STATE), f32),
            jax.ShapeDtypeStruct((inner + RIM, STATE), bf16),
            *layout.dealt_shape(rows, d),
        ],
        scratch_shapes=[
            pltpu.VMEM((groups, length, TILE), f32),
            pltpu.VMEM((length, 2 * STATE), bf16),
            pltpu.VMEM((length, STATE), bf16),
            pltpu.VMEM((length, STATE), f32),
            pltpu.VMEM((layout.owners, layout.places, rows, d), bf16),
            pltpu.VMEM((layout.owners, layout.places, rows, d), bf16),
        ],
        compiler_params=pltpu.CompilerParams(vmem_limit_bytes=VMEM),
        cost_estimate=NO_COST,
        name="gate_back",
    )(jnp.concatenate([slots.near, at]), *after, *slots.arrays, grad_low, y, gate, gated, scale, gain, cv, cv, lam, starts, dec)


def within_back_kernel(
    plan, skip, at_ref, *refs
):
    refs = refs[skip:]
    w_refs, rest = refs[: len(plan)], refs[len(plan) :]
    within_back_body(plan, at_ref, w_refs, *rest)


def within_back_body(
    plan, at_ref, w_refs, gy_ref, x_ref, bc_ref, dt_ref, lam_ref, lamt_ref, starts_ref, s0_ref, fresh_ref, dec_ref,
    ggate_ref, nrmt_ref,
    gxd_ref, glam_ref, gbc_ref, gnrm_ref, *more
):
    cross_sc, gcross_sc, mask_sc, dt_sc, u_sc, act_sc, w_sc, d_sc = more[-8:]
    keep_ref, send_ref = more[0], more[-9]
    group = pl.program_id(0)
    length = starts_ref.shape[0]
    blocks = length // BLOCK
    groups = lamt_ref.shape[0]

    @pl.when(group == 0)
    def _():
        act = silu(bc_ref[...].astype(f32)).astype(bf16)
        act_sc[...] = act
        for b in range(blocks):
            s = block_of(b)
            cross_sc[b] = dot(act[s, STATE:], act[s, :STATE], 1, 1)
            u_sc[s] = split(reach_weights(starts_ref[...], lam_ref[...], b))
        fill_mask(mask_sc, starts_ref[...], blocks)
        dt_sc[...] = split(dt_ref[...])
        gcross_sc[...] = jnp.zeros_like(gcross_sc)
        glam_ref[...] = jnp.zeros_like(glam_ref)
        gbc_ref[...] = jnp.zeros_like(gbc_ref)
        gnrm_ref[...] = jnp.zeros_like(gnrm_ref)

    ggate = ggate_ref[...]
    gnrm_ref[...] += dot(ggate, assemble(w_refs, w_sc, at_ref, plan), 1, 1)
    deal(dot(nrmt_ref[:, RIM:], ggate), keep_ref, send_ref, d_sc, at_ref)

    x = silu(x_ref[...].astype(f32))
    xd = (x * spread(dt_sc[...], group)).astype(bf16)
    gy = gy_ref[...]
    u = spread(u_sc[...], group)
    before = states_of(s0_ref[...].astype(f32), fresh_ref, dec_ref, group, blocks)
    lam = pltpu.roll(lam_ref[...], lax.rem(STATE - PER * group, STATE), 1)
    lamt = lamt_ref[group]
    left = pair_of(2 * HEADDIM)
    for b in range(blocks):
        s = block_of(b)
        gcross = gcross_sc[b]
        ys, gxds = [], []
        for p in range(PER // 2):
            c = slice(2 * HEADDIM * p, 2 * HEADDIM * (p + 1))
            y2, g2 = [], []
            for h in (2 * p, 2 * p + 1):
                decay = jnp.exp((lam[s, h : h + 1] - lamt[h : h + 1, s]) + mask_sc[b])
                weight = (decay * cross_sc[b]).astype(bf16)
                y2.append(dot(weight, xd[s, c]))
                g2.append(dot(weight, gy[s, c], 0, 0))
                own = left if h % 2 == 0 else ~left
                mine = jnp.where(own, gy[s, c], jnp.zeros((), bf16))
                gcross = gcross + dot(mine, xd[s, c], 1, 1) * decay
            ys.append(jnp.where(left, y2[0], y2[1]))
            gxds.append(jnp.where(left, g2[0], g2[1]))
        gcross_sc[b] = gcross
        state = before[b].astype(bf16)
        y = jnp.concatenate(ys, axis=1) + u[s] * dot(act_sc[s, STATE:], state, 1, 1)
        gxd = jnp.concatenate(gxds, axis=1)
        gxd_ref[s] = gxd
        gyf = gy[s].astype(f32)
        glam_ref[s] += gather_heads(gyf * y - xd[s].astype(f32) * gxd, group)
        gbc_ref[s, STATE:] += dot((u[s] * gyf).astype(bf16), state)

    @pl.when(group == groups - 1)
    def _():
        for b in range(blocks):
            s = block_of(b)
            low = gcross_sc[b].astype(bf16)
            gbc_ref[s, :STATE] += dot(low, act_sc[s, STATE:], 0, 0)
            gbc_ref[s, STATE:] += dot(low, act_sc[s, :STATE])


def within_back(after, at, layout, slots, gate_at, gy, cv, dt, lam, lamt, starts, s0, fresh, dec, ggate, nrmt):
    length, inner = gy.shape
    d, ext = nrmt.shape
    blocks = length // BLOCK
    groups = inner // TILE
    full = lambda *shape: pl.BlockSpec(shape, lambda s: (0,) * len(shape))
    tile = pl.BlockSpec((length, TILE), lambda s: (0, s))
    return pl.pallas_call(
        functools.partial(within_back_kernel, slots.plan, len(after)),
        grid=(groups,),
        in_specs=[
            SMEM,
            *[pl.BlockSpec(memory_space=pl.ANY)] * len(after),
            *slots.tiles(lambda s: gate_at + s),
            tile,
            tile,
            pl.BlockSpec((length, TILE), lambda s: (0, groups)),
            full(length, STATE),
            full(length, STATE),
            full(groups, PER, length),
            full(length, 1),
            pl.BlockSpec((TILE, STATE), lambda s: (s, 0)),
            pl.BlockSpec((blocks - 1, TILE, STATE), lambda s: (0, s, 0)),
            full(8, STATE),
            tile,
            full(d, ext),
        ],
        out_specs=[
            tile, full(length, STATE), full(length, 2 * STATE), full(length, d),
            *layout.dealt(lambda s: s),
        ],
        out_shape=[
            jax.ShapeDtypeStruct((length, inner), f32),
            jax.ShapeDtypeStruct((length, STATE), f32),
            jax.ShapeDtypeStruct((length, 2 * STATE), f32),
            jax.ShapeDtypeStruct((length, d), f32),
            *layout.dealt_shape(layout.rows, inner),
        ],
        scratch_shapes=[
            pltpu.VMEM((blocks, BLOCK, BLOCK), f32),
            pltpu.VMEM((blocks, BLOCK, BLOCK), f32),
            pltpu.VMEM((blocks, BLOCK, BLOCK), f32),
            pltpu.VMEM((length, 2 * STATE), bf16),
            pltpu.VMEM((length, 2 * STATE), bf16),
            pltpu.VMEM((length, 2 * STATE), bf16),
            layout.scratch(TILE),
            layout.scratch(TILE),
        ],
        compiler_params=pltpu.CompilerParams(vmem_limit_bytes=VMEM),
        cost_estimate=NO_COST,
        name="within_back",
    )(jnp.concatenate([slots.near, at]), *after, *slots.arrays, gy, cv, cv, dt, lam, lamt, starts, s0, fresh, dec, ggate, nrmt)


def last_kernel(
    plan, skip, at_ref, *refs
):
    refs = refs[skip:]
    w_refs, rest = refs[: len(plan)], refs[len(plan) :]
    last_body(plan, at_ref, w_refs, *rest)


def last_body(
    plan, at_ref, w_refs, gxd_ref, cv_ref, cin_ref, gy_ref, bc_ref, dt_ref, lam_ref, sig_ref, starts_ref, gend_ref,
    later_ref, s0_ref, fresh_ref, dec_ref, nrmt_ref, glam_ref, gbc_ref, gin_ref, skip_ref,
    rate_ref, cw_ref,
    gnrm_ref, gcw_ref, gcb_ref, gsmall_ref, *more
):
    b_sc, gb_sc, dt_sc, e_sc, gdt_sc, zs_sc, over_sc, gp_sc, w_sc, d_sc = more[-10:]
    keep_ref, send_ref = more[0], more[-11]
    step = pl.program_id(0)
    length = starts_ref.shape[0]
    blocks = length // BLOCK
    groups = pl.num_programs(0) - 2
    starts = starts_ref[...]
    ext = gnrm_ref.shape[0]

    @pl.when(step == 0)
    def _():
        b_sc[...] = silu(bc_ref[:, :STATE].astype(f32)).astype(bf16)
        gb_sc[...] = gbc_ref[:, :STATE]
        dt_sc[...] = split(dt_ref[...])
        for b in range(blocks):
            e_sc[block_of(b)] = split(end_weights(starts, lam_ref[...], b))
        gdt_sc[...] = jnp.zeros_like(gdt_sc)
        zs_sc[...] = jnp.zeros_like(zs_sc)
        over_sc[...] = jnp.zeros_like(over_sc)
        gnrm_ref[:RIM] = jnp.zeros((RIM, gnrm_ref.shape[1]), f32)
        gnrm_ref[RIM:] = gin_ref[...]

    def conv_back(gact):
        gcv = gact * dsilu(cv_ref[...].astype(f32))
        gcb_ref[...] = jnp.sum(gcv, axis=0, keepdims=True)
        place = iota((length, 1), 0)
        taps = cw_ref.shape[0]
        cin = cin_ref[...].astype(f32)
        zeros = jnp.zeros((RIM, TILE), f32)
        acc = None
        rows = []
        for k in range(taps):
            back = taps - 1 - k
            term = gcv if back == 0 else jnp.where(place - back >= starts, gcv, 0.0)
            moved = jnp.concatenate([zeros, term], axis=0)
            if back:
                moved = pltpu.roll(moved, ext - back, 0)
            rows.append(jnp.sum(moved * cin, axis=0, keepdims=True))
            part = cw_ref[k : k + 1] * moved
            acc = part if acc is None else acc + part
        gcw_ref[...] = jnp.concatenate(rows, axis=0)
        gp_sc[...] = acc.astype(bf16)

    @pl.when(step < groups)
    def _():
        group = step
        x = silu(cv_ref[...].astype(f32))
        dt = spread(dt_sc[...], group)
        e = spread(e_sc[...], group)
        xd = x * dt
        gend = gend_ref[...].astype(f32)
        grads = [None] * blocks
        for b in reversed(range(blocks)):
            grads[b] = gend
            if b > 0:
                gend = head_rows(dec_ref[b : b + 1], group) * gend + later_ref[b - 1]
        before = states_of(s0_ref[...].astype(f32), fresh_ref, dec_ref, group, blocks)
        parts = []
        for b in range(blocks):
            s = block_of(b)
            low = grads[b].astype(bf16)
            parts.append(e[s] * dot(b_sc[s], low, 1, 1))
            gb_sc[s] += dot((e[s] * xd[s]).astype(bf16), low)
            over = jnp.sum(grads[b] * before[b], axis=1, keepdims=True)
            over_sc[b : b + 1] += dec_ref[b : b + 1] * jnp.sum(
                jnp.where(chooser(group), over, 0.0), axis=0, keepdims=True
            )
        more = jnp.concatenate(parts, axis=0)
        gxd = gxd_ref[...] + more
        zs_sc[...] += gather_heads(xd * more, group)
        gdt_sc[...] += gather_heads(x * gxd, group)
        conv_back(dt * gxd + skip_ref[...] * gy_ref[...].astype(f32))

    @pl.when(step == groups)
    def _():
        conv_back(jnp.concatenate([gb_sc[...], gbc_ref[:, STATE:]], axis=1))

    @pl.when(step <= groups)
    def _():
        gp = gp_sc[...]
        gnrm_ref[...] += dot(gp, assemble(w_refs, w_sc, at_ref, plan), 1, 1)
        deal(dot(nrmt_ref[...], gp), keep_ref, send_ref, d_sc, at_ref)

    @pl.when(step == groups + 1)
    def _():
        tri = lower(BLOCK).astype(f32)
        glam = glam_ref[...] - zs_sc[...]
        rows = []
        for b in range(blocks):
            s = block_of(b)
            end = jnp.sum(zs_sc[s], axis=0, keepdims=True) + over_sc[b : b + 1]
            rows.append(dot(tri, glam[s], 0, 0, precision=PRECISE) + end)
        back = jnp.concatenate(rows, axis=0)
        dt = dt_ref[...]
        gz = (gdt_sc[...] + rate_ref[...] * back) * sig_ref[...]
        gsmall_ref[0:1] = jnp.sum(gz, axis=0, keepdims=True)
        gsmall_ref[1:2] = rate_ref[...] * jnp.sum(dt * back, axis=0, keepdims=True)
        gsmall_ref[2:8] = jnp.zeros((6, STATE), f32)
        low = gz.astype(bf16)
        heads = groups * PER
        w = assemble(w_refs, w_sc, at_ref, plan)[:, :STATE]
        w = jnp.where(iota(w.shape, 1) < heads, w, jnp.zeros((), bf16))
        gnrm_ref[RIM:] += dot(low, w, 1, 1)
        dw = dot(nrmt_ref[:, RIM:], low)
        deal(jnp.concatenate([dw, jnp.zeros_like(dw)], axis=1), keep_ref, send_ref, d_sc, at_ref)


def last(
    after, at, layout, slots, rest_at, gxd, cv, cin, gy, dt, lam, sig, starts, gend, later, s0, fresh, dec, nrmt, glam, gbc,
    gin, skip, rate, cw,
):
    length, inner = gy.shape
    d, ext = nrmt.shape
    blocks = length // BLOCK
    groups = inner // TILE
    heads = inner // HEADDIM
    taps = cw.shape[0]
    full = lambda *shape: pl.BlockSpec(shape, lambda s: (0,) * len(shape))
    own = lambda s: jnp.minimum(s, groups - 1)
    col = lambda s: jnp.minimum(s, groups)
    tile = pl.BlockSpec((length, TILE), lambda s: (0, own(s)))
    state = pl.BlockSpec((TILE, STATE), lambda s: (own(s), 0))
    states = pl.BlockSpec((blocks - 1, TILE, STATE), lambda s: (0, own(s), 0))
    return pl.pallas_call(
        functools.partial(last_kernel, slots.plan, len(after)),
        grid=(groups + 2,),
        in_specs=[
            SMEM,
            *[pl.BlockSpec(memory_space=pl.ANY)] * len(after),
            *slots.tiles(lambda s: rest_at + s),
            tile,
            pl.BlockSpec((length, TILE), lambda s: (0, col(s))),
            pl.BlockSpec((ext, TILE), lambda s: (0, col(s))),
            tile,
            pl.BlockSpec((length, TILE), lambda s: (0, groups)),
            full(length, STATE),
            full(length, STATE),
            full(length, STATE),
            full(length, 1),
            state,
            states,
            state,
            states,
            full(8, STATE),
            full(d, ext),
            full(length, STATE),
            full(length, 2 * STATE),
            full(length, d),
            pl.BlockSpec((1, TILE), lambda s: (0, own(s))),
            full(1, STATE),
            pl.BlockSpec((taps, TILE), lambda s: (0, col(s))),
        ],
        out_specs=[
            full(ext, d),
            pl.BlockSpec((taps, TILE), lambda s: (0, col(s))),
            pl.BlockSpec((1, TILE), lambda s: (0, col(s))),
            full(8, STATE),
            *layout.dealt(lambda s: s),
        ],
        out_shape=[
            jax.ShapeDtypeStruct((ext, d), f32),
            jax.ShapeDtypeStruct((taps, inner + 2 * STATE), f32),
            jax.ShapeDtypeStruct((1, inner + 2 * STATE), f32),
            jax.ShapeDtypeStruct((8, STATE), f32),
            *layout.dealt_shape(layout.rows, inner + 2 * STATE + heads),
        ],
        scratch_shapes=[
            pltpu.VMEM((length, STATE), bf16),
            pltpu.VMEM((length, STATE), f32),
            pltpu.VMEM((length, 2 * STATE), bf16),
            pltpu.VMEM((length, 2 * STATE), bf16),
            pltpu.VMEM((length, STATE), f32),
            pltpu.VMEM((length, STATE), f32),
            pltpu.VMEM((8, STATE), f32),
            pltpu.VMEM((ext, TILE), bf16),
            layout.scratch(TILE),
            layout.scratch(TILE),
        ],
        compiler_params=pltpu.CompilerParams(vmem_limit_bytes=VMEM),
        cost_estimate=NO_COST,
        name="last",
    )(
        jnp.concatenate([slots.near, at]), *after, *slots.arrays, gxd, cv, cin, gy, cv, dt, lam, sig, starts, gend, later, s0, fresh, dec, nrmt,
        glam, gbc, gin, skip, rate, cw,
    )


def rms_back(resid, gain, grad_normed):
    width = resid.shape[1]
    scale = lax.rsqrt(jnp.mean(resid * resid, axis=1, keepdims=True) + EPSILON)
    scaled = grad_normed * gain
    inner = jnp.sum(scaled * resid, axis=1, keepdims=True)
    grad = scale * scaled - resid * (inner * scale * scale * scale / width)
    return grad, jnp.sum(grad_normed * resid * scale, axis=0)


def passed_along(shard, axis, by):
    devices = lax.axis_size(axis)
    pairs = [(i, i + by) for i in range(devices) if 0 <= i + by < devices]
    return lax.ppermute(shard, axis, pairs)


def swap(value, axis, by):
    return lax.ppermute(value, axis, [(i, i ^ by) for i in range(lax.axis_size(axis))])


def decay_of(ref, at):
    return ref[at : at + 1].astype(f32) + ref[at + 1 : at + 2].astype(f32)


def joint_kernel(reverse, at_ref, mine_ref, other_ref, *refs):
    sent_ref = refs[-1]
    half = sent_ref.shape[0] - RIM
    odd = at_ref[1] % 2
    mine, other = decay_of(mine_ref, 2 * half), decay_of(other_ref, 2 * half)
    by = jnp.where((odd == 1) == reverse, other, mine)
    for g in range(half // TILE):
        rows = pl.ds(pl.multiple_of(odd * half + g * TILE, TILE), TILE)
        here, there = mine_ref[rows].astype(f32), other_ref[rows].astype(f32)
        first = jnp.where((odd == 1) == reverse, here, there)
        second = jnp.where((odd == 1) == reverse, there, here)
        scale = head_rows(by, odd * (half // TILE) + g)
        sent_ref[g * TILE : (g + 1) * TILE] = (scale * first + second).astype(bf16)
    sent_ref[half:] = decay_rows(mine * other)


def entering_kernel(reverse, pairs, at_ref, *refs):
    got, out_ref = refs[: pairs - 1], refs[-1]
    half = out_ref.shape[0]
    odd, chip = at_ref[1] % 2, at_ref[1] // 2
    decays = [decay_of(a, half) for a in got]
    shares = []
    for i in range(1, pairs):
        source = chip ^ i
        counts = source > chip if reverse else source < chip
        share = jnp.where(counts, jnp.ones((1, STATE), f32), 0.0)
        for j in range(1, pairs):
            if j != i:
                by = chip ^ j
                inside = (by < source) & (by > chip) if reverse else (by > source) & (by < chip)
                share = jnp.where(inside, share * decays[j - 1], share)
        shares.append(share)
    for g in range(half // TILE):
        rows = slice(g * TILE, (g + 1) * TILE)
        total = None
        for share, a in zip(shares, got):
            part = head_rows(share, odd * (half // TILE) + g) * a[rows].astype(f32)
            total = part if total is None else total + part
        out_ref[rows] = total.astype(bf16)


def behind_kernel(reverse, at_ref, half_ref, rest_ref, other_ref, out_ref):
    half = half_ref.shape[0]
    odd = at_ref[1] % 2
    decay = decay_of(other_ref, 2 * half)
    for g in range(2 * half // TILE):
        rows = slice(g * TILE, (g + 1) * TILE)
        upper = g * TILE >= half
        short = slice(rows.start % half, rows.start % half + TILE)
        own = (odd == 1) == upper
        value = jnp.where(own, half_ref[short].astype(f32), rest_ref[short].astype(f32))
        later = head_rows(decay, g) * value + other_ref[rows].astype(f32)
        out_ref[rows] = jnp.where((odd == 1) != reverse, later, value)


def small_call(kernel, at, args, shapes, after=(), name=None):
    args = list(args) + list(after)
    count = len(args) - len(after)
    vmem = pl.BlockSpec(memory_space=pltpu.VMEM)
    return pl.pallas_call(
        kernel,
        in_specs=[SMEM] + [vmem] * count + [pl.BlockSpec(memory_space=pl.ANY)] * len(after),
        out_specs=[vmem] * len(shapes),
        out_shape=shapes,
        compiler_params=pltpu.CompilerParams(vmem_limit_bytes=VMEM),
        cost_estimate=NO_COST,
        name=name,
    )(at, *args)


def carried_over(here, state, reverse, meanwhile):
    pairs = lax.axis_size("seq") // 2
    rows = state.shape[0] - RIM
    other = swap(state, "seq", 1)
    sent_shape = jax.ShapeDtypeStruct((rows // 2 + RIM, STATE), bf16)
    (sent,) = small_call(
        functools.partial(joint_kernel, reverse), here, [state, other], [sent_shape], name="joint"
    )
    got = [swap(sent, "seq", 2 * i) for i in range(1, pairs)]
    beside = meanwhile(sent)
    half_shape = jax.ShapeDtypeStruct((rows // 2, STATE), bf16)
    (half,) = small_call(
        functools.partial(entering_kernel, reverse, pairs), here, got, [half_shape],
        after=[beside[0]], name="entering",
    )
    rest = swap(half, "seq", 1)
    (whole,) = small_call(
        functools.partial(behind_kernel, reverse), here, [half, rest, other],
        [jax.ShapeDtypeStruct((rows, STATE), f32)], name="behind",
    )
    return whole, beside


def cut_kernel(ins, at_ref, in_ref, out_ref, *refs):
    target = refs[-1]
    rows, share = target.shape[0], in_ref.shape[2]

    @pl.when(pl.program_id(0) < ins)
    def _():
        pick = iota((rows, share), 1) == rows * at_ref[1] + iota((rows, share), 0)
        target[...] = dot(pick.astype(f32).astype(bf16), in_ref[0], 1, 1).astype(bf16)

    @pl.when(pl.program_id(0) >= ins)
    def _():
        target[...] = out_ref[0]


CUT = 512


def cut(at, layout, layer, in_turned, out_weight, late, after=()):
    wide, share = in_turned.shape[1:]
    width = out_weight.shape[2]
    fold = out_weight.shape[1] // share
    inner = fold * width
    across = width // CUT
    first = 0 if late else inner // CUT
    ins = inner // CUT if late else -(-(wide - inner) // CUT)
    outs = fold * across if late else 0

    def out_tile(s, at_ref):
        s = jnp.maximum(s - ins, 0)
        return (layer, at_ref[1] * fold + s // across, s % across)

    return pl.pallas_call(
        functools.partial(cut_kernel, ins),
        grid_spec=pltpu.PrefetchScalarGridSpec(
            num_scalar_prefetch=1,
            grid=(ins + outs,),
            in_specs=[
                pl.BlockSpec(
                    (1, CUT, share), lambda s, at_ref: (layer, first + jnp.minimum(s, ins - 1), 0)
                ),
                pl.BlockSpec((1, layout.rows, CUT), out_tile),
            ]
            + [pl.BlockSpec(memory_space=pl.ANY)] * len(after),
            out_specs=pl.BlockSpec((layout.rows, CUT), lambda s, at_ref: (0, s)),
        ),
        out_shape=jax.ShapeDtypeStruct((layout.rows, 2 * inner if late else wide - inner), bf16),
        compiler_params=pltpu.CompilerParams(vmem_limit_bytes=VMEM),
        cost_estimate=NO_COST,
        name="cut",
    )(at, in_turned, out_weight, *after)


X, Y = 2, 4


def over_wa(piece, layout):
    return [piece] + [swap(piece, "wa", q) for q in range(1, layout.owners)]


def stack_kernel(count, *refs):
    for i in range(count):
        refs[-1][0, i] = refs[i][...]


def stack(pieces, after=()):
    vmem = pl.BlockSpec(memory_space=pltpu.VMEM)
    return pl.pallas_call(
        functools.partial(stack_kernel, len(pieces)),
        in_specs=[vmem] * len(pieces) + [pl.BlockSpec(memory_space=pl.ANY)] * len(after),
        out_specs=vmem,
        out_shape=jax.ShapeDtypeStruct((1, len(pieces), *pieces[0].shape), pieces[0].dtype),
        compiler_params=pltpu.CompilerParams(vmem_limit_bytes=VMEM),
        cost_estimate=NO_COST,
        name="stack",
    )(*pieces, *after)


def straight(here, pieces, after=()):
    own = stack(pieces, after)
    arrays = [own] + [swap(own, "seq", by) for by in (X, Y, X + Y)]
    plan = [((r,), 0) for r in (0, X, Y, X + Y)]
    return Slots(
        here, arrays + [swap(a, "seq", 1) for a in arrays],
        plan + [((r + 1,), 0) for (r,), _ in plan],
    )


def halved(here, pieces, after=()):
    half = len(pieces) // 2
    arrays, plan, firsts = [], [], []
    for some, first_owner, one, two in ((pieces[:half], 0, X, Y), (pieces[half:], half, Y, X)):
        own = stack(some, after)
        firsts.append((own, swap(own, "seq", one), first_owner, one, two))
    for own, got, first_owner, one, two in firsts:
        both = stack([own[0], got[0]])[0]
        arrays += [both, swap(both, "seq", two)]
        plan += [((0, one), first_owner), ((two, one + two), first_owner)]
    return Slots(here, arrays, plan)


def near_by(slots, after=()):
    arrays = [tie(a, after) if after else a for a in slots.arrays]
    return Slots(
        slots.near, arrays + [swap(a, "seq", 1) for a in arrays],
        slots.plan + tuple((tuple(r + 1 for r in places), owner) for places, owner in slots.plan),
    )


def gathered(piece, layout):
    whole = lax.all_gather(piece, ("seq", "wa"))
    whole = whole.reshape(layout.places, layout.owners, *piece.shape)
    return Slots(jnp.zeros((2,), jnp.int32), [whole], [(tuple(range(layout.places)), 0)])


def tie(value, after):
    def kernel(*refs):
        pass

    return pl.pallas_call(
        kernel,
        in_specs=[pl.BlockSpec(memory_space=pl.ANY)] * (1 + len(after)),
        out_specs=pl.BlockSpec(memory_space=pl.ANY),
        out_shape=jax.ShapeDtypeStruct(value.shape, value.dtype),
        input_output_aliases={0: 0},
        cost_estimate=NO_COST,
        name="tie",
    )(value, *after)


def pack_kernel(count, rows, *refs):
    outs = refs[-4:]
    at = 0
    for k in range(count):
        keeps, gots = refs[4 * k : 4 * k + 2], refs[4 * k + 2 : 4 * k + 4]
        width = keeps[0].shape[-1]
        for f in range(keeps[0].shape[2] // rows):
            s = slice(f * rows, (f + 1) * rows)
            for part, pairs in ((0, ((0, 2), (1, 3))), (1, ((0, 1), (2, 3)))):
                for place, target in zip(pairs, outs[2 * part : 2 * part + 2]):
                    for n, i in enumerate(place):
                        total = keeps[part][i, 0, s].astype(f32) + gots[part][i, 0, s].astype(f32)
                        target[n, 0, :, at : at + width] = total.astype(bf16)
            at += width


def pack(parts, layout, after=()):
    half = layout.owners // 2
    flat, specs = [], []
    for pair in parts:
        for a in pair:
            block = (a.shape[0], 1, *a.shape[2:])
            flat += [a, a]
            specs += [
                pl.BlockSpec(block, lambda q: (0, q, 0, 0)),
                pl.BlockSpec(block, lambda q: (0, half + q, 0, 0)),
            ]
    width = sum(keep.shape[2] // layout.rows * keep.shape[3] for keep, _ in parts)
    out = jax.ShapeDtypeStruct((2, half, layout.rows, width), bf16)
    return pl.pallas_call(
        functools.partial(pack_kernel, len(parts), layout.rows),
        grid=(half,),
        in_specs=specs + [pl.BlockSpec(memory_space=pl.ANY)] * len(after),
        out_specs=[pl.BlockSpec((2, 1, layout.rows, width), lambda q: (0, q, 0, 0))] * 4,
        out_shape=[out] * 4,
        compiler_params=pltpu.CompilerParams(vmem_limit_bytes=VMEM),
        cost_estimate=NO_COST,
        name="pack",
    )(*flat, *after)


def halve_kernel(*refs):
    outs = refs[-4:]
    for part in (0, 1):
        keep, got = refs[2 * part : 2 * part + 2]
        for n in (0, 1):
            total = keep[n].astype(f32) + got[n].astype(f32)
            outs[2 * part + n][...] = total.astype(bf16)


def halve(arrays, after=()):
    two, half, rows, width = arrays[0].shape
    return pl.pallas_call(
        halve_kernel,
        grid=(half,),
        in_specs=[pl.BlockSpec((2, 1, rows, width), lambda q: (0, q, 0, 0))] * 4
        + [pl.BlockSpec(memory_space=pl.ANY)] * len(after),
        out_specs=[pl.BlockSpec((1, rows, width), lambda q: (q, 0, 0))] * 4,
        out_shape=[jax.ShapeDtypeStruct((half, rows, width), bf16)] * 4,
        compiler_params=pltpu.CompilerParams(vmem_limit_bytes=VMEM),
        cost_estimate=NO_COST,
        name="halve",
    )(*arrays, *after)


def apart_kernel(owners, at_ref, *refs):
    outs = refs[-owners:]
    half = owners // 2
    for q in range(owners):
        keep, got = refs[:2] if q < half else refs[2:4]
        outs[q][...] = (keep[q % half].astype(f32) + got[q % half].astype(f32)).astype(bf16)


def sum_kernel(count, at_ref, *refs):
    total = refs[0][...].astype(f32)
    for a in refs[1:count]:
        total = total + a[...].astype(f32)
    refs[-1][...] = total.astype(bf16)


class Collect:
    def __init__(self, here, layout):
        self.here, self.layout, self.parts = here, layout, {}

    def add(self, order, keep, send, after=()):
        if after:
            send = tie(send, after)
        self.parts[order] = (keep, swap(send, "seq", 1))
        return self.parts[order][1]

    def pack(self, *after):
        parts = [self.parts[k] for k in sorted(self.parts)]
        keep_a, send_a, keep_b, send_b = pack(parts, self.layout, after)
        self.now = [keep_a, swap(send_a, "seq", X), keep_b, swap(send_b, "seq", Y)]

    def halve(self, *after):
        keep_a, send_a, keep_b, send_b = halve(self.now, after)
        self.now = [keep_a, swap(send_a, "seq", Y), keep_b, swap(send_b, "seq", X)]

    def apart(self, *after):
        owners = self.layout.owners
        shape = jax.ShapeDtypeStruct(self.now[0].shape[1:], bf16)
        out = small_call(
            functools.partial(apart_kernel, owners), self.here, self.now, [shape] * owners, after,
            name="apart",
        )
        self.now = [out[0]] + [swap(out[q], "wa", q) for q in range(1, owners)]

    def whole(self, *after):
        shape = jax.ShapeDtypeStruct(self.now[0].shape, bf16)
        (own,) = small_call(
            functools.partial(sum_kernel, len(self.now)), self.here, self.now, [shape], after,
            name="whole",
        )
        self.now = [own]

    def gathered(self):
        places = lax.all_gather(self.now[0], "seq")
        self.now = [places[::2], places[1::2]]

    def spread(self, *after):
        own = tie(self.now[0], after) if after else self.now[0]
        even = jnp.stack([own] + [swap(own, "seq", by) for by in (X, Y, X + Y)])
        self.now = [even, swap(even, "seq", 1)]


WIDE = 1024


def place_kernel(ins, given, at_ref, steps_ref, even_ref, odd_ref, *refs):
    outs, own_sc = refs[given:-1], refs[-1]
    pairs = even_ref.shape[0]
    for i in range(pairs):
        own_sc[(2 * i) ^ at_ref[1]] = even_ref[i]
        own_sc[(2 * i + 1) ^ at_ref[1]] = odd_ref[i]
    value = own_sc[...].astype(f32)
    if ins:
        @pl.when(pl.program_id(0) < ins)
        def _():
            outs[0][0] = value.reshape(-1, WIDE).T

    if len(outs) > (ins > 0):
        @pl.when(pl.program_id(0) >= ins)
        def _():
            outs[-1][0, :, 0] = value


def place(at, layer, found, parts, outs, shapes, layout, absolute=False):
    even, odd = found
    if absolute:
        at = jnp.zeros_like(at)
    rows = layout.rows
    sources, in_tiles, out_tiles = [], [], []
    ins = sum(count for inside, _, count, _ in parts if inside)
    for inside, source, count, target in parts:
        sources += range(source, source + count)
        (in_tiles if inside else out_tiles).extend(range(target, target + count))
    steps = len(sources)
    in_tiles = in_tiles + (in_tiles[-1:] or [0]) * (steps - len(in_tiles))
    out_tiles = (out_tiles[:1] or [0]) * (steps - len(out_tiles)) + out_tiles
    table = jnp.array([sources, in_tiles, out_tiles], jnp.int32)
    across = shapes[1][-1] // WIDE
    both = [
        pl.BlockSpec((1, WIDE, shapes[0][2]), lambda s, at_ref, t: (layer, t[1, s], 0)),
        pl.BlockSpec(
            (1, layout.places, 1, rows, WIDE),
            lambda s, at_ref, t: (layer, 0, t[2, s] // across, 0, t[2, s] % across),
        ),
    ]
    used = [i for i, needed in enumerate((ins > 0, ins < steps)) if needed]
    given = [outs[i] for i in used if outs[i] is not None]
    source = pl.BlockSpec((layout.places // 2, rows, WIDE), lambda s, at_ref, t: (0, 0, t[0, s]))
    made = pl.pallas_call(
        functools.partial(place_kernel, ins, len(given)),
        grid_spec=pltpu.PrefetchScalarGridSpec(
            num_scalar_prefetch=2,
            grid=(steps,),
            in_specs=[source] * 2 + [pl.BlockSpec(memory_space=pl.ANY)] * len(given),
            out_specs=[both[i] for i in used],
            scratch_shapes=[pltpu.VMEM((layout.places, rows, WIDE), bf16)],
        ),
        out_shape=[jax.ShapeDtypeStruct(shapes[i], f32) for i in used],
        input_output_aliases={4 + i: i for i in range(len(given))},
        compiler_params=pltpu.CompilerParams(vmem_limit_bytes=VMEM),
        cost_estimate=NO_COST,
        name="place",
    )(at, table, even, odd, *given)
    outs = list(outs)
    for i, a in zip(used, made):
        outs[i] = a
    return outs


def lanes(row):
    return jnp.pad(row, (0, STATE - row.shape[0]))[None]


def local(
    tokens,
    in_weight,
    out_weight,
    conv_weight,
    conv_bias,
    a_log,
    dt_bias,
    skip_d,
    norm_gain,
    gated_gain,
    doc_start,
    cotangent,
):
    layers = in_weight.shape[0]
    length, width = tokens.shape[1:]
    taps, channels = conv_weight.shape[1:]
    owners = lax.axis_size("wa")
    heads = a_log.shape[1] * owners
    inner = heads * HEADDIM
    starts = (doc_start[0] - lax.axis_index("seq") * length)[:, None]

    own_small = [
        conv_weight.reshape(layers, taps * channels), conv_bias, a_log, dt_bias, skip_d,
        norm_gain, gated_gain,
    ]
    small = jnp.concatenate(own_small, axis=1)
    if owners & (owners - 1) == 0:
        small = jnp.stack([small] + [swap(small, "wa", q) for q in range(1, owners)])
        small = jnp.take(small, jnp.arange(owners) ^ lax.axis_index("wa"), axis=0).astype(f32)
    else:
        small = lax.all_gather(small, "wa", axis=0).astype(f32)
    sizes = [a.shape[1] for a in own_small]
    params = []
    for layer in range(layers):
        found, at = [], 0
        for i, size in enumerate(sizes):
            part = small[:, layer, at : at + size]
            at += size
            if i == 0:
                part = part.reshape(owners, taps, channels).swapaxes(0, 1)
                found.append(part.reshape(taps, owners * channels))
            else:
                found.append(part.reshape(owners * size))
        params.append(found)

    devices = lax.axis_size("seq")
    rows = in_weight.shape[1] // devices
    here = jnp.stack([lax.axis_index("wa"), lax.axis_index("seq")]).astype(jnp.int32)
    fold = inner // width
    dealing = devices == 2 * Y and owners > 1 and owners & (owners - 1) == 0 and rows % RIM == 0
    weights = []
    if dealing:
        layout = Layout(owners, devices, rows)
        at = here
        in_turned = in_weight.swapaxes(1, 2)
        column = over_wa(cut(at, layout, 0, in_turned, out_weight, False), layout)
        first_in = column[1:2]
        late_piece = cut(at, layout, 0, in_turned, out_weight, True, first_in)
        pieces = [
            cut(at, layout, layer, in_turned, out_weight, late, first_in)
            for layer in range(1, layers)
            for late in (False, True)
        ]
        early = straight(here, column, [late_piece, *pieces])
        late_column = over_wa(late_piece, layout)
        weights.append((early, 0, halved(here, late_column, early.arrays[1:4])))
        for layer in range(1, layers):
            early, late = [gathered(piece, layout) for piece in pieces[2 * layer - 2 : 2 * layer]]
            weights.append((early, 0, late))
    else:
        layout = Layout(owners, 1, in_weight.shape[1])
        at = jnp.zeros((2,), jnp.int32)
        for layer in range(layers):
            out = out_weight[layer].reshape(fold, layout.rows, width).swapaxes(0, 1)
            out = out.reshape(layout.rows, fold * width)
            gate, rest = in_weight[layer][:, :inner], in_weight[layer][:, inner:]
            found = [
                Slots(at, [lax.all_gather(part, "wa")[None]], [((0,), 0)])
                for part in (rest, jnp.concatenate([gate, out], axis=1))
            ]
            weights.append((found[0], 0, found[1]))
    resid = tokens[0].astype(f32)
    normed = (
        resid
        * lax.rsqrt(jnp.mean(resid * resid, axis=1, keepdims=True) + EPSILON)
        * params[0][5]
    ).astype(bf16)
    records = []
    for layer in range(layers):
        cw, cb, alog, dtb, skip, ngain, ggain = params[layer]
        rate = lanes(-jnp.exp(alog))
        skip_row = jnp.repeat(skip, HEADDIM)[None]
        early, rest_at, late = weights[layer]
        rim = passed_along(normed[length - RIM :], "seq", 1)
        nrm = jnp.concatenate([rim, normed], axis=0)
        cin, cv, dt, lam, sig, lamt, state, fresh, dec, nrmt = first(
            layout, nrm, early, rest_at, cw, cb[None], lanes(dtb), rate, starts, heads
        )
        if dealing and layer == 0:
            late = near_by(late, [dec])
            weights[0] = (early, 0, late)

        def beside(sent):
            return within(layout, nrm, late, 0, cv, dt, lam, lamt, starts, skip_row)

        s0, (gate, y) = carried_over(here, state, False, beside)
        gain_next = params[min(layer + 1, layers - 1)][5][None]
        y, gated, scale, resid_next, low, normed = join(
            layout, late, 1, y, cv, lam, starts, gate, s0, fresh, dec, ggain[None], resid, gain_next
        )
        records.append(
            (resid, cin, cv, dt, lam, sig, lamt, fresh, dec, nrmt, s0, gate, y, gated, scale,
             rate, skip_row)
        )
        resid = resid_next
    result = low[None]
    grad = cotangent[0].astype(f32)
    big = [None] * layers
    little = [None] * layers
    for layer in reversed(range(layers)):
        cw, cb, alog, dtb, skip, ngain, ggain = params[layer]
        early, rest_at, late = weights[layer]
        (resid, cin, cv, dt, lam, sig, lamt, fresh, dec, nrmt, s0, gate, y, gated, scale,
         rate, skip_row) = records[layer]
        top = layer == layers - 1
        if dealing and not top:
            third.pack()
        gy, ggate, gggain, gskip, later, total, *dwo = gate_back(
            [third.now[0], upper.now[0]] if dealing and not top else (), at, layout, late, 1, grad.astype(bf16), y, gate, gated, scale, ggain[None], cv, lam,
            starts, dec,
        )
        if dealing and top:
            upper, third = Collect(here, layout), Collect(here, layout)
            upper.add(1, *dwo)
        elif dealing:
            under = Collect(here, layout)
            moved = under.add(1, *dwo)

        def beside(sent):
            if dealing and not top:
                upper.whole(sent)
                third.halve(upper.now[0], moved)
            return within_back(
                third.now[:1] if dealing and not top else (), at, layout, late, 0, gy, cv, dt, lam, lamt, starts, s0, fresh, dec, ggate, nrmt
            )

        gend, (gxd, glam, gbc, gnrm_gate, *dw_gate) = carried_over(here, total, True, beside)
        if dealing and top:
            upper.add(0, *dw_gate)
            upper.pack(gend)
        elif dealing:
            third.apart(gend)
            upper.gathered()
            under.add(0, *dw_gate, [third.now[0]])
            under.pack()
        gnrm, gcw, gcb, gsmall, *dw_rest = last(
            () if not dealing else upper.now[:1] if top else [third.now[0], under.now[0]], at, layout, early,
            rest_at, gxd, cv, cin, gy, dt, lam, sig, starts, gend, later, s0,
            fresh, dec, nrmt, glam, gbc, gnrm_gate, skip_row, rate, cw,
        )
        edge = gnrm[:RIM]
        if dealing and top:
            upper.halve(gsmall)
            third.add(0, *dw_rest, [upper.now[0]])
            edge = tie(edge, [upper.now[0]])
            upper.apart(third.parts[0][1])
        elif dealing:
            under.halve(gsmall)
            third.whole(under.now[0])
            third.gathered()
            tail = Collect(here, layout)
            tail.add(0, *dw_rest, [third.now[0]] if False else [under.now[0]])
            edge = tie(edge, [under.now[0]])
            tail.pack()
            under.apart(tail.now[0])
            tail.halve(under.now[0])
        rim = passed_along(edge, "seq", -1)
        gnormed = gnrm[RIM:]
        gnormed = jnp.concatenate([gnormed[: length - RIM], gnormed[length - RIM :] + rim], axis=0)
        grad_resid, gngain = rms_back(resid, ngain, gnormed)
        grad = grad + grad_resid
        big[layer] = (dw_gate, dwo, dw_rest)
        little[layer] = (
            gcw, gcb[0], gsmall[1, :heads], gsmall[0, :heads],
            jnp.sum(gskip.reshape(heads, HEADDIM), axis=1), gngain, gggain[0],
        )

    rows = []
    for layer in range(layers):
        gcw = little[layer][0].reshape(taps, owners, channels).swapaxes(0, 1)
        parts = [gcw.reshape(owners, taps * channels)]
        parts += [a.reshape(owners, -1) for a in little[layer][1:]]
        rows.append(jnp.concatenate(parts, axis=1))
    packed = jnp.concatenate(rows, axis=1)
    if dealing:
        size = packed.shape[1]
        packed = jnp.pad(packed, ((0, 0), (0, -size % (8 * STATE))))
        packed = jnp.take(packed, jnp.arange(owners) ^ here[0], axis=0).reshape(owners, -1, STATE)
        for by in (1, X, Y):
            packed = packed + swap(packed, "seq", by)
        mine = sum((swap(packed[q], "wa", q) for q in range(1, owners)), packed[0])
        mine = mine.reshape(-1)[:size].reshape(layers, -1)
    else:
        mine = lax.dynamic_index_in_dim(
            lax.psum(packed, ("wa", "seq")), lax.axis_index("wa"), 0, keepdims=False
        ).reshape(layers, -1)
    in_width, rest = in_weight.shape[2], in_weight.shape[2] - inner
    if layout.places == 1:

        def owned(part):
            part = part.reshape(owners, -1, part.shape[-1])
            part = lax.psum_scatter(part, "wa", scatter_dimension=0)
            return lax.psum(part, "seq").astype(f32)

        in_grad = jnp.stack(
            [
                jnp.concatenate([owned(big[layer][0][0]), owned(big[layer][2][0])], axis=1)
                for layer in range(layers)
            ]
        )
        out_grad = jnp.stack([owned(big[layer][1][0]) for layer in range(layers)])
    else:
        assert layers == 2
        assert layers == 2
        both = [(layers, in_width, in_weight.shape[1]), (layers, layout.places, fold, layout.rows, width)]
        tiles = inner // WIDE
        more = -(-rest // WIDE)
        made = place(
            at, 1, upper.now, ((True, 0, tiles, 0), (False, tiles, tiles, 0)), [None, None], both,
            layout, True,
        )
        under.whole(tail.now[0])
        tail.apart(under.now[0])
        under.spread(tail.now[0])
        made = place(at, 1, third.now, ((True, 0, more, tiles),), made, both, layout, True)
        tail.whole(made[0])
        tail.spread()
        made = place(
            at, 0, under.now, ((True, 0, tiles, 0), (False, tiles, tiles, 0)), made, both, layout
        )
        made = place(at, 0, tail.now, ((True, 0, more, tiles),), made, both, layout)
        in_grad = made[0].swapaxes(1, 2)
        out_grad = made[1].reshape(out_weight.shape)
    found, at = [], 0
    for i, size in enumerate(sizes):
        part = mine[:, at : at + size]
        at += size
        found.append(part.reshape(layers, taps, channels) if i == 0 else part)
    return (result, grad[None], in_grad, out_grad, *found)


def solution(mesh):
    in_specs = (
        P("wa", "seq", None),
        P(None, "wa", None),
        P(None, "wa", None),
        P(None, None, "wa"),
        P(None, "wa"),
        P(None, "wa"),
        P(None, "wa"),
        P(None, "wa"),
        P(None, "wa"),
        P(None, "wa"),
        P("wa", "seq"),
        P("wa", "seq", None),
    )
    out_specs = (
        P("wa", "seq", None),
        P("wa", "seq", None),
        P(None, "wa", None),
        P(None, "wa", None),
        P(None, None, "wa"),
        P(None, "wa"),
        P(None, "wa"),
        P(None, "wa"),
        P(None, "wa"),
        P(None, "wa"),
        P(None, "wa"),
    )
    return jax.shard_map(local, mesh=mesh, in_specs=in_specs, out_specs=out_specs, check_vma=False)
```

```python
import functools

import jax
import jax.numpy as jnp
from jax import lax
from jax.experimental import pallas as pl
from jax.experimental.pallas import tpu as pltpu
from jax.sharding import PartitionSpec as P

HEADDIM = 64
STATE = 128
BLOCK = 256
TILE = 256
PER = TILE // HEADDIM
RIM = 16
EPSILON = 1e-05
PRECISE = lax.Precision.HIGHEST
f32 = jnp.float32
bf16 = jnp.bfloat16
FAR = -1e30
VMEM = 60 * 2**20
NO_COST = pl.CostEstimate(flops=0, bytes_accessed=0, transcendentals=0)


def dot(a, b, ca=1, cb=0, precision=None):
    return lax.dot_general(
        a, b, (((ca,), (cb,)), ((), ())), precision=precision, preferred_element_type=f32
    )


def iota(shape, axis):
    return lax.broadcasted_iota(jnp.int32, shape, axis)


def logistic(v):
    return 0.5 + 0.5 * jnp.tanh(0.5 * v)


def silu(v):
    return v * logistic(v)


def dsilu(v):
    s = logistic(v)
    return s * (1.0 + v * (1.0 - s))


def split(q):
    high = q.astype(bf16)
    return jnp.concatenate([high, (q - high.astype(f32)).astype(bf16)], axis=1)


def spread(pair, group):
    rows = iota((2 * STATE, TILE), 0) % STATE
    cols = PER * group + iota((2 * STATE, TILE), 1) // HEADDIM
    return dot(pair, (rows == cols).astype(f32).astype(bf16))


def chooser(group):
    return iota((TILE, STATE), 1) == PER * group + iota((TILE, STATE), 0) // HEADDIM


def gather_heads(z, group):
    pick = chooser(group).astype(f32).astype(bf16)
    high = z.astype(bf16)
    low = (z - high.astype(f32)).astype(bf16)
    return dot(high, pick) + dot(low, pick)


def head_rows(row, group):
    return jnp.sum(jnp.where(chooser(group), row, 0.0), axis=1, keepdims=True)


def lower(n):
    return iota((n, n), 0) >= iota((n, n), 1)


def decay_rows(decay):
    high = decay.astype(bf16).astype(f32)
    zeros = jnp.zeros((RIM - 2, STATE), f32)
    return jnp.concatenate([high, decay - high, zeros], axis=0).astype(bf16)


def block_of(b):
    return slice(b * BLOCK, (b + 1) * BLOCK)


def end_weights(starts, lam, b):
    s = block_of(b)
    last = (b + 1) * BLOCK - 1
    place = b * BLOCK + iota((BLOCK, 1), 0)
    keep = place >= starts[last : last + 1]
    return jnp.where(keep, jnp.exp(lam[last : last + 1] - lam[s]), 0.0)


def reach_weights(starts, lam, b):
    s = block_of(b)
    return jnp.where(starts[s] < b * BLOCK, jnp.exp(lam[s]), 0.0)


def fill_mask(mask_ref, starts, blocks):
    for b in range(blocks):
        t = b * BLOCK + iota((BLOCK, BLOCK), 0)
        s = b * BLOCK + iota((BLOCK, BLOCK), 1)
        mask_ref[b] = jnp.where((s <= t) & (s >= starts[block_of(b)]), 0.0, FAR)


def assemble(w_refs, w_sc, at_ref, plan):
    for w_ref, (places, first_owner) in zip(w_refs, plan):
        for i, r in enumerate(places):
            for q in range(w_ref.shape[1]):
                w_sc[at_ref[0] ^ (first_owner + q), at_ref[1] ^ r] = w_ref[i, q]
    return w_sc[...].reshape(-1, w_sc.shape[-1])


def deal(value, keep_ref, send_ref, d_sc, at_ref):
    owners, places = d_sc.shape[:2]
    d_sc[...] = value.astype(bf16).reshape(d_sc.shape)
    for r in range(places):
        target = send_ref if r % 2 else keep_ref
        for q in range(owners):
            target[r // 2, q] = d_sc[at_ref[2] ^ q, at_ref[3] ^ r]


class Layout:
    def __init__(self, owners, places, rows):
        self.owners, self.places, self.rows = owners, places, rows

    def scratch(self, width):
        return pltpu.VMEM((self.owners, self.places, self.rows, width), bf16)

    def dealt(self, col):
        block = (max(self.places // 2, 1), self.owners, self.rows, TILE)
        return [pl.BlockSpec(block, lambda *s: (0, 0, 0, col(*s)))] * (1 if self.places == 1 else 2)

    def dealt_shape(self, rows, width):
        shape = (max(self.places // 2, 1), self.owners, rows, width)
        return [jax.ShapeDtypeStruct(shape, bf16)] * (1 if self.places == 1 else 2)


class Slots:
    def __init__(self, near, arrays, plan):
        self.near, self.arrays, self.plan = near, tuple(arrays), tuple(plan)

    def tiles(self, col):
        return [
            pl.BlockSpec((*a.shape[:3], TILE), lambda *s: (0, 0, 0, col(*s))) for a in self.arrays
        ]

    def whole(self, width, at):
        return [pl.BlockSpec((*a.shape[:3], width), lambda *s: (0, 0, 0, at)) for a in self.arrays]


SMEM = pl.BlockSpec(memory_space=pltpu.SMEM)


def first_kernel(
    plan, at_ref, rim_ref, normed_ref, *refs
):
    w_refs, rest = refs[: len(plan)], refs[len(plan) :]
    first_body(plan, at_ref, rim_ref, normed_ref, w_refs, *rest)


def first_body(
    plan, at_ref, rim_ref, normed_ref, w_refs, cw_ref, cb_ref, dtb_ref, rate_ref, starts_ref,
    cin_ref, cv_ref, dt_ref, lam_ref, sig_ref, lamt_ref, state_ref, fresh_ref, dec_ref, nrmt_ref,
    b_sc, e_sc, w_sc, nrm_ref,
):
    step = pl.program_id(0)
    length = starts_ref.shape[0]
    blocks = length // BLOCK
    heads = lamt_ref.shape[0] * PER
    starts = starts_ref[...]
    w = assemble(w_refs, w_sc, at_ref, plan)

    @pl.when(step == 0)
    def _():
        nrm_ref[:length] = normed_ref[...]
        nrm_ref[length:] = rim_ref[...]

    def conv():
        pe = dot(nrm_ref[...], w)
        cin_ref[...] = pe.astype(bf16)
        place = iota((length, 1), 0)
        taps = cw_ref.shape[0]
        acc = cb_ref[...] + cw_ref[taps - 1 : taps] * pe[:length]
        for k in range(taps - 1):
            back = taps - 1 - k
            keep = place - back >= starts
            acc = acc + jnp.where(keep, cw_ref[k : k + 1] * pltpu.roll(pe, back, 0)[:length], 0.0)
        cv = acc.astype(bf16)
        cv_ref[...] = cv
        return silu(cv.astype(f32))

    @pl.when(step == 0)
    def _():
        act = conv()
        b_sc[...] = act[:, :STATE].astype(bf16)
        nrmt_ref[...] = nrm_ref[...].T

    @pl.when(step == 1)
    def _():
        z = dot(nrm_ref[:length], w[:, :STATE]) + dtb_ref[...]
        live = iota(z.shape, 1) < heads
        dt = jnp.where(live, jnp.maximum(z, 0.0) + jnp.log1p(jnp.exp(-jnp.abs(z))), 0.0)
        dt_ref[...] = dt
        sig_ref[...] = jnp.where(live, 1.0 / (1.0 + jnp.exp(-z)), 0.0)
        change = dt * rate_ref[...]
        tri = lower(BLOCK).astype(f32)
        lam = jnp.concatenate(
            [dot(tri, change[block_of(b)], precision=PRECISE) for b in range(blocks)], axis=0
        )
        lam_ref[...] = lam
        across = lam.T
        for g in range(lamt_ref.shape[0]):
            lamt_ref[g] = across[PER * g : PER * (g + 1)]
        total = None
        rows = []
        for b in range(blocks):
            e_sc[block_of(b)] = split(end_weights(starts, lam, b) * dt[block_of(b)])
            last = (b + 1) * BLOCK - 1
            decay = jnp.where(
                starts[last : last + 1] < b * BLOCK, jnp.exp(lam[last : last + 1]), 0.0
            )
            decay = jnp.where(iota(decay.shape, 1) < heads, decay, 0.0)
            rows.append(decay)
            total = decay if total is None else total * decay
        rows.append(total)
        rows.append(jnp.zeros((8 - len(rows), STATE), f32))
        dec_ref[...] = jnp.concatenate(rows, axis=0)
        state_ref[:RIM] = decay_rows(total)

    @pl.when(step >= 2)
    def _():
        group = step - 2
        xe = (conv() * spread(e_sc[...], group)).astype(bf16)
        total = None
        for b in range(blocks):
            fresh = dot(xe[block_of(b)], b_sc[block_of(b)], 0, 0)
            if b + 1 < blocks:
                fresh_ref[b] = fresh
            if total is None:
                total = fresh
            else:
                total = head_rows(dec_ref[b : b + 1], group) * total + fresh
        state_ref[...] = total.astype(state_ref.dtype)


def first(layout, rim, normed, slots, rest_at, cw, cb, dtb, rate, starts, heads):
    d = normed.shape[1]
    length = starts.shape[0]
    ext = length + RIM
    blocks = length // BLOCK
    inner = heads * HEADDIM
    groups = inner // TILE
    col = lambda s: jnp.where(s == 0, groups, jnp.maximum(s - 2, 0))
    wcol = lambda s: rest_at + jnp.where(s < 2, groups + s, s - 2)
    tile = lambda s: jnp.maximum(s - 2, 0)
    full = lambda *shape: pl.BlockSpec(shape, lambda s: (0,) * len(shape))
    state = lambda s: jnp.where(s < 2, groups, s - 2)
    return pl.pallas_call(
        functools.partial(first_kernel, slots.plan),
        grid=(groups + 2,),
        in_specs=[
            SMEM,
            full(RIM, d),
            full(length, d),
            *slots.tiles(wcol),
            pl.BlockSpec((cw.shape[0], TILE), lambda s: (0, col(s))),
            pl.BlockSpec((1, TILE), lambda s: (0, col(s))),
            full(1, STATE),
            full(1, STATE),
            full(length, 1),
        ],
        out_specs=[
            pl.BlockSpec((ext, TILE), lambda s: (0, col(s))),
            pl.BlockSpec((length, TILE), lambda s: (0, col(s))),
            full(length, STATE),
            full(length, STATE),
            full(length, STATE),
            full(groups, PER, length),
            pl.BlockSpec((TILE, STATE), lambda s: (state(s), 0)),
            pl.BlockSpec((blocks - 1, TILE, STATE), lambda s: (0, tile(s), 0)),
            full(8, STATE),
            full(d, ext),
        ],
        out_shape=[
            jax.ShapeDtypeStruct((ext, inner + 2 * STATE), bf16),
            jax.ShapeDtypeStruct((length, inner + 2 * STATE), bf16),
            jax.ShapeDtypeStruct((length, STATE), f32),
            jax.ShapeDtypeStruct((length, STATE), f32),
            jax.ShapeDtypeStruct((length, STATE), f32),
            jax.ShapeDtypeStruct((groups, PER, length), f32),
            jax.ShapeDtypeStruct((inner + RIM, STATE), bf16),
            jax.ShapeDtypeStruct((blocks - 1, inner, STATE), f32),
            jax.ShapeDtypeStruct((8, STATE), f32),
            jax.ShapeDtypeStruct((d, ext), bf16),
        ],
        scratch_shapes=[
            pltpu.VMEM((length, STATE), bf16),
            pltpu.VMEM((length, 2 * STATE), bf16),
            layout.scratch(TILE),
            pltpu.VMEM((ext, d), bf16),
        ],
        compiler_params=pltpu.CompilerParams(vmem_limit_bytes=VMEM),
        cost_estimate=NO_COST,
        name="project",
    )(slots.near, rim, normed, *slots.arrays, cw, cb, dtb, rate, starts)


def pair_of(width):
    return iota((1, width), 1) < HEADDIM


def within_kernel(
    x_ref, bc_ref, dt_ref, lam_ref, lamt_ref, starts_ref, skip_ref,
    y_ref,
    cross_sc, mask_sc, dt_sc,
):
    group = pl.program_id(0)
    length = starts_ref.shape[0]
    blocks = length // BLOCK

    @pl.when(group == 0)
    def _():
        act = silu(bc_ref[...].astype(f32)).astype(bf16)
        for b in range(blocks):
            s = block_of(b)
            cross_sc[b] = dot(act[s, STATE:], act[s, :STATE], 1, 1)
        fill_mask(mask_sc, starts_ref[...], blocks)
        dt_sc[...] = split(dt_ref[...])

    x = silu(x_ref[...].astype(f32))
    xd = (x * spread(dt_sc[...], group)).astype(bf16)
    lam = pltpu.roll(lam_ref[...], lax.rem(STATE - PER * group, STATE), 1)
    lamt = lamt_ref[group]
    left = pair_of(2 * HEADDIM)
    for b in range(blocks):
        s = block_of(b)
        parts = []
        for p in range(PER // 2):
            c = slice(2 * HEADDIM * p, 2 * HEADDIM * (p + 1))
            two = []
            for h in (2 * p, 2 * p + 1):
                gap = (lam[s, h : h + 1] - lamt[h : h + 1, s]) + mask_sc[b]
                two.append(dot((jnp.exp(gap) * cross_sc[b]).astype(bf16), xd[s, c]))
            parts.append(jnp.where(left, two[0], two[1]))
        y = jnp.concatenate(parts, axis=1) + skip_ref[...] * x[s]
        y_ref[s] = y.astype(bf16)


def within(cv, dt, lam, lamt, starts, skip):
    length = starts.shape[0]
    blocks = length // BLOCK
    groups = lamt.shape[0]
    inner = groups * TILE
    full = lambda *shape: pl.BlockSpec(shape, lambda s: (0,) * len(shape))
    tile = pl.BlockSpec((length, TILE), lambda s: (0, s))
    return pl.pallas_call(
        within_kernel,
        grid=(groups,),
        in_specs=[
            tile,
            pl.BlockSpec((length, TILE), lambda s: (0, groups)),
            full(length, STATE),
            full(length, STATE),
            full(groups, PER, length),
            full(length, 1),
            pl.BlockSpec((1, TILE), lambda s: (0, s)),
        ],
        out_specs=tile,
        out_shape=jax.ShapeDtypeStruct((length, inner), bf16),
        scratch_shapes=[
            pltpu.VMEM((blocks, BLOCK, BLOCK), f32),
            pltpu.VMEM((blocks, BLOCK, BLOCK), f32),
            pltpu.VMEM((length, 2 * STATE), bf16),
        ],
        compiler_params=pltpu.CompilerParams(vmem_limit_bytes=VMEM),
        cost_estimate=NO_COST,
        name="within",
    )(cv, cv, dt, lam, lamt, starts, skip)


def states_of(s0, fresh_ref, dec_ref, group, blocks):
    found = [s0]
    for b in range(blocks - 1):
        found.append(head_rows(dec_ref[b : b + 1], group) * found[-1] + fresh_ref[b])
    return found


def unfold(wo_refs, wo_sc, at_ref, plan):
    rows, width = wo_sc.shape[-2:]
    short = wo_refs[0].shape[2]
    for wo_ref, (places, first_owner) in zip(wo_refs, plan):
        for i, r in enumerate(places):
            for q in range(wo_ref.shape[1]):
                for f in range(rows // short):
                    part = wo_ref[i, q, :, f * width : (f + 1) * width]
                    owner = at_ref[0] ^ (first_owner + q)
                    wo_sc[owner, at_ref[1] ^ r, f * short : (f + 1) * short] = part


def pieces_of(shape, group):
    share = shape[1] * shape[2]
    parts = share // TILE
    if parts == 1:
        return group, slice(None)
    many = TILE // shape[2]
    return group // parts, pl.ds(many * (group % parts), many)


def join_kernel(
    plan, at_ref, *refs
):
    many = len(plan)
    join_body(plan, at_ref, refs[:many], refs[many : 2 * many], *refs[2 * many :])


def join_body(
    plan, at_ref, w_refs, wo_refs, nrm_ref, y_ref, bc_ref, lam_ref, starts_ref, s0_ref, fresh_ref, dec_ref, gain_ref,
    resid_ref, gain_next_ref,
    gate_ref, y_out_ref, gated_ref, scale_ref, next_ref, low_ref, normed_ref,
    u_sc, c_sc, v_sc, sq_sc, wo_sc, w_sc,
):
    group = pl.program_id(0)
    length = starts_ref.shape[0]
    blocks = length // BLOCK
    groups = v_sc.shape[0]
    inner = groups * TILE

    @pl.when(group == 0)
    def _():
        c_sc[...] = silu(bc_ref[:, STATE:].astype(f32)).astype(bf16)
        for b in range(blocks):
            u_sc[block_of(b)] = split(reach_weights(starts_ref[...], lam_ref[...], b))
        sq_sc[...] = jnp.zeros_like(sq_sc)

    u = spread(u_sc[...], group)
    before = states_of(s0_ref[...].astype(f32), fresh_ref, dec_ref, group, blocks)
    carried = jnp.concatenate(
        [dot(c_sc[block_of(b)], before[b].astype(bf16), 1, 1) for b in range(blocks)], axis=0
    )
    y = (y_ref[...].astype(f32) + u * carried).astype(bf16)
    y_out_ref[...] = y
    gate = dot(nrm_ref[...], assemble(w_refs, w_sc, at_ref, plan)).astype(bf16)
    gate_ref[...] = gate
    v = y.astype(f32) * silu(gate.astype(f32))
    v_sc[group] = v
    sq = v * v
    sq_sc[...] += sq[:, :STATE] + sq[:, STATE:]

    @pl.when(group == groups - 1)
    def _():
        mean = jnp.sum(sq_sc[...], axis=1, keepdims=True) / inner
        scale = lax.rsqrt(mean + EPSILON)
        scale_ref[...] = scale
        acc = resid_ref[...]
        unfold(wo_refs, wo_sc, at_ref, plan)
        for g in range(groups):
            c = slice(g * TILE, (g + 1) * TILE)
            low = (v_sc[g] * scale * gain_ref[:, c]).astype(bf16)
            gated_ref[:, c] = low
            owner, piece = pieces_of(wo_sc.shape, g)
            acc = acc + dot(low, wo_sc[owner, piece].reshape(TILE, -1))
        next_ref[...] = acc
        low_ref[...] = acc.astype(bf16)
        norm = lax.rsqrt(jnp.mean(acc * acc, axis=1, keepdims=True) + EPSILON)
        normed_ref[...] = (acc * norm * gain_next_ref[...]).astype(bf16)


def join(layout, slots, gate_at, out_at, nrm, y, cv, lam, starts, s0, fresh, dec, gain, resid, gain_next):
    length, inner = y.shape
    d = resid.shape[1]
    fold = inner // d
    blocks = length // BLOCK
    groups = inner // TILE
    full = lambda *shape: pl.BlockSpec(shape, lambda s: (0,) * len(shape))
    tile = pl.BlockSpec((length, TILE), lambda s: (0, s))
    return pl.pallas_call(
        functools.partial(join_kernel, slots.plan),
        grid=(groups,),
        in_specs=[
            SMEM,
            *slots.tiles(lambda s: gate_at + s),
            *slots.whole(inner, out_at),
            full(length, d),
            tile,
            pl.BlockSpec((length, TILE), lambda s: (0, groups)),
            full(length, STATE),
            full(length, 1),
            pl.BlockSpec((TILE, STATE), lambda s: (s, 0)),
            pl.BlockSpec((blocks - 1, TILE, STATE), lambda s: (0, s, 0)),
            full(8, STATE),
            full(1, inner),
            full(length, d),
            full(1, d),
        ],
        out_specs=[
            tile,
            tile,
            full(length, inner),
            full(length, 1),
            full(length, d),
            full(length, d),
            full(length, d),
        ],
        out_shape=[
            jax.ShapeDtypeStruct((length, inner), bf16),
            jax.ShapeDtypeStruct((length, inner), bf16),
            jax.ShapeDtypeStruct((length, inner), bf16),
            jax.ShapeDtypeStruct((length, 1), f32),
            jax.ShapeDtypeStruct((length, d), f32),
            jax.ShapeDtypeStruct((length, d), bf16),
            jax.ShapeDtypeStruct((length, d), bf16),
        ],
        scratch_shapes=[
            pltpu.VMEM((length, 2 * STATE), bf16),
            pltpu.VMEM((length, STATE), bf16),
            pltpu.VMEM((groups, length, TILE), f32),
            pltpu.VMEM((length, STATE), f32),
            pltpu.VMEM((layout.owners, layout.places, fold * layout.rows, d), bf16),
            layout.scratch(TILE),
        ],
        compiler_params=pltpu.CompilerParams(vmem_limit_bytes=VMEM),
        cost_estimate=NO_COST,
        name="join",
    )(
        slots.near, *slots.arrays, *slots.arrays, nrm, y, cv, lam, starts, s0, fresh, dec, gain, resid,
        gain_next,
    )


def gate_back_kernel(
    plan, skip, at_ref, *refs
):
    refs = refs[skip:]
    wo_refs, rest = refs[: len(plan)], refs[len(plan) :]
    gate_back_body(plan, at_ref, wo_refs, *rest)


def gate_back_body(
    plan, at_ref, wo_refs, grad_ref, y_ref, gate_ref, gated_ref, scale_ref, gain_ref, x_ref, bc_ref, lam_ref,
    starts_ref, dec_ref,
    gy_ref, ggate_ref, ggain_ref, gskip_ref, later_ref, total_ref, *more
):
    gg_sc, u_sc, c_sc, dot_sc, wo_sc, dwo_sc = more[-6:]
    keep_ref, send_ref = more[0], more[-7]
    phase, group = pl.program_id(0), pl.program_id(1)
    length = starts_ref.shape[0]
    blocks = length // BLOCK
    groups = gg_sc.shape[0]
    inner = groups * TILE

    @pl.when((phase == 0) & (group == 0))
    def _():
        c_sc[...] = silu(bc_ref[:, STATE:].astype(f32)).astype(bf16)
        for b in range(blocks):
            u_sc[block_of(b)] = split(reach_weights(starts_ref[...], lam_ref[...], b))
        dot_sc[...] = jnp.zeros_like(dot_sc)
        unfold(wo_refs, wo_sc, at_ref, plan)

    y = y_ref[...].astype(f32)
    gate = gate_ref[...].astype(f32)
    sig = logistic(gate)
    act = gate * sig
    v = y * act
    scale = scale_ref[...]

    @pl.when(phase == 0)
    def _():
        owners, places, rows, width = wo_sc.shape
        owner, piece = pieces_of(wo_sc.shape, group)
        gg = dot(grad_ref[...], wo_sc[owner, piece].reshape(TILE, width), 1, 1)
        gv = gg * v
        ggain_ref[...] = jnp.sum(gv * scale, axis=0, keepdims=True)
        total_ref[:RIM] = decay_rows(dec_ref[blocks : blocks + 1])
        gv = gv * gain_ref[...]
        dot_sc[...] += gv[:, :STATE] + gv[:, STATE:]
        gg_sc[group] = gg * gain_ref[...]
        dwo = dot(gated_ref[...], grad_ref[...], 0, 0).astype(bf16)
        dwo_sc[owner, piece] = dwo.reshape(-1, rows, width)

        @pl.when(group == groups - 1)
        def _():
            for r in range(places):
                target = send_ref if r % 2 else keep_ref
                for q in range(owners):
                    target[r // 2, q] = dwo_sc[at_ref[2] ^ q, at_ref[3] ^ r]

    @pl.when(phase == 1)
    def _():
        @pl.when(group == 0)
        def _():
            total = jnp.sum(dot_sc[...], axis=1, keepdims=True)
            dot_sc[...] = jnp.broadcast_to(
                total * scale * scale * scale * (1.0 / inner), dot_sc.shape
            )

        gv = scale * gg_sc[group] - v * dot_sc[:, :1]
        gy = gv * act
        ggate_ref[...] = (gv * y * (sig + act * (1.0 - sig))).astype(bf16)
        low = gy.astype(bf16)
        gy_ref[...] = low
        x = silu(x_ref[...].astype(f32))
        skip = jnp.sum(low.astype(f32) * x, axis=0, keepdims=True)
        skip = gather_heads(jnp.broadcast_to(skip, (8, TILE)), group)[:1]

        @pl.when(group == 0)
        def _():
            gskip_ref[...] = jnp.zeros_like(gskip_ref)

        gskip_ref[...] += skip
        ug = (gy * spread(u_sc[...], group)).astype(bf16)
        total = None
        for b in reversed(range(blocks)):
            direct = dot(ug[block_of(b)], c_sc[block_of(b)], 0, 0)
            if total is None:
                total = direct
            else:
                total = head_rows(dec_ref[b : b + 1], group) * total + direct
            if b > 0:
                later_ref[b - 1] = direct
        total_ref[...] = total.astype(total_ref.dtype)


def gate_back(after, at, layout, slots, out_at, grad_low, y, gate, gated, scale, gain, cv, lam, starts, dec):
    length, inner = y.shape
    d = grad_low.shape[1]
    rows = inner // d * layout.rows
    blocks = length // BLOCK
    groups = inner // TILE
    full = lambda *shape: pl.BlockSpec(shape, lambda p, s: (0,) * len(shape))
    early = lambda p, s: jnp.where(p == 0, s, groups - 1)
    late = lambda p, s: s * p
    tile = pl.BlockSpec((length, TILE), lambda p, s: (0, s))
    late_tile = pl.BlockSpec((length, TILE), lambda p, s: (0, late(p, s)))
    return pl.pallas_call(
        functools.partial(gate_back_kernel, slots.plan, len(after)),
        grid=(2, groups),
        in_specs=[
            SMEM,
            *[pl.BlockSpec(memory_space=pl.ANY)] * len(after),
            *slots.whole(inner, out_at),
            full(length, d),
            tile,
            tile,
            pl.BlockSpec((length, TILE), lambda p, s: (0, early(p, s))),
            full(length, 1),
            pl.BlockSpec((1, TILE), lambda p, s: (0, s)),
            late_tile,
            pl.BlockSpec((length, TILE), lambda p, s: (0, groups)),
            full(length, STATE),
            full(length, 1),
            full(8, STATE),
        ],
        out_specs=[
            late_tile,
            late_tile,
            pl.BlockSpec((1, TILE), lambda p, s: (0, early(p, s))),
            full(1, STATE),
            pl.BlockSpec((blocks - 1, TILE, STATE), lambda p, s: (0, late(p, s), 0)),
            pl.BlockSpec((TILE, STATE), lambda p, s: (jnp.where(p == 0, groups, s), 0)),
            *[full(*a.shape) for a in layout.dealt_shape(rows, d)],
        ],
        out_shape=[
            jax.ShapeDtypeStruct((length, inner), bf16),
            jax.ShapeDtypeStruct((length, inner), bf16),
            jax.ShapeDtypeStruct((1, inner), f32),
            jax.ShapeDtypeStruct((1, STATE), f32),
            jax.ShapeDtypeStruct((blocks - 1, inner, STATE), f32),
            jax.ShapeDtypeStruct((inner + RIM, STATE), bf16),
            *layout.dealt_shape(rows, d),
        ],
        scratch_shapes=[
            pltpu.VMEM((groups, length, TILE), f32),
            pltpu.VMEM((length, 2 * STATE), bf16),
            pltpu.VMEM((length, STATE), bf16),
            pltpu.VMEM((length, STATE), f32),
            pltpu.VMEM((layout.owners, layout.places, rows, d), bf16),
            pltpu.VMEM((layout.owners, layout.places, rows, d), bf16),
        ],
        compiler_params=pltpu.CompilerParams(vmem_limit_bytes=VMEM),
        cost_estimate=NO_COST,
        name="gate_back",
    )(jnp.concatenate([slots.near, at]), *after, *slots.arrays, grad_low, y, gate, gated, scale, gain, cv, cv, lam, starts, dec)


def within_back_kernel(
    plan, skip, at_ref, *refs
):
    refs = refs[skip:]
    w_refs, rest = refs[: len(plan)], refs[len(plan) :]
    within_back_body(plan, at_ref, w_refs, *rest)


def within_back_body(
    plan, at_ref, w_refs, gy_ref, x_ref, bc_ref, dt_ref, lam_ref, lamt_ref, starts_ref, s0_ref, fresh_ref, dec_ref,
    ggate_ref, nrmt_ref,
    gxd_ref, glam_ref, gbc_ref, gnrm_ref, *more
):
    cross_sc, gcross_sc, mask_sc, dt_sc, u_sc, act_sc, w_sc, d_sc = more[-8:]
    keep_ref, send_ref = more[0], more[-9]
    group = pl.program_id(0)
    length = starts_ref.shape[0]
    blocks = length // BLOCK
    groups = lamt_ref.shape[0]

    @pl.when(group == 0)
    def _():
        act = silu(bc_ref[...].astype(f32)).astype(bf16)
        act_sc[...] = act
        for b in range(blocks):
            s = block_of(b)
            cross_sc[b] = dot(act[s, STATE:], act[s, :STATE], 1, 1)
            u_sc[s] = split(reach_weights(starts_ref[...], lam_ref[...], b))
        fill_mask(mask_sc, starts_ref[...], blocks)
        dt_sc[...] = split(dt_ref[...])
        gcross_sc[...] = jnp.zeros_like(gcross_sc)
        glam_ref[...] = jnp.zeros_like(glam_ref)
        gbc_ref[...] = jnp.zeros_like(gbc_ref)
        gnrm_ref[...] = jnp.zeros_like(gnrm_ref)

    ggate = ggate_ref[...]
    gnrm_ref[...] += dot(ggate, assemble(w_refs, w_sc, at_ref, plan), 1, 1)
    deal(dot(nrmt_ref[:, :length], ggate), keep_ref, send_ref, d_sc, at_ref)

    x = silu(x_ref[...].astype(f32))
    xd = (x * spread(dt_sc[...], group)).astype(bf16)
    gy = gy_ref[...]
    u = spread(u_sc[...], group)
    before = states_of(s0_ref[...].astype(f32), fresh_ref, dec_ref, group, blocks)
    lam = pltpu.roll(lam_ref[...], lax.rem(STATE - PER * group, STATE), 1)
    lamt = lamt_ref[group]
    left = pair_of(2 * HEADDIM)
    for b in range(blocks):
        s = block_of(b)
        gcross = gcross_sc[b]
        ys, gxds = [], []
        for p in range(PER // 2):
            c = slice(2 * HEADDIM * p, 2 * HEADDIM * (p + 1))
            y2, g2 = [], []
            for h in (2 * p, 2 * p + 1):
                decay = jnp.exp((lam[s, h : h + 1] - lamt[h : h + 1, s]) + mask_sc[b])
                weight = (decay * cross_sc[b]).astype(bf16)
                y2.append(dot(weight, xd[s, c]))
                g2.append(dot(weight, gy[s, c], 0, 0))
                own = left if h % 2 == 0 else ~left
                mine = jnp.where(own, gy[s, c], jnp.zeros((), bf16))
                gcross = gcross + dot(mine, xd[s, c], 1, 1) * decay
            ys.append(jnp.where(left, y2[0], y2[1]))
            gxds.append(jnp.where(left, g2[0], g2[1]))
        gcross_sc[b] = gcross
        state = before[b].astype(bf16)
        y = jnp.concatenate(ys, axis=1) + u[s] * dot(act_sc[s, STATE:], state, 1, 1)
        gxd = jnp.concatenate(gxds, axis=1)
        gxd_ref[s] = gxd
        gyf = gy[s].astype(f32)
        glam_ref[s] += gather_heads(gyf * y - xd[s].astype(f32) * gxd, group)
        gbc_ref[s, STATE:] += dot((u[s] * gyf).astype(bf16), state)

    @pl.when(group == groups - 1)
    def _():
        for b in range(blocks):
            s = block_of(b)
            low = gcross_sc[b].astype(bf16)
            gbc_ref[s, :STATE] += dot(low, act_sc[s, STATE:], 0, 0)
            gbc_ref[s, STATE:] += dot(low, act_sc[s, :STATE])


def within_back(after, at, layout, slots, gate_at, gy, cv, dt, lam, lamt, starts, s0, fresh, dec, ggate, nrmt):
    length, inner = gy.shape
    d, ext = nrmt.shape
    blocks = length // BLOCK
    groups = inner // TILE
    full = lambda *shape: pl.BlockSpec(shape, lambda s: (0,) * len(shape))
    tile = pl.BlockSpec((length, TILE), lambda s: (0, s))
    return pl.pallas_call(
        functools.partial(within_back_kernel, slots.plan, len(after)),
        grid=(groups,),
        in_specs=[
            SMEM,
            *[pl.BlockSpec(memory_space=pl.ANY)] * len(after),
            *slots.tiles(lambda s: gate_at + s),
            tile,
            tile,
            pl.BlockSpec((length, TILE), lambda s: (0, groups)),
            full(length, STATE),
            full(length, STATE),
            full(groups, PER, length),
            full(length, 1),
            pl.BlockSpec((TILE, STATE), lambda s: (s, 0)),
            pl.BlockSpec((blocks - 1, TILE, STATE), lambda s: (0, s, 0)),
            full(8, STATE),
            tile,
            full(d, ext),
        ],
        out_specs=[
            tile, full(length, STATE), full(length, 2 * STATE), full(length, d),
            *layout.dealt(lambda s: s),
        ],
        out_shape=[
            jax.ShapeDtypeStruct((length, inner), f32),
            jax.ShapeDtypeStruct((length, STATE), f32),
            jax.ShapeDtypeStruct((length, 2 * STATE), f32),
            jax.ShapeDtypeStruct((length, d), f32),
            *layout.dealt_shape(layout.rows, inner),
        ],
        scratch_shapes=[
            pltpu.VMEM((blocks, BLOCK, BLOCK), f32),
            pltpu.VMEM((blocks, BLOCK, BLOCK), f32),
            pltpu.VMEM((blocks, BLOCK, BLOCK), f32),
            pltpu.VMEM((length, 2 * STATE), bf16),
            pltpu.VMEM((length, 2 * STATE), bf16),
            pltpu.VMEM((length, 2 * STATE), bf16),
            layout.scratch(TILE),
            layout.scratch(TILE),
        ],
        compiler_params=pltpu.CompilerParams(vmem_limit_bytes=VMEM),
        cost_estimate=NO_COST,
        name="within_back",
    )(jnp.concatenate([slots.near, at]), *after, *slots.arrays, gy, cv, cv, dt, lam, lamt, starts, s0, fresh, dec, ggate, nrmt)


def last_kernel(
    plan, skip, at_ref, *refs
):
    refs = refs[skip:]
    w_refs, rest = refs[: len(plan)], refs[len(plan) :]
    last_body(plan, at_ref, w_refs, *rest)


def last_body(
    plan, at_ref, w_refs, gxd_ref, cv_ref, cin_ref, gy_ref, bc_ref, dt_ref, lam_ref, sig_ref, starts_ref, gend_ref,
    later_ref, s0_ref, fresh_ref, dec_ref, nrmt_ref, glam_ref, gbc_ref, gin_ref, skip_ref,
    rate_ref, cw_ref, rim_ref, nrm_ref, gain_ref,
    edge_ref, out_ref, gcw_ref, gcb_ref, gsmall_ref, ngain_ref, *more
):
    b_sc, gb_sc, dt_sc, e_sc, gdt_sc, zs_sc, over_sc, gp_sc, w_sc, d_sc, gnrm_ref = more[-11:]
    keep_ref, send_ref = more[0], more[-12]
    step = pl.program_id(0)
    length = starts_ref.shape[0]
    blocks = length // BLOCK
    groups = pl.num_programs(0) - 2
    starts = starts_ref[...]
    ext = gnrm_ref.shape[0]

    @pl.when(step == 0)
    def _():
        b_sc[...] = silu(bc_ref[:, :STATE].astype(f32)).astype(bf16)
        gb_sc[...] = gbc_ref[:, :STATE]
        dt_sc[...] = split(dt_ref[...])
        for b in range(blocks):
            e_sc[block_of(b)] = split(end_weights(starts, lam_ref[...], b))
        gdt_sc[...] = jnp.zeros_like(gdt_sc)
        zs_sc[...] = jnp.zeros_like(zs_sc)
        over_sc[...] = jnp.zeros_like(over_sc)
        gnrm_ref[length:] = jnp.zeros((RIM, gnrm_ref.shape[1]), f32)
        gnrm_ref[:length] = gin_ref[...]

    def conv_back(gact):
        gcv = gact * dsilu(cv_ref[...].astype(f32))
        gcb_ref[...] = jnp.sum(gcv, axis=0, keepdims=True)
        place = iota((length, 1), 0)
        taps = cw_ref.shape[0]
        cin = cin_ref[...].astype(f32)
        zeros = jnp.zeros((RIM, TILE), f32)
        acc = None
        rows = []
        for k in range(taps):
            back = taps - 1 - k
            term = gcv if back == 0 else jnp.where(place - back >= starts, gcv, 0.0)
            moved = jnp.concatenate([term, zeros], axis=0)
            if back:
                moved = pltpu.roll(moved, ext - back, 0)
            rows.append(jnp.sum(moved * cin, axis=0, keepdims=True))
            part = cw_ref[k : k + 1] * moved
            acc = part if acc is None else acc + part
        gcw_ref[...] = jnp.concatenate(rows, axis=0)
        gp_sc[...] = acc.astype(bf16)

    @pl.when(step < groups)
    def _():
        group = step
        x = silu(cv_ref[...].astype(f32))
        dt = spread(dt_sc[...], group)
        e = spread(e_sc[...], group)
        xd = x * dt
        gend = gend_ref[...].astype(f32)
        grads = [None] * blocks
        for b in reversed(range(blocks)):
            grads[b] = gend
            if b > 0:
                gend = head_rows(dec_ref[b : b + 1], group) * gend + later_ref[b - 1]
        before = states_of(s0_ref[...].astype(f32), fresh_ref, dec_ref, group, blocks)
        parts = []
        for b in range(blocks):
            s = block_of(b)
            low = grads[b].astype(bf16)
            parts.append(e[s] * dot(b_sc[s], low, 1, 1))
            gb_sc[s] += dot((e[s] * xd[s]).astype(bf16), low)
            over = jnp.sum(grads[b] * before[b], axis=1, keepdims=True)
            over_sc[b : b + 1] += dec_ref[b : b + 1] * jnp.sum(
                jnp.where(chooser(group), over, 0.0), axis=0, keepdims=True
            )
        more = jnp.concatenate(parts, axis=0)
        gxd = gxd_ref[...] + more
        zs_sc[...] += gather_heads(xd * more, group)
        gdt_sc[...] += gather_heads(x * gxd, group)
        conv_back(dt * gxd + skip_ref[...] * gy_ref[...].astype(f32))

    @pl.when(step == groups)
    def _():
        conv_back(jnp.concatenate([gb_sc[...], gbc_ref[:, STATE:]], axis=1))

    @pl.when(step <= groups)
    def _():
        gp = gp_sc[...]
        gnrm_ref[...] += dot(gp, assemble(w_refs, w_sc, at_ref, plan), 1, 1)
        deal(dot(nrmt_ref[...], gp), keep_ref, send_ref, d_sc, at_ref)

    @pl.when(step == groups + 1)
    def _():
        tri = lower(BLOCK).astype(f32)
        glam = glam_ref[...] - zs_sc[...]
        rows = []
        for b in range(blocks):
            s = block_of(b)
            end = jnp.sum(zs_sc[s], axis=0, keepdims=True) + over_sc[b : b + 1]
            rows.append(dot(tri, glam[s], 0, 0, precision=PRECISE) + end)
        back = jnp.concatenate(rows, axis=0)
        dt = dt_ref[...]
        gz = (gdt_sc[...] + rate_ref[...] * back) * sig_ref[...]
        gsmall_ref[0:1] = jnp.sum(gz, axis=0, keepdims=True)
        gsmall_ref[1:2] = rate_ref[...] * jnp.sum(dt * back, axis=0, keepdims=True)
        gsmall_ref[2:8] = jnp.zeros((6, STATE), f32)
        low = gz.astype(bf16)
        heads = groups * PER
        w = assemble(w_refs, w_sc, at_ref, plan)[:, :STATE]
        w = jnp.where(iota(w.shape, 1) < heads, w, jnp.zeros((), bf16))
        gnrm_ref[:length] += dot(low, w, 1, 1)
        dw = dot(nrmt_ref[:, :length], low)
        deal(jnp.concatenate([dw, jnp.zeros_like(dw)], axis=1), keep_ref, send_ref, d_sc, at_ref)
        gnrm = gnrm_ref[...]
        edge_ref[...] = gnrm[length:]
        out_ref[...] = gnrm[:length]
        ngain = jnp.sum(gnrm[length:] * rim_ref[...].astype(f32), axis=0, keepdims=True)
        ngain = ngain + jnp.sum(gnrm[:length] * nrm_ref[...].astype(f32), axis=0, keepdims=True)
        ngain_ref[...] = ngain / gain_ref[...]


def last(
    after, at, layout, slots, rest_at, gxd, cv, cin, gy, dt, lam, sig, starts, gend, later, s0, fresh, dec, nrmt, glam, gbc,
    gin, skip, rate, cw, rim, nrm, gain,
):
    length, inner = gy.shape
    d, ext = nrmt.shape
    blocks = length // BLOCK
    groups = inner // TILE
    heads = inner // HEADDIM
    taps = cw.shape[0]
    full = lambda *shape: pl.BlockSpec(shape, lambda s: (0,) * len(shape))
    own = lambda s: jnp.minimum(s, groups - 1)
    col = lambda s: jnp.minimum(s, groups)
    tile = pl.BlockSpec((length, TILE), lambda s: (0, own(s)))
    state = pl.BlockSpec((TILE, STATE), lambda s: (own(s), 0))
    states = pl.BlockSpec((blocks - 1, TILE, STATE), lambda s: (0, own(s), 0))
    return pl.pallas_call(
        functools.partial(last_kernel, slots.plan, len(after)),
        grid=(groups + 2,),
        in_specs=[
            SMEM,
            *[pl.BlockSpec(memory_space=pl.ANY)] * len(after),
            *slots.tiles(lambda s: rest_at + s),
            tile,
            pl.BlockSpec((length, TILE), lambda s: (0, col(s))),
            pl.BlockSpec((ext, TILE), lambda s: (0, col(s))),
            tile,
            pl.BlockSpec((length, TILE), lambda s: (0, groups)),
            full(length, STATE),
            full(length, STATE),
            full(length, STATE),
            full(length, 1),
            state,
            states,
            state,
            states,
            full(8, STATE),
            full(d, ext),
            full(length, STATE),
            full(length, 2 * STATE),
            full(length, d),
            pl.BlockSpec((1, TILE), lambda s: (0, own(s))),
            full(1, STATE),
            pl.BlockSpec((taps, TILE), lambda s: (0, col(s))),
            full(RIM, d),
            full(length, d),
            full(1, d),
        ],
        out_specs=[
            full(RIM, d),
            full(length, d),
            pl.BlockSpec((taps, TILE), lambda s: (0, col(s))),
            pl.BlockSpec((1, TILE), lambda s: (0, col(s))),
            full(8, STATE),
            full(1, d),
            *layout.dealt(lambda s: s),
        ],
        out_shape=[
            jax.ShapeDtypeStruct((RIM, d), f32),
            jax.ShapeDtypeStruct((length, d), f32),
            jax.ShapeDtypeStruct((taps, inner + 2 * STATE), f32),
            jax.ShapeDtypeStruct((1, inner + 2 * STATE), f32),
            jax.ShapeDtypeStruct((8, STATE), f32),
            jax.ShapeDtypeStruct((1, d), f32),
            *layout.dealt_shape(layout.rows, inner + 2 * STATE + heads),
        ],
        scratch_shapes=[
            pltpu.VMEM((length, STATE), bf16),
            pltpu.VMEM((length, STATE), f32),
            pltpu.VMEM((length, 2 * STATE), bf16),
            pltpu.VMEM((length, 2 * STATE), bf16),
            pltpu.VMEM((length, STATE), f32),
            pltpu.VMEM((length, STATE), f32),
            pltpu.VMEM((8, STATE), f32),
            pltpu.VMEM((ext, TILE), bf16),
            layout.scratch(TILE),
            layout.scratch(TILE),
            pltpu.VMEM((ext, d), f32),
        ],
        compiler_params=pltpu.CompilerParams(vmem_limit_bytes=VMEM),
        cost_estimate=NO_COST,
        name="last",
    )(
        jnp.concatenate([slots.near, at]), *after, *slots.arrays, gxd, cv, cin, gy, cv, dt, lam, sig, starts, gend, later, s0, fresh, dec, nrmt,
        glam, gbc, gin, skip, rate, cw, rim, nrm, gain,
    )


def norm_back_kernel(grad_ref, gnrm_ref, rim_ref, resid_ref, gain_ref, *refs):
    out_ref, low_ref = refs[-2:]
    rows, width = out_ref.shape
    gnrm = gnrm_ref[...]
    last = pl.program_id(0) == pl.num_programs(0) - 1
    more = jnp.where(last, rim_ref[...], 0.0)
    gnrm = jnp.concatenate([gnrm[: rows - RIM], gnrm[rows - RIM :] + more], axis=0)
    resid = resid_ref[...]
    scale = lax.rsqrt(jnp.mean(resid * resid, axis=1, keepdims=True) + EPSILON)
    scaled = gnrm * gain_ref[...]
    inner = jnp.sum(scaled * resid, axis=1, keepdims=True)
    total = grad_ref[...] + scale * scaled - resid * (inner * scale * scale * scale / width)
    out_ref[...] = total
    low_ref[...] = total.astype(bf16)


def norm_back(grad, gnrm, rim, resid, gain, after=()):
    length, width = grad.shape
    rows = 128
    block = pl.BlockSpec((rows, width), lambda s: (s, 0))
    fixed = lambda n: pl.BlockSpec((n, width), lambda s: (0, 0))
    return pl.pallas_call(
        norm_back_kernel,
        grid=(length // rows,),
        in_specs=[block, block, fixed(RIM), block, fixed(1)]
        + [pl.BlockSpec(memory_space=pl.ANY)] * len(after),
        out_specs=[block, block],
        out_shape=[
            jax.ShapeDtypeStruct((length, width), f32),
            jax.ShapeDtypeStruct((length, width), bf16),
        ],
        compiler_params=pltpu.CompilerParams(vmem_limit_bytes=VMEM),
        cost_estimate=NO_COST,
        name="norm_back",
    )(grad, gnrm, rim, resid, gain, *after)


def passed_along(shard, axis, by):
    devices = lax.axis_size(axis)
    pairs = [(i, i + by) for i in range(devices) if 0 <= i + by < devices]
    return lax.ppermute(shard, axis, pairs)


def swap(value, axis, by):
    return lax.ppermute(value, axis, [(i, i ^ by) for i in range(lax.axis_size(axis))])


def decay_of(ref, at):
    return ref[at : at + 1].astype(f32) + ref[at + 1 : at + 2].astype(f32)


def joint_kernel(reverse, at_ref, mine_ref, other_ref, *refs):
    sent_ref = refs[-1]
    half = sent_ref.shape[0] - RIM
    odd = at_ref[1] % 2
    mine, other = decay_of(mine_ref, 2 * half), decay_of(other_ref, 2 * half)
    by = jnp.where((odd == 1) == reverse, other, mine)
    for g in range(half // TILE):
        rows = pl.ds(pl.multiple_of(odd * half + g * TILE, TILE), TILE)
        here, there = mine_ref[rows].astype(f32), other_ref[rows].astype(f32)
        first = jnp.where((odd == 1) == reverse, here, there)
        second = jnp.where((odd == 1) == reverse, there, here)
        scale = head_rows(by, odd * (half // TILE) + g)
        sent_ref[g * TILE : (g + 1) * TILE] = (scale * first + second).astype(bf16)
    sent_ref[half:] = decay_rows(mine * other)


def entering_kernel(reverse, pairs, at_ref, *refs):
    got, out_ref = refs[: pairs - 1], refs[-1]
    half = out_ref.shape[0]
    odd, chip = at_ref[1] % 2, at_ref[1] // 2
    decays = [decay_of(a, half) for a in got]
    shares = []
    for i in range(1, pairs):
        source = chip ^ i
        counts = source > chip if reverse else source < chip
        share = jnp.where(counts, jnp.ones((1, STATE), f32), 0.0)
        for j in range(1, pairs):
            if j != i:
                by = chip ^ j
                inside = (by < source) & (by > chip) if reverse else (by > source) & (by < chip)
                share = jnp.where(inside, share * decays[j - 1], share)
        shares.append(share)
    for g in range(half // TILE):
        rows = slice(g * TILE, (g + 1) * TILE)
        total = None
        for share, a in zip(shares, got):
            part = head_rows(share, odd * (half // TILE) + g) * a[rows].astype(f32)
            total = part if total is None else total + part
        out_ref[rows] = total.astype(bf16)


def behind_kernel(reverse, at_ref, half_ref, rest_ref, other_ref, out_ref):
    half = half_ref.shape[0]
    odd = at_ref[1] % 2
    decay = decay_of(other_ref, 2 * half)
    for g in range(2 * half // TILE):
        rows = slice(g * TILE, (g + 1) * TILE)
        upper = g * TILE >= half
        short = slice(rows.start % half, rows.start % half + TILE)
        own = (odd == 1) == upper
        value = jnp.where(own, half_ref[short].astype(f32), rest_ref[short].astype(f32))
        later = head_rows(decay, g) * value + other_ref[rows].astype(f32)
        out_ref[rows] = jnp.where((odd == 1) != reverse, later, value)


def small_call(kernel, at, args, shapes, after=(), name=None):
    args = list(args) + list(after)
    count = len(args) - len(after)
    vmem = pl.BlockSpec(memory_space=pltpu.VMEM)
    return pl.pallas_call(
        kernel,
        in_specs=[SMEM] + [vmem] * count + [pl.BlockSpec(memory_space=pl.ANY)] * len(after),
        out_specs=[vmem] * len(shapes),
        out_shape=shapes,
        compiler_params=pltpu.CompilerParams(vmem_limit_bytes=VMEM),
        cost_estimate=NO_COST,
        name=name,
    )(at, *args)


def carried_over(here, state, reverse, meanwhile):
    pairs = lax.axis_size("seq") // 2
    rows = state.shape[0] - RIM
    other = swap(state, "seq", 1)
    sent_shape = jax.ShapeDtypeStruct((rows // 2 + RIM, STATE), bf16)
    (sent,) = small_call(
        functools.partial(joint_kernel, reverse), here, [state, other], [sent_shape], name="joint"
    )
    got = [swap(sent, "seq", 2 * i) for i in range(1, pairs)]
    beside = meanwhile(sent)
    half_shape = jax.ShapeDtypeStruct((rows // 2, STATE), bf16)
    (half,) = small_call(
        functools.partial(entering_kernel, reverse, pairs), here, got, [half_shape],
        after=[beside[0]], name="entering",
    )
    rest = swap(half, "seq", 1)
    (whole,) = small_call(
        functools.partial(behind_kernel, reverse), here, [half, rest, other],
        [jax.ShapeDtypeStruct((rows, STATE), f32)], name="behind",
    )
    return whole, beside, half


def cut_kernel(inner, at_ref, in_ref, out_ref, rest_ref, *targets):
    rows, share, width = rest_ref.shape[0], in_ref.shape[2], out_ref.shape[2]
    for layer, target in enumerate(targets):

        @pl.when(pl.program_id(0) == layer)
        def _():
            pick = iota((rows, share), 1) == rows * at_ref[1] + iota((rows, share), 0)
            pick = pick.astype(f32).astype(bf16)
            rest = dot(pick, in_ref[0, inner:], 1, 1).astype(bf16)
            if layer == 0:
                rest_ref[...] = rest
            else:
                target[:, 2 * inner :] = rest
            target[:, :inner] = dot(pick, in_ref[0, :inner], 1, 1).astype(bf16)
            for f in range(inner // width):
                part = out_ref[0, f * rows : (f + 1) * rows]
                target[:, inner + f * width : inner + (f + 1) * width] = part


def cut(at, layout, in_turned, out_weight):
    layers, wide, share = in_turned.shape
    width = out_weight.shape[2]
    rows = layout.rows
    fold = out_weight.shape[1] // share
    inner = fold * width
    shapes = [
        jax.ShapeDtypeStruct((rows, n), bf16)
        for n in (wide - inner, 2 * inner, *[wide + inner] * (layers - 1))
    ]
    return pl.pallas_call(
        functools.partial(cut_kernel, inner),
        grid_spec=pltpu.PrefetchScalarGridSpec(
            num_scalar_prefetch=1,
            grid=(layers,),
            in_specs=[
                pl.BlockSpec((1, wide, share), lambda s, at_ref: (s, 0, 0)),
                pl.BlockSpec((1, fold * rows, width), lambda s, at_ref: (s, at_ref[1], 0)),
            ],
            out_specs=[pl.BlockSpec(a.shape, lambda s, at_ref: (0, 0)) for a in shapes],
        ),
        out_shape=shapes,
        compiler_params=pltpu.CompilerParams(vmem_limit_bytes=VMEM),
        cost_estimate=NO_COST,
        name="cut",
    )(at, in_turned, out_weight)


X, Y = 2, 4


def over_wa(piece, layout):
    return [piece] + [swap(piece, "wa", q) for q in range(1, layout.owners)]


def stack_kernel(count, *refs):
    for i in range(count):
        refs[-1][0, i] = refs[i][...]


def stack(pieces, after=()):
    vmem = pl.BlockSpec(memory_space=pltpu.VMEM)
    return pl.pallas_call(
        functools.partial(stack_kernel, len(pieces)),
        in_specs=[vmem] * len(pieces) + [pl.BlockSpec(memory_space=pl.ANY)] * len(after),
        out_specs=vmem,
        out_shape=jax.ShapeDtypeStruct((1, len(pieces), *pieces[0].shape), pieces[0].dtype),
        compiler_params=pltpu.CompilerParams(vmem_limit_bytes=VMEM),
        cost_estimate=NO_COST,
        name="stack",
    )(*pieces, *after)


def straight(here, pieces, after=()):
    return across(here, stack(pieces, after))


def across(near, own):
    arrays = [own] + [swap(own, "seq", by) for by in (X, Y, X + Y)]
    return Slots(near, arrays, [((r,), 0) for r in (0, X, Y, X + Y)])


def near_by(slots, after=()):
    arrays = [tie(a, after) if after else a for a in slots.arrays]
    return Slots(
        slots.near, arrays + [swap(a, "seq", 1) for a in arrays],
        slots.plan + tuple((tuple(r + 1 for r in places), owner) for places, owner in slots.plan),
    )


def like_cores(layout):
    places, owners = layout.places, layout.owners
    return [
        [p * owners + w for p in range(near, places, 2) for w in range(owners)] for near in (0, 1)
    ]


def tie(value, after):
    def kernel(*refs):
        pass

    return pl.pallas_call(
        kernel,
        in_specs=[pl.BlockSpec(memory_space=pl.ANY)] * (1 + len(after)),
        out_specs=pl.BlockSpec(memory_space=pl.ANY),
        out_shape=jax.ShapeDtypeStruct(value.shape, value.dtype),
        input_output_aliases={0: 0},
        cost_estimate=NO_COST,
        name="tie",
    )(value, *after)


def pack_kernel(count, rows, *refs):
    outs = refs[-4:]
    at = 0
    for k in range(count):
        keeps, gots = refs[4 * k : 4 * k + 2], refs[4 * k + 2 : 4 * k + 4]
        width = keeps[0].shape[-1]
        for f in range(keeps[0].shape[2] // rows):
            s = slice(f * rows, (f + 1) * rows)
            for part, pairs in ((0, ((0, 2), (1, 3))), (1, ((0, 1), (2, 3)))):
                for place, target in zip(pairs, outs[2 * part : 2 * part + 2]):
                    for n, i in enumerate(place):
                        total = keeps[part][i, 0, s].astype(f32) + gots[part][i, 0, s].astype(f32)
                        target[n, 0, :, at : at + width] = total.astype(bf16)
            at += -(-width // STATE) * STATE


def pack(parts, layout, after=()):
    half = layout.owners // 2
    flat, specs = [], []
    for pair in parts:
        for a in pair:
            block = (a.shape[0], 1, *a.shape[2:])
            flat += [a, a]
            specs += [
                pl.BlockSpec(block, lambda q: (0, q, 0, 0)),
                pl.BlockSpec(block, lambda q: (0, half + q, 0, 0)),
            ]
    width = 0
    for keep, _ in parts:
        width = -(-width // STATE) * STATE + keep.shape[2] // layout.rows * keep.shape[3]
    out = jax.ShapeDtypeStruct((2, half, layout.rows, width), bf16)
    return pl.pallas_call(
        functools.partial(pack_kernel, len(parts), layout.rows),
        grid=(half,),
        in_specs=specs + [pl.BlockSpec(memory_space=pl.ANY)] * len(after),
        out_specs=[pl.BlockSpec((2, 1, layout.rows, width), lambda q: (0, q, 0, 0))] * 4,
        out_shape=[out] * 4,
        compiler_params=pltpu.CompilerParams(vmem_limit_bytes=VMEM),
        cost_estimate=NO_COST,
        name="pack",
    )(*flat, *after)


def small_rows(layer_shapes):
    table = []
    for k, shape in enumerate(layer_shapes):
        for at in range(0, shape[1], STATE):
            table.append((k, shape[0], at))
    return sorted(table, key=lambda entry: -entry[1])


def deal_small_kernel(table, arrays, at_ref, *refs):
    keep_ref, send_ref, all_sc = refs[arrays : arrays + 3]
    places, rows, width = all_sc.shape
    all_sc[...] = jnp.zeros_like(all_sc)
    row = 0
    for k, count, at in table:
        all_sc[row // rows, row % rows : row % rows + count] = refs[k][:count, at : at + width]
        row += count
    for r in range(places):
        target = send_ref if r % 2 else keep_ref
        part = all_sc[at_ref[1] ^ r].astype(bf16)
        for q in range(target.shape[1]):
            target[r // 2, q] = part


def deal_small(here, values, layout):
    shapes = [(min(a.shape[0], 4), a.shape[1]) for a in values]
    table = small_rows(shapes)
    assert sum(entry[1] for entry in table) <= layout.places * layout.rows
    shape = jax.ShapeDtypeStruct((layout.places // 2, layout.owners, layout.rows, STATE), bf16)
    vmem = pl.BlockSpec(memory_space=pltpu.VMEM)
    return pl.pallas_call(
        functools.partial(deal_small_kernel, table, len(values)),
        in_specs=[SMEM] + [vmem] * len(values),
        out_specs=[vmem, vmem],
        out_shape=[shape, shape],
        scratch_shapes=[pltpu.VMEM((layout.places, layout.rows, STATE), f32)],
        compiler_params=pltpu.CompilerParams(vmem_limit_bytes=VMEM),
        cost_estimate=NO_COST,
        name="deal_small",
    )(here, *values)


def place_small_kernel(table, shapes, at_ref, even_ref, odd_ref, *refs):
    count = len(shapes)
    outs, all_sc, row_scs = refs[:-1 - count], refs[-1 - count], refs[-count:]
    pairs, rows = even_ref.shape[:2]
    for i in range(pairs):
        all_sc[(2 * i) ^ at_ref[1]] = even_ref[i].astype(f32)
        all_sc[(2 * i + 1) ^ at_ref[1]] = odd_ref[i].astype(f32)
    row = 0
    for k, n, at in table:
        row_scs[k][:n, at : at + STATE] = all_sc[row // rows, row % rows : row % rows + n]
        row += n
    each = len(shapes) // outs[0].shape[0]

    def share(k, width):
        whole = row_scs[k][...]
        return pltpu.roll(whole, lax.rem(whole.shape[1] - width * at_ref[0], whole.shape[1]), 1)

    for layer in range(outs[0].shape[0]):
        cw, cb, heads, gain_in, gain_gated, skip = range(each * layer, each * layer + each)
        outs[0][layer] = share(cw, outs[0].shape[2])[:4, : outs[0].shape[2]]
        one = slice(layer, layer + 1)
        outs[1][one] = share(cb, outs[1].shape[1])[:1, : outs[1].shape[1]]
        per = outs[2].shape[1]
        two = share(heads, per)
        outs[2][one] = two[1:2, :per]
        outs[3][one] = two[:1, :per]
        outs[4][one] = share(skip, per)[:1, :per]
        outs[5][one] = share(gain_in, outs[5].shape[1])[:1, : outs[5].shape[1]]
        outs[6][one] = share(gain_gated, outs[6].shape[1])[:1, : outs[6].shape[1]]


def place_small(here, even, odd, values, shapes, layout):
    sizes = [(min(a.shape[0], 4), a.shape[1]) for a in values]
    table = small_rows(sizes)
    vmem = pl.BlockSpec(memory_space=pltpu.VMEM)
    block = (layout.places // 2, layout.rows, STATE)
    last = even.shape[2] // STATE - 1
    return pl.pallas_call(
        functools.partial(place_small_kernel, table, sizes),
        grid=(1,),
        in_specs=[SMEM] + [pl.BlockSpec(block, lambda s: (0, 0, last))] * 2,
        out_specs=[vmem] * len(shapes),
        out_shape=[jax.ShapeDtypeStruct(shape, f32) for shape in shapes],
        scratch_shapes=[pltpu.VMEM((layout.places, layout.rows, STATE), f32)]
        + [pltpu.VMEM((8, width), f32) for _, width in sizes],
        compiler_params=pltpu.CompilerParams(vmem_limit_bytes=VMEM),
        cost_estimate=NO_COST,
        name="place_small",
    )(here, even, odd)


def pair_kernel(count, rows, *refs):
    target = refs[-1]
    at = 0
    for k in range(count):
        keep, got = refs[2 * k : 2 * k + 2]
        width = keep.shape[-1]
        for f in range(keep.shape[2] // rows):
            s = slice(f * rows, (f + 1) * rows)
            total = keep[:, 0, s].astype(f32) + got[:, 0, s].astype(f32)
            target[:, 0, :, at : at + width] = total.astype(bf16)
            at += width


def pair_sums(parts, layout, after=()):
    flat = [a for pair in parts for a in pair]
    width = sum(keep.shape[2] // layout.rows * keep.shape[3] for keep, _ in parts)
    pairs = layout.places // 2
    return pl.pallas_call(
        functools.partial(pair_kernel, len(parts), layout.rows),
        grid=(layout.owners,),
        in_specs=[pl.BlockSpec((pairs, 1, *a.shape[2:]), lambda q: (0, q, 0, 0)) for a in flat]
        + [pl.BlockSpec(memory_space=pl.ANY)] * len(after),
        out_specs=pl.BlockSpec((pairs, 1, layout.rows, width), lambda q: (0, q, 0, 0)),
        out_shape=jax.ShapeDtypeStruct((pairs, layout.owners, layout.rows, width), bf16),
        compiler_params=pltpu.CompilerParams(vmem_limit_bytes=VMEM),
        cost_estimate=NO_COST,
        name="pair_sums",
    )(*flat, *after)


def halve_kernel(*refs):
    outs = refs[-4:]
    for part in (0, 1):
        keep, got = refs[2 * part : 2 * part + 2]
        for n in (0, 1):
            total = keep[n].astype(f32) + got[n].astype(f32)
            outs[2 * part + n][...] = total.astype(bf16)


def halve(arrays, after=()):
    two, half, rows, width = arrays[0].shape
    return pl.pallas_call(
        halve_kernel,
        grid=(half,),
        in_specs=[pl.BlockSpec((2, 1, rows, width), lambda q: (0, q, 0, 0))] * 4
        + [pl.BlockSpec(memory_space=pl.ANY)] * len(after),
        out_specs=[pl.BlockSpec((1, rows, width), lambda q: (q, 0, 0))] * 4,
        out_shape=[jax.ShapeDtypeStruct((half, rows, width), bf16)] * 4,
        compiler_params=pltpu.CompilerParams(vmem_limit_bytes=VMEM),
        cost_estimate=NO_COST,
        name="halve",
    )(*arrays, *after)


def apart_kernel(owners, at_ref, *refs):
    outs = refs[-owners:]
    half = owners // 2
    for q in range(owners):
        keep, got = refs[:2] if q < half else refs[2:4]
        outs[q][...] = (keep[q % half].astype(f32) + got[q % half].astype(f32)).astype(bf16)


def sum_kernel(count, at_ref, *refs):
    total = refs[0][...].astype(f32)
    for a in refs[1:count]:
        total = total + a[...].astype(f32)
    refs[-1][...] = total.astype(bf16)


class Collect:
    def __init__(self, here, layout):
        self.here, self.layout, self.parts = here, layout, {}

    def add(self, order, keep, send, after=()):
        if after:
            send = tie(send, after)
        self.parts[order] = (keep, swap(send, "seq", 1))
        return self.parts[order][1]

    def pack(self, *after):
        parts = [self.parts[k] for k in sorted(self.parts)]
        keep_a, send_a, keep_b, send_b = pack(parts, self.layout, after)
        self.now = [keep_a, swap(send_a, "seq", X), keep_b, swap(send_b, "seq", Y)]

    def halve(self, *after):
        keep_a, send_a, keep_b, send_b = halve(self.now, after)
        self.now = [keep_a, swap(send_a, "seq", Y), keep_b, swap(send_b, "seq", X)]

    def apart(self, *after):
        owners = self.layout.owners
        shape = jax.ShapeDtypeStruct(self.now[0].shape[1:], bf16)
        out = small_call(
            functools.partial(apart_kernel, owners), self.here, self.now, [shape] * owners, after,
            name="apart",
        )
        self.now = [out[0]] + [swap(out[q], "wa", q) for q in range(1, owners)]

    def whole(self, *after):
        shape = jax.ShapeDtypeStruct(self.now[0].shape, bf16)
        (own,) = small_call(
            functools.partial(sum_kernel, len(self.now)), self.here, self.now, [shape], after,
            name="whole",
        )
        self.now = [own]

    def at_once(self):
        places, owners = self.layout.places, self.layout.owners
        parts = [self.parts[k] for k in sorted(self.parts)]
        total = pair_sums(parts, self.layout)
        total = total.reshape(places // 2 * owners, *total.shape[2:])
        like = like_cores(self.layout)
        self.now = [lax.psum_scatter(total, ("seq", "wa"), axis_index_groups=like)]

    def gathered(self, *after):
        self.now = [lax.all_gather(tie(self.now[0], after), "seq")]

    def spread(self, *after):
        own = tie(self.now[0], after) if after else self.now[0]
        even = jnp.stack([own] + [swap(own, "seq", by) for by in (X, Y, X + Y)])
        self.now = [even, swap(even, "seq", 1)]


WIDE = 1024


def place_kernel(ins, sources, given, at_ref, steps_ref, *refs):
    found, outs, own_sc = refs[:sources], refs[sources + given : -1], refs[-1]
    if sources == 1:
        value = found[0][...].astype(f32)
    else:
        for i in range(found[0].shape[0]):
            own_sc[(2 * i) ^ at_ref[1]] = found[0][i]
            own_sc[(2 * i + 1) ^ at_ref[1]] = found[1][i]
        value = own_sc[...].astype(f32)
    if ins:
        @pl.when(pl.program_id(0) < ins)
        def _():
            outs[0][0] = value.reshape(-1, WIDE).T

    if len(outs) > (ins > 0):
        @pl.when(pl.program_id(0) >= ins)
        def _():
            outs[-1][0, :, 0] = value


def place(at, layer, found, parts, outs, shapes, layout):
    rows = layout.rows
    sources, in_tiles, out_tiles = [], [], []
    ins = sum(count for inside, _, count, _ in parts if inside)
    for inside, source, count, target in parts:
        sources += range(source, source + count)
        (in_tiles if inside else out_tiles).extend(range(target, target + count))
    steps = len(sources)
    in_tiles = in_tiles + (in_tiles[-1:] or [0]) * (steps - len(in_tiles))
    out_tiles = (out_tiles[:1] or [0]) * (steps - len(out_tiles)) + out_tiles
    table = jnp.array([sources, in_tiles, out_tiles], jnp.int32)
    across = shapes[1][-1] // WIDE
    both = [
        pl.BlockSpec((1, WIDE, shapes[0][2]), lambda s, at_ref, t: (layer, t[1, s], 0)),
        pl.BlockSpec(
            (1, layout.places, 1, rows, WIDE),
            lambda s, at_ref, t: (layer, 0, t[2, s] // across, 0, t[2, s] % across),
        ),
    ]
    used = [i for i, needed in enumerate((ins > 0, ins < steps)) if needed]
    given = [outs[i] for i in used if outs[i] is not None]
    source = pl.BlockSpec((found[0].shape[0], rows, WIDE), lambda s, at_ref, t: (0, 0, t[0, s]))
    made = pl.pallas_call(
        functools.partial(place_kernel, ins, len(found), len(given)),
        grid_spec=pltpu.PrefetchScalarGridSpec(
            num_scalar_prefetch=2,
            grid=(steps,),
            in_specs=[source] * len(found) + [pl.BlockSpec(memory_space=pl.ANY)] * len(given),
            out_specs=[both[i] for i in used],
            scratch_shapes=[pltpu.VMEM((layout.places, rows, WIDE), bf16)],
        ),
        out_shape=[jax.ShapeDtypeStruct(shapes[i], f32) for i in used],
        input_output_aliases={2 + len(found) + i: i for i in range(len(given))},
        compiler_params=pltpu.CompilerParams(vmem_limit_bytes=VMEM),
        cost_estimate=NO_COST,
        name="place",
    )(at, table, *found, *given)
    outs = list(outs)
    for i, a in zip(used, made):
        outs[i] = a
    return outs


def lanes(row):
    return jnp.pad(row, (0, STATE - row.shape[0]))[None]


def local(
    tokens,
    in_weight,
    out_weight,
    conv_weight,
    conv_bias,
    a_log,
    dt_bias,
    skip_d,
    norm_gain,
    gated_gain,
    doc_start,
    cotangent,
):
    layers = in_weight.shape[0]
    length, width = tokens.shape[1:]
    taps, channels = conv_weight.shape[1:]
    owners = lax.axis_size("wa")
    heads = a_log.shape[1] * owners
    inner = heads * HEADDIM
    starts = (doc_start[0] - lax.axis_index("seq") * length)[:, None]

    devices = lax.axis_size("seq")
    rows = in_weight.shape[1] // devices
    here = jnp.stack([lax.axis_index("wa"), lax.axis_index("seq")]).astype(jnp.int32)
    fold = inner // width
    dealing = devices == 2 * Y and owners > 1 and owners & (owners - 1) == 0 and rows % RIM == 0
    weights = []
    if dealing:
        layout = Layout(owners, devices, rows)
        at = here
        in_turned = in_weight.swapaxes(1, 2)
        pieces = cut(at, layout, in_turned, out_weight)
        first_column = over_wa(pieces[0], layout)
        early = straight(here, first_column)
        column = over_wa(pieces[1], layout)
        late = straight(here, column, early.arrays[1:])
        weights.append((near_by(early), 0, late))
        next_own = lax.all_gather(tie(pieces[2], column[1:]), "wa")[None]
        straight_place = jnp.stack([jnp.zeros_like(here[0]), here[1]])
        assert layers == 2
    else:
        layout = Layout(owners, 1, in_weight.shape[1])
        at = jnp.zeros((2,), jnp.int32)
        for layer in range(layers):
            out = out_weight[layer].reshape(fold, layout.rows, width).swapaxes(0, 1)
            out = out.reshape(layout.rows, fold * width)
            gate, rest = in_weight[layer][:, :inner], in_weight[layer][:, inner:]
            found = [
                Slots(at, [lax.all_gather(part, "wa")[None]], [((0,), 0)])
                for part in (rest, jnp.concatenate([gate, out], axis=1))
            ]
            weights.append((found[0], 0, found[1]))
    own_small = [
        conv_weight.reshape(layers, taps * channels), conv_bias, a_log, dt_bias, skip_d,
        norm_gain, gated_gain,
    ]
    small = jnp.concatenate(own_small, axis=1)
    if dealing:
        small = tie(small, weights[0][0].arrays[:1])
    if owners & (owners - 1) == 0:
        small = jnp.stack([small] + [swap(small, "wa", q) for q in range(1, owners)])
        small = jnp.take(small, jnp.arange(owners) ^ lax.axis_index("wa"), axis=0).astype(f32)
    else:
        small = lax.all_gather(small, "wa", axis=0).astype(f32)
    sizes = [a.shape[1] for a in own_small]
    params = []
    for layer in range(layers):
        found, col = [], 0
        for i, size in enumerate(sizes):
            part = small[:, layer, col : col + size]
            col += size
            if i == 0:
                part = part.reshape(owners, taps, channels).swapaxes(0, 1)
                found.append(part.reshape(taps, owners * channels))
            else:
                found.append(part.reshape(owners * size))
        params.append(found)

    resid = tokens[0].astype(f32)
    normed = (
        resid
        * lax.rsqrt(jnp.mean(resid * resid, axis=1, keepdims=True) + EPSILON)
        * params[0][5]
    ).astype(bf16)
    records = []
    for layer in range(layers):
        cw, cb, alog, dtb, skip, ngain, ggain = params[layer]
        rate = lanes(-jnp.exp(alog))
        skip_row = jnp.repeat(skip, HEADDIM)[None]
        if dealing and layer > 0:
            split = inner + fold * width
            found = across(straight_place, tie(next_own[..., split:], [beside_out]))
            late = across(straight_place, tie(next_own[..., :split], found.arrays[1:]))
            weights.append((near_by(found, [normed]), 0, late))
        early, rest_at, late = weights[layer]
        rim = passed_along(normed[length - RIM :], "seq", 1)
        nrm = normed
        cin, cv, dt, lam, sig, lamt, state, fresh, dec, nrmt = first(
            layout, rim, nrm, early, rest_at, cw, cb[None], lanes(dtb), rate, starts, heads
        )
        y = within(cv, dt, lam, lamt, starts, skip_row)
        if dealing:
            state = tie(state, [*late.arrays[1:], y])
        s0, _, entered = carried_over(here, state, False, lambda sent: [sent])
        if dealing:
            late = near_by(late)
            weights[layer] = (early, 0, late)
        beside_out = s0 if not dealing else entered
        gain_next = params[min(layer + 1, layers - 1)][5][None]
        gate, y, gated, scale, resid_next, low, normed = join(
            layout, late, 0, 1, nrm, y, cv, lam, starts, s0, fresh, dec, ggain[None], resid, gain_next
        )
        records.append(
            (resid, cin, cv, dt, lam, sig, lamt, fresh, dec, nrmt, s0, gate, y, gated, scale,
             rate, skip_row, rim, nrm)
        )
        resid = resid_next
    result = low[None]
    grad_low = cotangent[0]
    grad = grad_low.astype(f32)
    big = [None] * layers
    little = [None] * layers
    for layer in reversed(range(layers)):
        cw, cb, alog, dtb, skip, ngain, ggain = params[layer]
        early, rest_at, late = weights[layer]
        (resid, cin, cv, dt, lam, sig, lamt, fresh, dec, nrmt, s0, gate, y, gated, scale,
         rate, skip_row, first_rim, nrm) = records[layer]
        top = layer == layers - 1
        to = at
        if dealing and top:
            to = jnp.stack([jnp.zeros_like(at[0]), at[1] % 2])
        gy, ggate, gggain, gskip, later, total, *dwo = gate_back(
            (), to, layout, late, 1, grad_low, y, gate, gated, scale, ggain[None], cv, lam, starts,
            dec,
        )
        if dealing and top:
            upper = Collect(here, layout)
            upper.add(1, *dwo)
        elif dealing:
            under = Collect(here, layout)

        def beside(sent):
            return within_back(
                (), to, layout, late, 0, gy, cv, dt, lam, lamt, starts, s0, fresh, dec, ggate, nrmt
            )

        gend, (gxd, glam, gbc, gnrm_gate, *dw_gate), _ = carried_over(here, total, True, beside)
        if dealing and top:
            upper.add(0, *dw_gate, [gend])
        elif dealing:
            under.add(1, *dwo, [gend])
            under.add(0, *dw_gate, [gend])
            under.pack()
        edge, gnrm, gcw, gcb, gsmall, gngain, *dw_rest = last(
            under.now[:1] if dealing and not top else (), to, layout, early, rest_at, gxd, cv, cin, gy, dt, lam, sig, starts, gend, later, s0,
            fresh, dec, nrmt, glam, gbc, gnrm_gate, skip_row, rate, cw, first_rim, nrm,
            ngain[None],
        )
        if dealing and top:
            upper.add(2, *dw_rest)
        elif dealing:
            under.halve(gsmall)
            tail = Collect(here, layout)
            tail.add(0, *dw_rest, [under.now[0]])
            edge = tie(edge, [under.now[0]])
        rim = passed_along(edge, "seq", -1)
        if layer > 0 or not dealing:
            grad, grad_low = norm_back(grad, gnrm, rim, resid, ngain[None])
        if dealing and top:
            upper.at_once()
        big[layer] = (dw_gate, dwo, dw_rest)
        little[layer] = (gcw, gcb, gsmall[:2], gngain, gggain, gskip)

    in_width, rest = in_weight.shape[2], in_weight.shape[2] - inner
    if dealing:
        assert layers == 2
        values = [a for layer in range(layers) for a in little[layer]]
        tail.add(1, *deal_small(here, values, layout))
        tail.pack()
        under.apart(tail.now[0])
        tail.halve(under.now[0])
        upper.gathered(tail.now[0])
        grad, _ = norm_back(grad, gnrm, rim, resid, ngain[None], tail.now[:1])
        both = [(layers, in_width, in_weight.shape[1]), (layers, layout.places, fold, layout.rows, width)]
        tiles = inner // WIDE
        more = -(-rest // WIDE)
        under.whole(grad)
        tail.apart(under.now[0])
        under.spread(tail.now[0])
        made = place(
            at, 1, upper.now,
            ((True, 0, tiles, 0), (True, 2 * tiles, more, tiles), (False, tiles, tiles, 0)),
            [None, None], both, layout,
        )
        tail.whole(made[0])
        tail.spread()
        made = place(
            at, 0, under.now, ((True, 0, tiles, 0), (False, tiles, tiles, 0)), made, both, layout
        )
        made = place(at, 0, tail.now, ((True, 0, more, tiles),), made, both, layout)
        in_grad = made[0].swapaxes(1, 2)
        out_grad = made[1].reshape(out_weight.shape)
        found = place_small(
            here, *tail.now, values, [a.shape for a in (conv_weight, conv_bias, a_log, dt_bias, skip_d, norm_gain, gated_gain)], layout
        )
    else:

        def owned(part):
            part = part.reshape(owners, -1, part.shape[-1])
            part = lax.psum_scatter(part, "wa", scatter_dimension=0)
            return lax.psum(part, "seq").astype(f32)

        in_grad = jnp.stack(
            [
                jnp.concatenate([owned(big[layer][0][0]), owned(big[layer][2][0])], axis=1)
                for layer in range(layers)
            ]
        )
        out_grad = jnp.stack([owned(big[layer][1][0]) for layer in range(layers)])
        rows = []
        for gcw, gcb, two, gngain, gggain, gskip in little:
            gcw = gcw.reshape(taps, owners, channels).swapaxes(0, 1).reshape(owners, -1)
            flat = (gcb[0], two[1, :heads], two[0, :heads], gskip[0, :heads], gngain[0], gggain[0])
            rows.append(jnp.concatenate([gcw] + [a.reshape(owners, -1) for a in flat], axis=1))
        mine = lax.dynamic_index_in_dim(
            lax.psum(jnp.stack(rows, axis=1), ("wa", "seq")), lax.axis_index("wa"), 0, keepdims=False
        )
        found, col = [], 0
        for i, size in enumerate(sizes):
            part = mine[:, col : col + size]
            col += size
            found.append(part.reshape(layers, taps, channels) if i == 0 else part)
    return (result, grad[None], in_grad, out_grad, *found)


def solution(mesh):
    in_specs = (
        P("wa", "seq", None),
        P(None, "wa", None),
        P(None, "wa", None),
        P(None, None, "wa"),
        P(None, "wa"),
        P(None, "wa"),
        P(None, "wa"),
        P(None, "wa"),
        P(None, "wa"),
        P(None, "wa"),
        P("wa", "seq"),
        P("wa", "seq", None),
    )
    out_specs = (
        P("wa", "seq", None),
        P("wa", "seq", None),
        P(None, "wa", None),
        P(None, "wa", None),
        P(None, None, "wa"),
        P(None, "wa"),
        P(None, "wa"),
        P(None, "wa"),
        P(None, "wa"),
        P(None, "wa"),
        P(None, "wa"),
    )
    return jax.shard_map(local, mesh=mesh, in_specs=in_specs, out_specs=out_specs, check_vma=False)
```

```python
import functools

import jax
import jax.numpy as jnp
from jax import lax
from jax.experimental import pallas as pl
from jax.experimental.pallas import tpu as pltpu
from jax.sharding import PartitionSpec as P

HEADDIM = 64
STATE = 128
BLOCK = 256
TILE = 256
PER = TILE // HEADDIM
RIM = 16
EPSILON = 1e-05
PRECISE = lax.Precision.HIGHEST
f32 = jnp.float32
bf16 = jnp.bfloat16
FAR = -1e30
VMEM = 60 * 2**20
NO_COST = pl.CostEstimate(flops=0, bytes_accessed=0, transcendentals=0)


def dot(a, b, ca=1, cb=0, precision=None):
    return lax.dot_general(
        a, b, (((ca,), (cb,)), ((), ())), precision=precision, preferred_element_type=f32
    )


def iota(shape, axis):
    return lax.broadcasted_iota(jnp.int32, shape, axis)


def logistic(v):
    return 0.5 + 0.5 * jnp.tanh(0.5 * v)


def silu(v):
    return v * logistic(v)


def dsilu(v):
    s = logistic(v)
    return s * (1.0 + v * (1.0 - s))


def split(q):
    high = q.astype(bf16)
    return jnp.concatenate([high, (q - high.astype(f32)).astype(bf16)], axis=1)


def spread(pair, group):
    rows = iota((2 * STATE, TILE), 0) % STATE
    cols = PER * group + iota((2 * STATE, TILE), 1) // HEADDIM
    return dot(pair, (rows == cols).astype(f32).astype(bf16))


def chooser(group):
    return iota((TILE, STATE), 1) == PER * group + iota((TILE, STATE), 0) // HEADDIM


def gather_heads(z, group):
    pick = chooser(group).astype(f32).astype(bf16)
    high = z.astype(bf16)
    low = (z - high.astype(f32)).astype(bf16)
    return dot(high, pick) + dot(low, pick)


def head_rows(row, group):
    return jnp.sum(jnp.where(chooser(group), row, 0.0), axis=1, keepdims=True)


def lower(n):
    return iota((n, n), 0) >= iota((n, n), 1)


def decay_rows(decay):
    high = decay.astype(bf16).astype(f32)
    zeros = jnp.zeros((RIM - 2, STATE), f32)
    return jnp.concatenate([high, decay - high, zeros], axis=0).astype(bf16)


def block_of(b):
    return slice(b * BLOCK, (b + 1) * BLOCK)


def end_weights(starts, lam, b):
    s = block_of(b)
    last = (b + 1) * BLOCK - 1
    place = b * BLOCK + iota((BLOCK, 1), 0)
    keep = place >= starts[last : last + 1]
    return jnp.where(keep, jnp.exp(lam[last : last + 1] - lam[s]), 0.0)


def reach_weights(starts, lam, b):
    s = block_of(b)
    return jnp.where(starts[s] < b * BLOCK, jnp.exp(lam[s]), 0.0)


def fill_mask(mask_ref, starts, blocks):
    for b in range(blocks):
        t = b * BLOCK + iota((BLOCK, BLOCK), 0)
        s = b * BLOCK + iota((BLOCK, BLOCK), 1)
        mask_ref[b] = jnp.where((s <= t) & (s >= starts[block_of(b)]), 0.0, FAR)


def assemble(w_refs, w_sc, at_ref, plan):
    for w_ref, (places, first_owner) in zip(w_refs, plan):
        for i, r in enumerate(places):
            for q in range(w_ref.shape[1]):
                w_sc[at_ref[0] ^ (first_owner + q), at_ref[1] ^ r] = w_ref[i, q]
    return w_sc[...].reshape(-1, w_sc.shape[-1])


def deal(value, keep_ref, send_ref, d_sc, at_ref):
    owners, places = d_sc.shape[:2]
    d_sc[...] = value.astype(bf16).reshape(d_sc.shape)
    for r in range(places):
        target = send_ref if r % 2 else keep_ref
        for q in range(owners):
            target[r // 2, q] = d_sc[at_ref[2] ^ q, at_ref[3] ^ r]


class Layout:
    def __init__(self, owners, places, rows):
        self.owners, self.places, self.rows = owners, places, rows

    def scratch(self, width):
        return pltpu.VMEM((self.owners, self.places, self.rows, width), bf16)

    def dealt(self, col):
        block = (max(self.places // 2, 1), self.owners, self.rows, TILE)
        return [pl.BlockSpec(block, lambda *s: (0, 0, 0, col(*s)))] * (1 if self.places == 1 else 2)

    def dealt_shape(self, rows, width):
        shape = (max(self.places // 2, 1), self.owners, rows, width)
        return [jax.ShapeDtypeStruct(shape, bf16)] * (1 if self.places == 1 else 2)


class Slots:
    def __init__(self, near, arrays, plan):
        self.near, self.arrays, self.plan = near, tuple(arrays), tuple(plan)

    def tiles(self, col):
        return [
            pl.BlockSpec((*a.shape[:3], TILE), lambda *s: (0, 0, 0, col(*s))) for a in self.arrays
        ]

    def whole(self, width, at):
        return [pl.BlockSpec((*a.shape[:3], width), lambda *s: (0, 0, 0, at)) for a in self.arrays]


SMEM = pl.BlockSpec(memory_space=pltpu.SMEM)


def first_kernel(
    plan, at_ref, rim_ref, normed_ref, *refs
):
    w_refs, rest = refs[: len(plan)], refs[len(plan) :]
    first_body(plan, at_ref, rim_ref, normed_ref, w_refs, *rest)


def first_body(
    plan, at_ref, rim_ref, normed_ref, w_refs, cw_ref, cb_ref, dtb_ref, rate_ref, starts_ref,
    cin_ref, cv_ref, dt_ref, lam_ref, sig_ref, lamt_ref, state_ref, fresh_ref, dec_ref, nrmt_ref,
    b_sc, e_sc, w_sc, nrm_ref,
):
    step = pl.program_id(0)
    length = starts_ref.shape[0]
    blocks = length // BLOCK
    heads = lamt_ref.shape[0] * PER
    starts = starts_ref[...]
    w = assemble(w_refs, w_sc, at_ref, plan)

    @pl.when(step == 0)
    def _():
        nrm_ref[:length] = normed_ref[...]
        nrm_ref[length:] = rim_ref[...]

    def conv():
        pe = dot(nrm_ref[...], w)
        cin_ref[...] = pe.astype(bf16)
        place = iota((length, 1), 0)
        taps = cw_ref.shape[0]
        acc = cb_ref[...] + cw_ref[taps - 1 : taps] * pe[:length]
        for k in range(taps - 1):
            back = taps - 1 - k
            keep = place - back >= starts
            acc = acc + jnp.where(keep, cw_ref[k : k + 1] * pltpu.roll(pe, back, 0)[:length], 0.0)
        cv = acc.astype(bf16)
        cv_ref[...] = cv
        return silu(cv.astype(f32))

    @pl.when(step == 0)
    def _():
        act = conv()
        b_sc[...] = act[:, :STATE].astype(bf16)
        nrmt_ref[...] = nrm_ref[...].T

    @pl.when(step == 1)
    def _():
        z = dot(nrm_ref[:length], w[:, :STATE]) + dtb_ref[...]
        live = iota(z.shape, 1) < heads
        dt = jnp.where(live, jnp.maximum(z, 0.0) + jnp.log1p(jnp.exp(-jnp.abs(z))), 0.0)
        dt_ref[...] = dt
        sig_ref[...] = jnp.where(live, 1.0 / (1.0 + jnp.exp(-z)), 0.0)
        change = dt * rate_ref[...]
        tri = lower(BLOCK).astype(f32)
        lam = jnp.concatenate(
            [dot(tri, change[block_of(b)], precision=PRECISE) for b in range(blocks)], axis=0
        )
        lam_ref[...] = lam
        across = lam.T
        for g in range(lamt_ref.shape[0]):
            lamt_ref[g] = across[PER * g : PER * (g + 1)]
        total = None
        rows = []
        for b in range(blocks):
            e_sc[block_of(b)] = split(end_weights(starts, lam, b) * dt[block_of(b)])
            last = (b + 1) * BLOCK - 1
            decay = jnp.where(
                starts[last : last + 1] < b * BLOCK, jnp.exp(lam[last : last + 1]), 0.0
            )
            decay = jnp.where(iota(decay.shape, 1) < heads, decay, 0.0)
            rows.append(decay)
            total = decay if total is None else total * decay
        rows.append(total)
        rows.append(jnp.zeros((8 - len(rows), STATE), f32))
        dec_ref[...] = jnp.concatenate(rows, axis=0)
        state_ref[:RIM] = decay_rows(total)

    @pl.when(step >= 2)
    def _():
        group = step - 2
        xe = (conv() * spread(e_sc[...], group)).astype(bf16)
        total = None
        for b in range(blocks):
            fresh = dot(xe[block_of(b)], b_sc[block_of(b)], 0, 0)
            if b + 1 < blocks:
                fresh_ref[b] = fresh
            if total is None:
                total = fresh
            else:
                total = head_rows(dec_ref[b : b + 1], group) * total + fresh
        state_ref[...] = total.astype(state_ref.dtype)


def first(layout, rim, normed, slots, rest_at, cw, cb, dtb, rate, starts, heads):
    d = normed.shape[1]
    length = starts.shape[0]
    ext = length + RIM
    blocks = length // BLOCK
    inner = heads * HEADDIM
    groups = inner // TILE
    col = lambda s: jnp.where(s == 0, groups, jnp.maximum(s - 2, 0))
    wcol = lambda s: rest_at + jnp.where(s < 2, groups + s, s - 2)
    tile = lambda s: jnp.maximum(s - 2, 0)
    full = lambda *shape: pl.BlockSpec(shape, lambda s: (0,) * len(shape))
    state = lambda s: jnp.where(s < 2, groups, s - 2)
    return pl.pallas_call(
        functools.partial(first_kernel, slots.plan),
        grid=(groups + 2,),
        in_specs=[
            SMEM,
            full(RIM, d),
            full(length, d),
            *slots.tiles(wcol),
            pl.BlockSpec((cw.shape[0], TILE), lambda s: (0, col(s))),
            pl.BlockSpec((1, TILE), lambda s: (0, col(s))),
            full(1, STATE),
            full(1, STATE),
            full(length, 1),
        ],
        out_specs=[
            pl.BlockSpec((ext, TILE), lambda s: (0, col(s))),
            pl.BlockSpec((length, TILE), lambda s: (0, col(s))),
            full(length, STATE),
            full(length, STATE),
            full(length, STATE),
            full(groups, PER, length),
            pl.BlockSpec((TILE, STATE), lambda s: (state(s), 0)),
            pl.BlockSpec((blocks - 1, TILE, STATE), lambda s: (0, tile(s), 0)),
            full(8, STATE),
            full(d, ext),
        ],
        out_shape=[
            jax.ShapeDtypeStruct((ext, inner + 2 * STATE), bf16),
            jax.ShapeDtypeStruct((length, inner + 2 * STATE), bf16),
            jax.ShapeDtypeStruct((length, STATE), f32),
            jax.ShapeDtypeStruct((length, STATE), f32),
            jax.ShapeDtypeStruct((length, STATE), f32),
            jax.ShapeDtypeStruct((groups, PER, length), f32),
            jax.ShapeDtypeStruct((inner + RIM, STATE), bf16),
            jax.ShapeDtypeStruct((blocks - 1, inner, STATE), f32),
            jax.ShapeDtypeStruct((8, STATE), f32),
            jax.ShapeDtypeStruct((d, ext), bf16),
        ],
        scratch_shapes=[
            pltpu.VMEM((length, STATE), bf16),
            pltpu.VMEM((length, 2 * STATE), bf16),
            layout.scratch(TILE),
            pltpu.VMEM((ext, d), bf16),
        ],
        compiler_params=pltpu.CompilerParams(vmem_limit_bytes=VMEM),
        cost_estimate=NO_COST,
        name="project",
    )(slots.near, rim, normed, *slots.arrays, cw, cb, dtb, rate, starts)


def pair_of(width):
    return iota((1, width), 1) < HEADDIM


def within_kernel(
    x_ref, bc_ref, dt_ref, lam_ref, lamt_ref, starts_ref, skip_ref,
    y_ref,
    cross_sc, mask_sc, dt_sc,
):
    group = pl.program_id(0)
    length = starts_ref.shape[0]
    blocks = length // BLOCK

    @pl.when(group == 0)
    def _():
        act = silu(bc_ref[...].astype(f32)).astype(bf16)
        for b in range(blocks):
            s = block_of(b)
            cross_sc[b] = dot(act[s, STATE:], act[s, :STATE], 1, 1)
        fill_mask(mask_sc, starts_ref[...], blocks)
        dt_sc[...] = split(dt_ref[...])

    x = silu(x_ref[...].astype(f32))
    xd = (x * spread(dt_sc[...], group)).astype(bf16)
    lam = pltpu.roll(lam_ref[...], lax.rem(STATE - PER * group, STATE), 1)
    lamt = lamt_ref[group]
    left = pair_of(2 * HEADDIM)
    for b in range(blocks):
        s = block_of(b)
        parts = []
        for p in range(PER // 2):
            c = slice(2 * HEADDIM * p, 2 * HEADDIM * (p + 1))
            two = []
            for h in (2 * p, 2 * p + 1):
                gap = (lam[s, h : h + 1] - lamt[h : h + 1, s]) + mask_sc[b]
                two.append(dot((jnp.exp(gap) * cross_sc[b]).astype(bf16), xd[s, c]))
            parts.append(jnp.where(left, two[0], two[1]))
        y = jnp.concatenate(parts, axis=1) + skip_ref[...] * x[s]
        y_ref[s] = y.astype(bf16)


def within(cv, dt, lam, lamt, starts, skip):
    length = starts.shape[0]
    blocks = length // BLOCK
    groups = lamt.shape[0]
    inner = groups * TILE
    full = lambda *shape: pl.BlockSpec(shape, lambda s: (0,) * len(shape))
    tile = pl.BlockSpec((length, TILE), lambda s: (0, s))
    return pl.pallas_call(
        within_kernel,
        grid=(groups,),
        in_specs=[
            tile,
            pl.BlockSpec((length, TILE), lambda s: (0, groups)),
            full(length, STATE),
            full(length, STATE),
            full(groups, PER, length),
            full(length, 1),
            pl.BlockSpec((1, TILE), lambda s: (0, s)),
        ],
        out_specs=tile,
        out_shape=jax.ShapeDtypeStruct((length, inner), bf16),
        scratch_shapes=[
            pltpu.VMEM((blocks, BLOCK, BLOCK), f32),
            pltpu.VMEM((blocks, BLOCK, BLOCK), f32),
            pltpu.VMEM((length, 2 * STATE), bf16),
        ],
        compiler_params=pltpu.CompilerParams(vmem_limit_bytes=VMEM),
        cost_estimate=NO_COST,
        name="within",
    )(cv, cv, dt, lam, lamt, starts, skip)


def states_of(s0, fresh_ref, dec_ref, group, blocks):
    found = [s0]
    for b in range(blocks - 1):
        found.append(head_rows(dec_ref[b : b + 1], group) * found[-1] + fresh_ref[b])
    return found


def unfold(wo_refs, wo_sc, at_ref, plan):
    rows, width = wo_sc.shape[-2:]
    short = wo_refs[0].shape[2]
    for wo_ref, (places, first_owner) in zip(wo_refs, plan):
        for i, r in enumerate(places):
            for q in range(wo_ref.shape[1]):
                for f in range(rows // short):
                    part = wo_ref[i, q, :, f * width : (f + 1) * width]
                    owner = at_ref[0] ^ (first_owner + q)
                    wo_sc[owner, at_ref[1] ^ r, f * short : (f + 1) * short] = part


def pieces_of(shape, group):
    share = shape[1] * shape[2]
    parts = share // TILE
    if parts == 1:
        return group, slice(None)
    many = TILE // shape[2]
    return group // parts, pl.ds(many * (group % parts), many)


def join_kernel(
    plan, at_ref, *refs
):
    many = len(plan)
    join_body(plan, at_ref, refs[:many], refs[many : 2 * many], *refs[2 * many :])


def join_body(
    plan, at_ref, w_refs, wo_refs, nrm_ref, y_ref, bc_ref, lam_ref, starts_ref, s0_ref, fresh_ref, dec_ref, gain_ref,
    resid_ref, gain_next_ref,
    gate_ref, y_out_ref, gated_ref, scale_ref, next_ref, low_ref, normed_ref,
    u_sc, c_sc, v_sc, sq_sc, wo_sc, w_sc,
):
    group = pl.program_id(0)
    length = starts_ref.shape[0]
    blocks = length // BLOCK
    groups = v_sc.shape[0]
    inner = groups * TILE

    @pl.when(group == 0)
    def _():
        c_sc[...] = silu(bc_ref[:, STATE:].astype(f32)).astype(bf16)
        for b in range(blocks):
            u_sc[block_of(b)] = split(reach_weights(starts_ref[...], lam_ref[...], b))
        sq_sc[...] = jnp.zeros_like(sq_sc)

    u = spread(u_sc[...], group)
    before = states_of(s0_ref[...].astype(f32), fresh_ref, dec_ref, group, blocks)
    carried = jnp.concatenate(
        [dot(c_sc[block_of(b)], before[b].astype(bf16), 1, 1) for b in range(blocks)], axis=0
    )
    y = (y_ref[...].astype(f32) + u * carried).astype(bf16)
    y_out_ref[...] = y
    gate = dot(nrm_ref[...], assemble(w_refs, w_sc, at_ref, plan)).astype(bf16)
    gate_ref[...] = gate
    v = y.astype(f32) * silu(gate.astype(f32))
    v_sc[group] = v
    sq = v * v
    sq_sc[...] += sq[:, :STATE] + sq[:, STATE:]

    @pl.when(group == groups - 1)
    def _():
        mean = jnp.sum(sq_sc[...], axis=1, keepdims=True) / inner
        scale = lax.rsqrt(mean + EPSILON)
        scale_ref[...] = scale
        acc = resid_ref[...].astype(f32)
        unfold(wo_refs, wo_sc, at_ref, plan)
        for g in range(groups):
            c = slice(g * TILE, (g + 1) * TILE)
            low = (v_sc[g] * scale * gain_ref[:, c]).astype(bf16)
            gated_ref[:, c] = low
            owner, piece = pieces_of(wo_sc.shape, g)
            acc = acc + dot(low, wo_sc[owner, piece].reshape(TILE, -1))
        next_ref[...] = acc
        low_ref[...] = acc.astype(bf16)
        norm = lax.rsqrt(jnp.mean(acc * acc, axis=1, keepdims=True) + EPSILON)
        normed_ref[...] = (acc * norm * gain_next_ref[...]).astype(bf16)


def join(layout, slots, gate_at, out_at, nrm, y, cv, lam, starts, s0, fresh, dec, gain, resid, gain_next):
    length, inner = y.shape
    d = resid.shape[1]
    fold = inner // d
    blocks = length // BLOCK
    groups = inner // TILE
    full = lambda *shape: pl.BlockSpec(shape, lambda s: (0,) * len(shape))
    tile = pl.BlockSpec((length, TILE), lambda s: (0, s))
    return pl.pallas_call(
        functools.partial(join_kernel, slots.plan),
        grid=(groups,),
        in_specs=[
            SMEM,
            *slots.tiles(lambda s: gate_at + s),
            *slots.whole(inner, out_at),
            full(length, d),
            tile,
            pl.BlockSpec((length, TILE), lambda s: (0, groups)),
            full(length, STATE),
            full(length, 1),
            pl.BlockSpec((TILE, STATE), lambda s: (s, 0)),
            pl.BlockSpec((blocks - 1, TILE, STATE), lambda s: (0, s, 0)),
            full(8, STATE),
            full(1, inner),
            full(length, d),
            full(1, d),
        ],
        out_specs=[
            tile,
            tile,
            full(length, inner),
            full(length, 1),
            full(length, d),
            full(length, d),
            full(length, d),
        ],
        out_shape=[
            jax.ShapeDtypeStruct((length, inner), bf16),
            jax.ShapeDtypeStruct((length, inner), bf16),
            jax.ShapeDtypeStruct((length, inner), bf16),
            jax.ShapeDtypeStruct((length, 1), f32),
            jax.ShapeDtypeStruct((length, d), f32),
            jax.ShapeDtypeStruct((length, d), bf16),
            jax.ShapeDtypeStruct((length, d), bf16),
        ],
        scratch_shapes=[
            pltpu.VMEM((length, 2 * STATE), bf16),
            pltpu.VMEM((length, STATE), bf16),
            pltpu.VMEM((groups, length, TILE), f32),
            pltpu.VMEM((length, STATE), f32),
            pltpu.VMEM((layout.owners, layout.places, fold * layout.rows, d), bf16),
            layout.scratch(TILE),
        ],
        compiler_params=pltpu.CompilerParams(vmem_limit_bytes=VMEM),
        cost_estimate=NO_COST,
        name="join",
    )(
        slots.near, *slots.arrays, *slots.arrays, nrm, y, cv, lam, starts, s0, fresh, dec, gain, resid,
        gain_next,
    )


def gate_back_kernel(
    plan, skip, at_ref, *refs
):
    refs = refs[skip:]
    wo_refs, rest = refs[: len(plan)], refs[len(plan) :]
    gate_back_body(plan, at_ref, wo_refs, *rest)


def gate_back_body(
    plan, at_ref, wo_refs, grad_ref, y_ref, gate_ref, gated_ref, scale_ref, gain_ref, x_ref, bc_ref, lam_ref,
    starts_ref, dec_ref,
    gy_ref, ggate_ref, ggain_ref, gskip_ref, later_ref, total_ref, *more
):
    gg_sc, u_sc, c_sc, dot_sc, wo_sc, dwo_sc = more[-6:]
    keep_ref, send_ref = more[0], more[-7]
    phase, group = pl.program_id(0), pl.program_id(1)
    length = starts_ref.shape[0]
    blocks = length // BLOCK
    groups = gg_sc.shape[0]
    inner = groups * TILE

    @pl.when((phase == 0) & (group == 0))
    def _():
        c_sc[...] = silu(bc_ref[:, STATE:].astype(f32)).astype(bf16)
        for b in range(blocks):
            u_sc[block_of(b)] = split(reach_weights(starts_ref[...], lam_ref[...], b))
        dot_sc[...] = jnp.zeros_like(dot_sc)
        unfold(wo_refs, wo_sc, at_ref, plan)

    y = y_ref[...].astype(f32)
    gate = gate_ref[...].astype(f32)
    sig = logistic(gate)
    act = gate * sig
    v = y * act
    scale = scale_ref[...]

    @pl.when(phase == 0)
    def _():
        owners, places, rows, width = wo_sc.shape
        owner, piece = pieces_of(wo_sc.shape, group)
        gg = dot(grad_ref[...], wo_sc[owner, piece].reshape(TILE, width), 1, 1)
        gv = gg * v
        ggain_ref[...] = jnp.sum(gv * scale, axis=0, keepdims=True)
        total_ref[:RIM] = decay_rows(dec_ref[blocks : blocks + 1])
        gv = gv * gain_ref[...]
        dot_sc[...] += gv[:, :STATE] + gv[:, STATE:]
        gg_sc[group] = gg * gain_ref[...]
        dwo = dot(gated_ref[...], grad_ref[...], 0, 0).astype(bf16)
        dwo_sc[owner, piece] = dwo.reshape(-1, rows, width)

        @pl.when(group == groups - 1)
        def _():
            for r in range(places):
                target = send_ref if r % 2 else keep_ref
                for q in range(owners):
                    target[r // 2, q] = dwo_sc[at_ref[2] ^ q, at_ref[3] ^ r]

    @pl.when(phase == 1)
    def _():
        @pl.when(group == 0)
        def _():
            total = jnp.sum(dot_sc[...], axis=1, keepdims=True)
            dot_sc[...] = jnp.broadcast_to(
                total * scale * scale * scale * (1.0 / inner), dot_sc.shape
            )

        gv = scale * gg_sc[group] - v * dot_sc[:, :1]
        gy = gv * act
        ggate_ref[...] = (gv * y * (sig + act * (1.0 - sig))).astype(bf16)
        low = gy.astype(bf16)
        gy_ref[...] = low
        x = silu(x_ref[...].astype(f32))
        skip = jnp.sum(low.astype(f32) * x, axis=0, keepdims=True)
        skip = gather_heads(jnp.broadcast_to(skip, (8, TILE)), group)[:1]

        @pl.when(group == 0)
        def _():
            gskip_ref[...] = jnp.zeros_like(gskip_ref)

        gskip_ref[...] += skip
        ug = (gy * spread(u_sc[...], group)).astype(bf16)
        total = None
        for b in reversed(range(blocks)):
            direct = dot(ug[block_of(b)], c_sc[block_of(b)], 0, 0)
            if total is None:
                total = direct
            else:
                total = head_rows(dec_ref[b : b + 1], group) * total + direct
            if b > 0:
                later_ref[b - 1] = direct
        total_ref[...] = total.astype(total_ref.dtype)


def gate_back(after, at, layout, slots, out_at, grad_low, y, gate, gated, scale, gain, cv, lam, starts, dec):
    length, inner = y.shape
    d = grad_low.shape[1]
    rows = inner // d * layout.rows
    blocks = length // BLOCK
    groups = inner // TILE
    full = lambda *shape: pl.BlockSpec(shape, lambda p, s: (0,) * len(shape))
    early = lambda p, s: jnp.where(p == 0, s, groups - 1)
    late = lambda p, s: s * p
    tile = pl.BlockSpec((length, TILE), lambda p, s: (0, s))
    late_tile = pl.BlockSpec((length, TILE), lambda p, s: (0, late(p, s)))
    return pl.pallas_call(
        functools.partial(gate_back_kernel, slots.plan, len(after)),
        grid=(2, groups),
        in_specs=[
            SMEM,
            *[pl.BlockSpec(memory_space=pl.ANY)] * len(after),
            *slots.whole(inner, out_at),
            full(length, d),
            tile,
            tile,
            pl.BlockSpec((length, TILE), lambda p, s: (0, early(p, s))),
            full(length, 1),
            pl.BlockSpec((1, TILE), lambda p, s: (0, s)),
            late_tile,
            pl.BlockSpec((length, TILE), lambda p, s: (0, groups)),
            full(length, STATE),
            full(length, 1),
            full(8, STATE),
        ],
        out_specs=[
            late_tile,
            late_tile,
            pl.BlockSpec((1, TILE), lambda p, s: (0, early(p, s))),
            full(1, STATE),
            pl.BlockSpec((blocks - 1, TILE, STATE), lambda p, s: (0, late(p, s), 0)),
            pl.BlockSpec((TILE, STATE), lambda p, s: (jnp.where(p == 0, groups, s), 0)),
            *[full(*a.shape) for a in layout.dealt_shape(rows, d)],
        ],
        out_shape=[
            jax.ShapeDtypeStruct((length, inner), bf16),
            jax.ShapeDtypeStruct((length, inner), bf16),
            jax.ShapeDtypeStruct((1, inner), f32),
            jax.ShapeDtypeStruct((1, STATE), f32),
            jax.ShapeDtypeStruct((blocks - 1, inner, STATE), f32),
            jax.ShapeDtypeStruct((inner + RIM, STATE), bf16),
            *layout.dealt_shape(rows, d),
        ],
        scratch_shapes=[
            pltpu.VMEM((groups, length, TILE), f32),
            pltpu.VMEM((length, 2 * STATE), bf16),
            pltpu.VMEM((length, STATE), bf16),
            pltpu.VMEM((length, STATE), f32),
            pltpu.VMEM((layout.owners, layout.places, rows, d), bf16),
            pltpu.VMEM((layout.owners, layout.places, rows, d), bf16),
        ],
        compiler_params=pltpu.CompilerParams(vmem_limit_bytes=VMEM),
        cost_estimate=NO_COST,
        name="gate_back",
    )(jnp.concatenate([slots.near, at]), *after, *slots.arrays, grad_low, y, gate, gated, scale, gain, cv, cv, lam, starts, dec)


def within_back_kernel(
    plan, skip, at_ref, *refs
):
    refs = refs[skip:]
    w_refs, rest = refs[: len(plan)], refs[len(plan) :]
    within_back_body(plan, at_ref, w_refs, *rest)


def within_back_body(
    plan, at_ref, w_refs, gy_ref, x_ref, bc_ref, dt_ref, lam_ref, lamt_ref, starts_ref, s0_ref, fresh_ref, dec_ref,
    ggate_ref, nrmt_ref,
    gxd_ref, glam_ref, gbc_ref, gnrm_ref, *more
):
    cross_sc, gcross_sc, mask_sc, dt_sc, u_sc, act_sc, w_sc, d_sc = more[-8:]
    keep_ref, send_ref = more[0], more[-9]
    group = pl.program_id(0)
    length = starts_ref.shape[0]
    blocks = length // BLOCK
    groups = lamt_ref.shape[0]

    @pl.when(group == 0)
    def _():
        act = silu(bc_ref[...].astype(f32)).astype(bf16)
        act_sc[...] = act
        for b in range(blocks):
            s = block_of(b)
            cross_sc[b] = dot(act[s, STATE:], act[s, :STATE], 1, 1)
            u_sc[s] = split(reach_weights(starts_ref[...], lam_ref[...], b))
        fill_mask(mask_sc, starts_ref[...], blocks)
        dt_sc[...] = split(dt_ref[...])
        gcross_sc[...] = jnp.zeros_like(gcross_sc)
        glam_ref[...] = jnp.zeros_like(glam_ref)
        gbc_ref[...] = jnp.zeros_like(gbc_ref)
        gnrm_ref[...] = jnp.zeros_like(gnrm_ref)

    ggate = ggate_ref[...]
    gnrm_ref[...] += dot(ggate, assemble(w_refs, w_sc, at_ref, plan), 1, 1)
    deal(dot(nrmt_ref[:, :length], ggate), keep_ref, send_ref, d_sc, at_ref)

    x = silu(x_ref[...].astype(f32))
    xd = (x * spread(dt_sc[...], group)).astype(bf16)
    gy = gy_ref[...]
    u = spread(u_sc[...], group)
    before = states_of(s0_ref[...].astype(f32), fresh_ref, dec_ref, group, blocks)
    lam = pltpu.roll(lam_ref[...], lax.rem(STATE - PER * group, STATE), 1)
    lamt = lamt_ref[group]
    left = pair_of(2 * HEADDIM)
    for b in range(blocks):
        s = block_of(b)
        gcross = gcross_sc[b]
        ys, gxds = [], []
        for p in range(PER // 2):
            c = slice(2 * HEADDIM * p, 2 * HEADDIM * (p + 1))
            y2, g2 = [], []
            for h in (2 * p, 2 * p + 1):
                decay = jnp.exp((lam[s, h : h + 1] - lamt[h : h + 1, s]) + mask_sc[b])
                weight = (decay * cross_sc[b]).astype(bf16)
                y2.append(dot(weight, xd[s, c]))
                g2.append(dot(weight, gy[s, c], 0, 0))
                own = left if h % 2 == 0 else ~left
                mine = jnp.where(own, gy[s, c], jnp.zeros((), bf16))
                gcross = gcross + dot(mine, xd[s, c], 1, 1) * decay
            ys.append(jnp.where(left, y2[0], y2[1]))
            gxds.append(jnp.where(left, g2[0], g2[1]))
        gcross_sc[b] = gcross
        state = before[b].astype(bf16)
        y = jnp.concatenate(ys, axis=1) + u[s] * dot(act_sc[s, STATE:], state, 1, 1)
        gxd = jnp.concatenate(gxds, axis=1)
        gxd_ref[s] = gxd
        gyf = gy[s].astype(f32)
        glam_ref[s] += gather_heads(gyf * y - xd[s].astype(f32) * gxd, group)
        gbc_ref[s, STATE:] += dot((u[s] * gyf).astype(bf16), state)

    @pl.when(group == groups - 1)
    def _():
        for b in range(blocks):
            s = block_of(b)
            low = gcross_sc[b].astype(bf16)
            gbc_ref[s, :STATE] += dot(low, act_sc[s, STATE:], 0, 0)
            gbc_ref[s, STATE:] += dot(low, act_sc[s, :STATE])


def within_back(after, at, layout, slots, gate_at, gy, cv, dt, lam, lamt, starts, s0, fresh, dec, ggate, nrmt):
    length, inner = gy.shape
    d, ext = nrmt.shape
    blocks = length // BLOCK
    groups = inner // TILE
    full = lambda *shape: pl.BlockSpec(shape, lambda s: (0,) * len(shape))
    tile = pl.BlockSpec((length, TILE), lambda s: (0, s))
    return pl.pallas_call(
        functools.partial(within_back_kernel, slots.plan, len(after)),
        grid=(groups,),
        in_specs=[
            SMEM,
            *[pl.BlockSpec(memory_space=pl.ANY)] * len(after),
            *slots.tiles(lambda s: gate_at + s),
            tile,
            tile,
            pl.BlockSpec((length, TILE), lambda s: (0, groups)),
            full(length, STATE),
            full(length, STATE),
            full(groups, PER, length),
            full(length, 1),
            pl.BlockSpec((TILE, STATE), lambda s: (s, 0)),
            pl.BlockSpec((blocks - 1, TILE, STATE), lambda s: (0, s, 0)),
            full(8, STATE),
            tile,
            full(d, ext),
        ],
        out_specs=[
            tile, full(length, STATE), full(length, 2 * STATE), full(length, d),
            *layout.dealt(lambda s: s),
        ],
        out_shape=[
            jax.ShapeDtypeStruct((length, inner), f32),
            jax.ShapeDtypeStruct((length, STATE), f32),
            jax.ShapeDtypeStruct((length, 2 * STATE), f32),
            jax.ShapeDtypeStruct((length, d), f32),
            *layout.dealt_shape(layout.rows, inner),
        ],
        scratch_shapes=[
            pltpu.VMEM((blocks, BLOCK, BLOCK), f32),
            pltpu.VMEM((blocks, BLOCK, BLOCK), f32),
            pltpu.VMEM((blocks, BLOCK, BLOCK), f32),
            pltpu.VMEM((length, 2 * STATE), bf16),
            pltpu.VMEM((length, 2 * STATE), bf16),
            pltpu.VMEM((length, 2 * STATE), bf16),
            layout.scratch(TILE),
            layout.scratch(TILE),
        ],
        compiler_params=pltpu.CompilerParams(vmem_limit_bytes=VMEM),
        cost_estimate=NO_COST,
        name="within_back",
    )(jnp.concatenate([slots.near, at]), *after, *slots.arrays, gy, cv, cv, dt, lam, lamt, starts, s0, fresh, dec, ggate, nrmt)


def last_kernel(
    plan, skip, at_ref, *refs
):
    refs = refs[skip:]
    w_refs, rest = refs[: len(plan)], refs[len(plan) :]
    last_body(plan, at_ref, w_refs, *rest)


def last_body(
    plan, at_ref, w_refs, gxd_ref, cv_ref, cin_ref, gy_ref, bc_ref, dt_ref, lam_ref, sig_ref, starts_ref, gend_ref,
    later_ref, s0_ref, fresh_ref, dec_ref, nrmt_ref, glam_ref, gbc_ref, gin_ref, skip_ref,
    rate_ref, cw_ref, rim_ref, nrm_ref, gain_ref,
    edge_ref, out_ref, gcw_ref, gcb_ref, gsmall_ref, ngain_ref, *more
):
    b_sc, gb_sc, dt_sc, e_sc, gdt_sc, zs_sc, over_sc, gp_sc, w_sc, d_sc, gnrm_ref = more[-11:]
    keep_ref, send_ref = more[0], more[-12]
    step = pl.program_id(0)
    length = starts_ref.shape[0]
    blocks = length // BLOCK
    groups = pl.num_programs(0) - 2
    starts = starts_ref[...]
    ext = gnrm_ref.shape[0]

    @pl.when(step == 0)
    def _():
        b_sc[...] = silu(bc_ref[:, :STATE].astype(f32)).astype(bf16)
        gb_sc[...] = gbc_ref[:, :STATE]
        dt_sc[...] = split(dt_ref[...])
        for b in range(blocks):
            e_sc[block_of(b)] = split(end_weights(starts, lam_ref[...], b))
        gdt_sc[...] = jnp.zeros_like(gdt_sc)
        zs_sc[...] = jnp.zeros_like(zs_sc)
        over_sc[...] = jnp.zeros_like(over_sc)
        gnrm_ref[length:] = jnp.zeros((RIM, gnrm_ref.shape[1]), f32)
        gnrm_ref[:length] = gin_ref[...]

    def conv_back(gact):
        gcv = gact * dsilu(cv_ref[...].astype(f32))
        gcb_ref[...] = jnp.sum(gcv, axis=0, keepdims=True)
        place = iota((length, 1), 0)
        taps = cw_ref.shape[0]
        cin = cin_ref[...].astype(f32)
        zeros = jnp.zeros((RIM, TILE), f32)
        acc = None
        rows = []
        for k in range(taps):
            back = taps - 1 - k
            term = gcv if back == 0 else jnp.where(place - back >= starts, gcv, 0.0)
            moved = jnp.concatenate([term, zeros], axis=0)
            if back:
                moved = pltpu.roll(moved, ext - back, 0)
            rows.append(jnp.sum(moved * cin, axis=0, keepdims=True))
            part = cw_ref[k : k + 1] * moved
            acc = part if acc is None else acc + part
        gcw_ref[...] = jnp.concatenate(rows, axis=0)
        gp_sc[...] = acc.astype(bf16)

    @pl.when(step < groups)
    def _():
        group = step
        x = silu(cv_ref[...].astype(f32))
        dt = spread(dt_sc[...], group)
        e = spread(e_sc[...], group)
        xd = x * dt
        gend = gend_ref[...].astype(f32)
        grads = [None] * blocks
        for b in reversed(range(blocks)):
            grads[b] = gend
            if b > 0:
                gend = head_rows(dec_ref[b : b + 1], group) * gend + later_ref[b - 1]
        before = states_of(s0_ref[...].astype(f32), fresh_ref, dec_ref, group, blocks)
        parts = []
        for b in range(blocks):
            s = block_of(b)
            low = grads[b].astype(bf16)
            parts.append(e[s] * dot(b_sc[s], low, 1, 1))
            gb_sc[s] += dot((e[s] * xd[s]).astype(bf16), low)
            over = jnp.sum(grads[b] * before[b], axis=1, keepdims=True)
            over_sc[b : b + 1] += dec_ref[b : b + 1] * jnp.sum(
                jnp.where(chooser(group), over, 0.0), axis=0, keepdims=True
            )
        more = jnp.concatenate(parts, axis=0)
        gxd = gxd_ref[...] + more
        zs_sc[...] += gather_heads(xd * more, group)
        gdt_sc[...] += gather_heads(x * gxd, group)
        conv_back(dt * gxd + skip_ref[...] * gy_ref[...].astype(f32))

    @pl.when(step == groups)
    def _():
        conv_back(jnp.concatenate([gb_sc[...], gbc_ref[:, STATE:]], axis=1))

    @pl.when(step <= groups)
    def _():
        gp = gp_sc[...]
        gnrm_ref[...] += dot(gp, assemble(w_refs, w_sc, at_ref, plan), 1, 1)
        deal(dot(nrmt_ref[...], gp), keep_ref, send_ref, d_sc, at_ref)

    @pl.when(step == groups + 1)
    def _():
        tri = lower(BLOCK).astype(f32)
        glam = glam_ref[...] - zs_sc[...]
        rows = []
        for b in range(blocks):
            s = block_of(b)
            end = jnp.sum(zs_sc[s], axis=0, keepdims=True) + over_sc[b : b + 1]
            rows.append(dot(tri, glam[s], 0, 0, precision=PRECISE) + end)
        back = jnp.concatenate(rows, axis=0)
        dt = dt_ref[...]
        gz = (gdt_sc[...] + rate_ref[...] * back) * sig_ref[...]
        gsmall_ref[0:1] = jnp.sum(gz, axis=0, keepdims=True)
        gsmall_ref[1:2] = rate_ref[...] * jnp.sum(dt * back, axis=0, keepdims=True)
        gsmall_ref[2:8] = jnp.zeros((6, STATE), f32)
        low = gz.astype(bf16)
        heads = groups * PER
        w = assemble(w_refs, w_sc, at_ref, plan)[:, :STATE]
        w = jnp.where(iota(w.shape, 1) < heads, w, jnp.zeros((), bf16))
        gnrm_ref[:length] += dot(low, w, 1, 1)
        dw = dot(nrmt_ref[:, :length], low)
        deal(jnp.concatenate([dw, jnp.zeros_like(dw)], axis=1), keep_ref, send_ref, d_sc, at_ref)
        gnrm = gnrm_ref[...]
        edge_ref[...] = gnrm[length:]
        out_ref[...] = gnrm[:length]
        ngain = jnp.sum(gnrm[length:] * rim_ref[...].astype(f32), axis=0, keepdims=True)
        ngain = ngain + jnp.sum(gnrm[:length] * nrm_ref[...].astype(f32), axis=0, keepdims=True)
        ngain_ref[...] = ngain / gain_ref[...]


def last(
    after, at, layout, slots, rest_at, gxd, cv, cin, gy, dt, lam, sig, starts, gend, later, s0, fresh, dec, nrmt, glam, gbc,
    gin, skip, rate, cw, rim, nrm, gain,
):
    length, inner = gy.shape
    d, ext = nrmt.shape
    blocks = length // BLOCK
    groups = inner // TILE
    heads = inner // HEADDIM
    taps = cw.shape[0]
    full = lambda *shape: pl.BlockSpec(shape, lambda s: (0,) * len(shape))
    own = lambda s: jnp.minimum(s, groups - 1)
    col = lambda s: jnp.minimum(s, groups)
    tile = pl.BlockSpec((length, TILE), lambda s: (0, own(s)))
    state = pl.BlockSpec((TILE, STATE), lambda s: (own(s), 0))
    states = pl.BlockSpec((blocks - 1, TILE, STATE), lambda s: (0, own(s), 0))
    return pl.pallas_call(
        functools.partial(last_kernel, slots.plan, len(after)),
        grid=(groups + 2,),
        in_specs=[
            SMEM,
            *[pl.BlockSpec(memory_space=pl.ANY)] * len(after),
            *slots.tiles(lambda s: rest_at + s),
            tile,
            pl.BlockSpec((length, TILE), lambda s: (0, col(s))),
            pl.BlockSpec((ext, TILE), lambda s: (0, col(s))),
            tile,
            pl.BlockSpec((length, TILE), lambda s: (0, groups)),
            full(length, STATE),
            full(length, STATE),
            full(length, STATE),
            full(length, 1),
            state,
            states,
            state,
            states,
            full(8, STATE),
            full(d, ext),
            full(length, STATE),
            full(length, 2 * STATE),
            full(length, d),
            pl.BlockSpec((1, TILE), lambda s: (0, own(s))),
            full(1, STATE),
            pl.BlockSpec((taps, TILE), lambda s: (0, col(s))),
            full(RIM, d),
            full(length, d),
            full(1, d),
        ],
        out_specs=[
            full(RIM, d),
            full(length, d),
            pl.BlockSpec((taps, TILE), lambda s: (0, col(s))),
            pl.BlockSpec((1, TILE), lambda s: (0, col(s))),
            full(8, STATE),
            full(1, d),
            *layout.dealt(lambda s: s),
        ],
        out_shape=[
            jax.ShapeDtypeStruct((RIM, d), f32),
            jax.ShapeDtypeStruct((length, d), f32),
            jax.ShapeDtypeStruct((taps, inner + 2 * STATE), f32),
            jax.ShapeDtypeStruct((1, inner + 2 * STATE), f32),
            jax.ShapeDtypeStruct((8, STATE), f32),
            jax.ShapeDtypeStruct((1, d), f32),
            *layout.dealt_shape(layout.rows, inner + 2 * STATE + heads),
        ],
        scratch_shapes=[
            pltpu.VMEM((length, STATE), bf16),
            pltpu.VMEM((length, STATE), f32),
            pltpu.VMEM((length, 2 * STATE), bf16),
            pltpu.VMEM((length, 2 * STATE), bf16),
            pltpu.VMEM((length, STATE), f32),
            pltpu.VMEM((length, STATE), f32),
            pltpu.VMEM((8, STATE), f32),
            pltpu.VMEM((ext, TILE), bf16),
            layout.scratch(TILE),
            layout.scratch(TILE),
            pltpu.VMEM((ext, d), f32),
        ],
        compiler_params=pltpu.CompilerParams(vmem_limit_bytes=VMEM),
        cost_estimate=NO_COST,
        name="last",
    )(
        jnp.concatenate([slots.near, at]), *after, *slots.arrays, gxd, cv, cin, gy, cv, dt, lam, sig, starts, gend, later, s0, fresh, dec, nrmt,
        glam, gbc, gin, skip, rate, cw, rim, nrm, gain,
    )


def norm_back_kernel(grad_ref, gnrm_ref, rim_ref, resid_ref, gain_ref, *refs):
    out_ref, low_ref = refs[-2:]
    rows, width = out_ref.shape
    gnrm = gnrm_ref[...]
    last = pl.program_id(0) == pl.num_programs(0) - 1
    more = jnp.where(last, rim_ref[...], 0.0)
    gnrm = jnp.concatenate([gnrm[: rows - RIM], gnrm[rows - RIM :] + more], axis=0)
    resid = resid_ref[...].astype(f32)
    scale = lax.rsqrt(jnp.mean(resid * resid, axis=1, keepdims=True) + EPSILON)
    scaled = gnrm * gain_ref[...]
    inner = jnp.sum(scaled * resid, axis=1, keepdims=True)
    total = grad_ref[...].astype(f32) + scale * scaled - resid * (inner * scale * scale * scale / width)
    out_ref[...] = total
    low_ref[...] = total.astype(bf16)


def norm_back(grad, gnrm, rim, resid, gain, after=()):
    length, width = grad.shape
    rows = 128
    block = pl.BlockSpec((rows, width), lambda s: (s, 0))
    fixed = lambda n: pl.BlockSpec((n, width), lambda s: (0, 0))
    return pl.pallas_call(
        norm_back_kernel,
        grid=(length // rows,),
        in_specs=[block, block, fixed(RIM), block, fixed(1)]
        + [pl.BlockSpec(memory_space=pl.ANY)] * len(after),
        out_specs=[block, block],
        out_shape=[
            jax.ShapeDtypeStruct((length, width), f32),
            jax.ShapeDtypeStruct((length, width), bf16),
        ],
        compiler_params=pltpu.CompilerParams(vmem_limit_bytes=VMEM),
        cost_estimate=NO_COST,
        name="norm_back",
    )(grad, gnrm, rim, resid, gain, *after)


def passed_along(shard, axis, by):
    devices = lax.axis_size(axis)
    pairs = [(i, i + by) for i in range(devices) if 0 <= i + by < devices]
    return lax.ppermute(shard, axis, pairs)


def swap(value, axis, by):
    return lax.ppermute(value, axis, [(i, i ^ by) for i in range(lax.axis_size(axis))])


def decay_of(ref, at):
    return ref[at : at + 1].astype(f32) + ref[at + 1 : at + 2].astype(f32)


def joint_kernel(reverse, at_ref, mine_ref, other_ref, *refs):
    sent_ref = refs[-1]
    half = sent_ref.shape[0] - RIM
    odd = at_ref[1] % 2
    mine, other = decay_of(mine_ref, 2 * half), decay_of(other_ref, 2 * half)
    by = jnp.where((odd == 1) == reverse, other, mine)
    for g in range(half // TILE):
        rows = pl.ds(pl.multiple_of(odd * half + g * TILE, TILE), TILE)
        here, there = mine_ref[rows].astype(f32), other_ref[rows].astype(f32)
        first = jnp.where((odd == 1) == reverse, here, there)
        second = jnp.where((odd == 1) == reverse, there, here)
        scale = head_rows(by, odd * (half // TILE) + g)
        sent_ref[g * TILE : (g + 1) * TILE] = (scale * first + second).astype(bf16)
    sent_ref[half:] = decay_rows(mine * other)


def entering_kernel(reverse, pairs, at_ref, *refs):
    got, out_ref = refs[: pairs - 1], refs[-1]
    half = out_ref.shape[0]
    odd, chip = at_ref[1] % 2, at_ref[1] // 2
    decays = [decay_of(a, half) for a in got]
    shares = []
    for i in range(1, pairs):
        source = chip ^ i
        counts = source > chip if reverse else source < chip
        share = jnp.where(counts, jnp.ones((1, STATE), f32), 0.0)
        for j in range(1, pairs):
            if j != i:
                by = chip ^ j
                inside = (by < source) & (by > chip) if reverse else (by > source) & (by < chip)
                share = jnp.where(inside, share * decays[j - 1], share)
        shares.append(share)
    for g in range(half // TILE):
        rows = slice(g * TILE, (g + 1) * TILE)
        total = None
        for share, a in zip(shares, got):
            part = head_rows(share, odd * (half // TILE) + g) * a[rows].astype(f32)
            total = part if total is None else total + part
        out_ref[rows] = total.astype(bf16)


def behind_kernel(reverse, at_ref, half_ref, rest_ref, other_ref, out_ref):
    half = half_ref.shape[0]
    odd = at_ref[1] % 2
    decay = decay_of(other_ref, 2 * half)
    for g in range(2 * half // TILE):
        rows = slice(g * TILE, (g + 1) * TILE)
        upper = g * TILE >= half
        short = slice(rows.start % half, rows.start % half + TILE)
        own = (odd == 1) == upper
        value = jnp.where(own, half_ref[short].astype(f32), rest_ref[short].astype(f32))
        later = head_rows(decay, g) * value + other_ref[rows].astype(f32)
        out_ref[rows] = jnp.where((odd == 1) != reverse, later, value)


def small_call(kernel, at, args, shapes, after=(), name=None):
    args = list(args) + list(after)
    count = len(args) - len(after)
    vmem = pl.BlockSpec(memory_space=pltpu.VMEM)
    return pl.pallas_call(
        kernel,
        in_specs=[SMEM] + [vmem] * count + [pl.BlockSpec(memory_space=pl.ANY)] * len(after),
        out_specs=[vmem] * len(shapes),
        out_shape=shapes,
        compiler_params=pltpu.CompilerParams(vmem_limit_bytes=VMEM),
        cost_estimate=NO_COST,
        name=name,
    )(at, *args)


def carried_over(here, state, reverse, meanwhile):
    pairs = lax.axis_size("seq") // 2
    rows = state.shape[0] - RIM
    other = swap(state, "seq", 1)
    sent_shape = jax.ShapeDtypeStruct((rows // 2 + RIM, STATE), bf16)
    (sent,) = small_call(
        functools.partial(joint_kernel, reverse), here, [state, other], [sent_shape], name="joint"
    )
    got = [swap(sent, "seq", 2 * i) for i in range(1, pairs)]
    beside = meanwhile(sent)
    half_shape = jax.ShapeDtypeStruct((rows // 2, STATE), bf16)
    (half,) = small_call(
        functools.partial(entering_kernel, reverse, pairs), here, got, [half_shape],
        after=[beside[0]], name="entering",
    )
    rest = swap(half, "seq", 1)
    (whole,) = small_call(
        functools.partial(behind_kernel, reverse), here, [half, rest, other],
        [jax.ShapeDtypeStruct((rows, STATE), f32)], name="behind",
    )
    return whole, beside, half


def cut_kernel(inner, at_ref, in_ref, out_ref, rest_ref, *targets):
    rows, share, width = rest_ref.shape[0], in_ref.shape[2], out_ref.shape[2]
    for layer, target in enumerate(targets):

        @pl.when(pl.program_id(0) == layer)
        def _():
            pick = iota((rows, share), 1) == rows * at_ref[1] + iota((rows, share), 0)
            pick = pick.astype(f32).astype(bf16)
            rest = dot(pick, in_ref[0, inner:], 1, 1).astype(bf16)
            if layer == 0:
                rest_ref[...] = rest
            else:
                target[:, 2 * inner :] = rest
            target[:, :inner] = dot(pick, in_ref[0, :inner], 1, 1).astype(bf16)
            for f in range(inner // width):
                part = out_ref[0, f * rows : (f + 1) * rows]
                target[:, inner + f * width : inner + (f + 1) * width] = part


def cut(at, layout, in_turned, out_weight):
    layers, wide, share = in_turned.shape
    width = out_weight.shape[2]
    rows = layout.rows
    fold = out_weight.shape[1] // share
    inner = fold * width
    shapes = [
        jax.ShapeDtypeStruct((rows, n), bf16)
        for n in (wide - inner, 2 * inner, *[wide + inner] * (layers - 1))
    ]
    return pl.pallas_call(
        functools.partial(cut_kernel, inner),
        grid_spec=pltpu.PrefetchScalarGridSpec(
            num_scalar_prefetch=1,
            grid=(layers,),
            in_specs=[
                pl.BlockSpec((1, wide, share), lambda s, at_ref: (s, 0, 0)),
                pl.BlockSpec((1, fold * rows, width), lambda s, at_ref: (s, at_ref[1], 0)),
            ],
            out_specs=[pl.BlockSpec(a.shape, lambda s, at_ref: (0, 0)) for a in shapes],
        ),
        out_shape=shapes,
        compiler_params=pltpu.CompilerParams(vmem_limit_bytes=VMEM),
        cost_estimate=NO_COST,
        name="cut",
    )(at, in_turned, out_weight)


X, Y = 2, 4


def over_wa(piece, layout):
    return [piece] + [swap(piece, "wa", q) for q in range(1, layout.owners)]


def stack_kernel(count, *refs):
    for i in range(count):
        refs[-1][0, i] = refs[i][...]


def stack(pieces, after=()):
    vmem = pl.BlockSpec(memory_space=pltpu.VMEM)
    return pl.pallas_call(
        functools.partial(stack_kernel, len(pieces)),
        in_specs=[vmem] * len(pieces) + [pl.BlockSpec(memory_space=pl.ANY)] * len(after),
        out_specs=vmem,
        out_shape=jax.ShapeDtypeStruct((1, len(pieces), *pieces[0].shape), pieces[0].dtype),
        compiler_params=pltpu.CompilerParams(vmem_limit_bytes=VMEM),
        cost_estimate=NO_COST,
        name="stack",
    )(*pieces, *after)


def straight(here, pieces, after=()):
    return across(here, stack(pieces, after))


def across(near, own):
    arrays = [own] + [swap(own, "seq", by) for by in (X, Y, X + Y)]
    return Slots(near, arrays, [((r,), 0) for r in (0, X, Y, X + Y)])


def near_by(slots, after=()):
    arrays = [tie(a, after) if after else a for a in slots.arrays]
    return Slots(
        slots.near, arrays + [swap(a, "seq", 1) for a in arrays],
        slots.plan + tuple((tuple(r + 1 for r in places), owner) for places, owner in slots.plan),
    )


def like_cores(layout):
    places, owners = layout.places, layout.owners
    return [
        [p * owners + w for p in range(near, places, 2) for w in range(owners)] for near in (0, 1)
    ]


def tie(value, after):
    def kernel(*refs):
        pass

    return pl.pallas_call(
        kernel,
        in_specs=[pl.BlockSpec(memory_space=pl.ANY)] * (1 + len(after)),
        out_specs=pl.BlockSpec(memory_space=pl.ANY),
        out_shape=jax.ShapeDtypeStruct(value.shape, value.dtype),
        input_output_aliases={0: 0},
        cost_estimate=NO_COST,
        name="tie",
    )(value, *after)


def pack_kernel(count, rows, *refs):
    outs = refs[-4:]
    at = 0
    for k in range(count):
        keeps, gots = refs[4 * k : 4 * k + 2], refs[4 * k + 2 : 4 * k + 4]
        width = keeps[0].shape[-1]
        for f in range(keeps[0].shape[2] // rows):
            s = slice(f * rows, (f + 1) * rows)
            for part, pairs in ((0, ((0, 2), (1, 3))), (1, ((0, 1), (2, 3)))):
                for place, target in zip(pairs, outs[2 * part : 2 * part + 2]):
                    for n, i in enumerate(place):
                        total = keeps[part][i, 0, s].astype(f32) + gots[part][i, 0, s].astype(f32)
                        target[n, 0, :, at : at + width] = total.astype(bf16)
            at += -(-width // STATE) * STATE


def pack(parts, layout, after=()):
    half = layout.owners // 2
    flat, specs = [], []
    for pair in parts:
        for a in pair:
            block = (a.shape[0], 1, *a.shape[2:])
            flat += [a, a]
            specs += [
                pl.BlockSpec(block, lambda q: (0, q, 0, 0)),
                pl.BlockSpec(block, lambda q: (0, half + q, 0, 0)),
            ]
    width = 0
    for keep, _ in parts:
        width = -(-width // STATE) * STATE + keep.shape[2] // layout.rows * keep.shape[3]
    out = jax.ShapeDtypeStruct((2, half, layout.rows, width), bf16)
    return pl.pallas_call(
        functools.partial(pack_kernel, len(parts), layout.rows),
        grid=(half,),
        in_specs=specs + [pl.BlockSpec(memory_space=pl.ANY)] * len(after),
        out_specs=[pl.BlockSpec((2, 1, layout.rows, width), lambda q: (0, q, 0, 0))] * 4,
        out_shape=[out] * 4,
        compiler_params=pltpu.CompilerParams(vmem_limit_bytes=VMEM),
        cost_estimate=NO_COST,
        name="pack",
    )(*flat, *after)


def small_rows(layer_shapes):
    table = []
    for k, shape in enumerate(layer_shapes):
        for at in range(0, shape[1], STATE):
            table.append((k, shape[0], at))
    return sorted(table, key=lambda entry: -entry[1])


def deal_small_kernel(table, arrays, at_ref, *refs):
    keep_ref, send_ref, all_sc = refs[arrays : arrays + 3]
    places, rows, width = all_sc.shape
    all_sc[...] = jnp.zeros_like(all_sc)
    row = 0
    for k, count, at in table:
        all_sc[row // rows, row % rows : row % rows + count] = refs[k][:count, at : at + width]
        row += count
    for r in range(places):
        target = send_ref if r % 2 else keep_ref
        part = all_sc[at_ref[1] ^ r].astype(bf16)
        for q in range(target.shape[1]):
            target[r // 2, q] = part


def deal_small(here, values, layout):
    shapes = [(min(a.shape[0], 4), a.shape[1]) for a in values]
    table = small_rows(shapes)
    assert sum(entry[1] for entry in table) <= layout.places * layout.rows
    shape = jax.ShapeDtypeStruct((layout.places // 2, layout.owners, layout.rows, STATE), bf16)
    vmem = pl.BlockSpec(memory_space=pltpu.VMEM)
    return pl.pallas_call(
        functools.partial(deal_small_kernel, table, len(values)),
        in_specs=[SMEM] + [vmem] * len(values),
        out_specs=[vmem, vmem],
        out_shape=[shape, shape],
        scratch_shapes=[pltpu.VMEM((layout.places, layout.rows, STATE), f32)],
        compiler_params=pltpu.CompilerParams(vmem_limit_bytes=VMEM),
        cost_estimate=NO_COST,
        name="deal_small",
    )(here, *values)


def place_small_kernel(table, shapes, at_ref, even_ref, odd_ref, *refs):
    count = len(shapes)
    outs, all_sc, row_scs = refs[:-1 - count], refs[-1 - count], refs[-count:]
    pairs, rows = even_ref.shape[:2]
    for i in range(pairs):
        all_sc[(2 * i) ^ at_ref[1]] = even_ref[i].astype(f32)
        all_sc[(2 * i + 1) ^ at_ref[1]] = odd_ref[i].astype(f32)
    row = 0
    for k, n, at in table:
        row_scs[k][:n, at : at + STATE] = all_sc[row // rows, row % rows : row % rows + n]
        row += n
    each = len(shapes) // outs[0].shape[0]

    def share(k, width):
        whole = row_scs[k][...]
        return pltpu.roll(whole, lax.rem(whole.shape[1] - width * at_ref[0], whole.shape[1]), 1)

    for layer in range(outs[0].shape[0]):
        cw, cb, heads, gain_in, gain_gated, skip = range(each * layer, each * layer + each)
        outs[0][layer] = share(cw, outs[0].shape[2])[:4, : outs[0].shape[2]]
        one = slice(layer, layer + 1)
        outs[1][one] = share(cb, outs[1].shape[1])[:1, : outs[1].shape[1]]
        per = outs[2].shape[1]
        two = share(heads, per)
        outs[2][one] = two[1:2, :per]
        outs[3][one] = two[:1, :per]
        outs[4][one] = share(skip, per)[:1, :per]
        outs[5][one] = share(gain_in, outs[5].shape[1])[:1, : outs[5].shape[1]]
        outs[6][one] = share(gain_gated, outs[6].shape[1])[:1, : outs[6].shape[1]]


def place_small(here, even, odd, values, shapes, layout):
    sizes = [(min(a.shape[0], 4), a.shape[1]) for a in values]
    table = small_rows(sizes)
    vmem = pl.BlockSpec(memory_space=pltpu.VMEM)
    block = (layout.places // 2, layout.rows, STATE)
    last = even.shape[2] // STATE - 1
    return pl.pallas_call(
        functools.partial(place_small_kernel, table, sizes),
        grid=(1,),
        in_specs=[SMEM] + [pl.BlockSpec(block, lambda s: (0, 0, last))] * 2,
        out_specs=[vmem] * len(shapes),
        out_shape=[jax.ShapeDtypeStruct(shape, f32) for shape in shapes],
        scratch_shapes=[pltpu.VMEM((layout.places, layout.rows, STATE), f32)]
        + [pltpu.VMEM((8, width), f32) for _, width in sizes],
        compiler_params=pltpu.CompilerParams(vmem_limit_bytes=VMEM),
        cost_estimate=NO_COST,
        name="place_small",
    )(here, even, odd)


def pair_kernel(count, rows, *refs):
    target = refs[-1]
    at = 0
    for k in range(count):
        keep, got = refs[2 * k : 2 * k + 2]
        width = keep.shape[-1]
        for f in range(keep.shape[2] // rows):
            s = slice(f * rows, (f + 1) * rows)
            total = keep[:, 0, s].astype(f32) + got[:, 0, s].astype(f32)
            target[:, 0, :, at : at + width] = total.astype(bf16)
            at += width


def pair_sums(parts, layout, after=()):
    flat = [a for pair in parts for a in pair]
    width = sum(keep.shape[2] // layout.rows * keep.shape[3] for keep, _ in parts)
    pairs = layout.places // 2
    return pl.pallas_call(
        functools.partial(pair_kernel, len(parts), layout.rows),
        grid=(layout.owners,),
        in_specs=[pl.BlockSpec((pairs, 1, *a.shape[2:]), lambda q: (0, q, 0, 0)) for a in flat]
        + [pl.BlockSpec(memory_space=pl.ANY)] * len(after),
        out_specs=pl.BlockSpec((pairs, 1, layout.rows, width), lambda q: (0, q, 0, 0)),
        out_shape=jax.ShapeDtypeStruct((pairs, layout.owners, layout.rows, width), bf16),
        compiler_params=pltpu.CompilerParams(vmem_limit_bytes=VMEM),
        cost_estimate=NO_COST,
        name="pair_sums",
    )(*flat, *after)


def halve_kernel(*refs):
    outs = refs[-4:]
    for part in (0, 1):
        keep, got = refs[2 * part : 2 * part + 2]
        for n in (0, 1):
            total = keep[n].astype(f32) + got[n].astype(f32)
            outs[2 * part + n][...] = total.astype(bf16)


def halve(arrays, after=()):
    two, half, rows, width = arrays[0].shape
    return pl.pallas_call(
        halve_kernel,
        grid=(half,),
        in_specs=[pl.BlockSpec((2, 1, rows, width), lambda q: (0, q, 0, 0))] * 4
        + [pl.BlockSpec(memory_space=pl.ANY)] * len(after),
        out_specs=[pl.BlockSpec((1, rows, width), lambda q: (q, 0, 0))] * 4,
        out_shape=[jax.ShapeDtypeStruct((half, rows, width), bf16)] * 4,
        compiler_params=pltpu.CompilerParams(vmem_limit_bytes=VMEM),
        cost_estimate=NO_COST,
        name="halve",
    )(*arrays, *after)


def apart_kernel(owners, at_ref, *refs):
    outs = refs[-owners:]
    half = owners // 2
    for q in range(owners):
        keep, got = refs[:2] if q < half else refs[2:4]
        outs[q][...] = (keep[q % half].astype(f32) + got[q % half].astype(f32)).astype(bf16)


def sum_kernel(count, at_ref, *refs):
    total = refs[0][...].astype(f32)
    for a in refs[1:count]:
        total = total + a[...].astype(f32)
    refs[-1][...] = total.astype(bf16)


class Collect:
    def __init__(self, here, layout):
        self.here, self.layout, self.parts = here, layout, {}

    def add(self, order, keep, send, after=()):
        if after:
            send = tie(send, after)
        self.parts[order] = (keep, swap(send, "seq", 1))
        return self.parts[order][1]

    def pack(self, *after):
        parts = [self.parts[k] for k in sorted(self.parts)]
        keep_a, send_a, keep_b, send_b = pack(parts, self.layout, after)
        self.now = [keep_a, swap(send_a, "seq", X), keep_b, swap(send_b, "seq", Y)]

    def halve(self, *after):
        keep_a, send_a, keep_b, send_b = halve(self.now, after)
        self.now = [keep_a, swap(send_a, "seq", Y), keep_b, swap(send_b, "seq", X)]

    def apart(self, *after):
        owners = self.layout.owners
        shape = jax.ShapeDtypeStruct(self.now[0].shape[1:], bf16)
        out = small_call(
            functools.partial(apart_kernel, owners), self.here, self.now, [shape] * owners, after,
            name="apart",
        )
        self.now = [out[0]] + [swap(out[q], "wa", q) for q in range(1, owners)]

    def whole(self, *after):
        shape = jax.ShapeDtypeStruct(self.now[0].shape, bf16)
        (own,) = small_call(
            functools.partial(sum_kernel, len(self.now)), self.here, self.now, [shape], after,
            name="whole",
        )
        self.now = [own]

    def at_once(self, *after):
        places, owners = self.layout.places, self.layout.owners
        parts = [self.parts[k] for k in sorted(self.parts)]
        self.pairs = pair_sums(parts, self.layout, after)
        total = self.pairs
        total = total.reshape(places // 2 * owners, *total.shape[2:])
        like = like_cores(self.layout)
        self.now = [lax.psum_scatter(total, ("seq", "wa"), axis_index_groups=like)]

    def gathered(self, *after):
        self.now = [lax.all_gather(tie(self.now[0], after), "seq")]

    def spread(self, *after):
        own = tie(self.now[0], after) if after else self.now[0]
        even = jnp.stack([own] + [swap(own, "seq", by) for by in (X, Y, X + Y)])
        self.now = [even, swap(even, "seq", 1)]


WIDE = 1024


def place_kernel(ins, sources, given, at_ref, steps_ref, *refs):
    found, outs, own_sc = refs[:sources], refs[sources + given : -1], refs[-1]
    if sources == 1:
        value = found[0][...].astype(f32)
    else:
        for i in range(found[0].shape[0]):
            own_sc[(2 * i) ^ at_ref[1]] = found[0][i]
            own_sc[(2 * i + 1) ^ at_ref[1]] = found[1][i]
        value = own_sc[...].astype(f32)
    if ins:
        @pl.when(pl.program_id(0) < ins)
        def _():
            outs[0][0] = value.reshape(-1, WIDE).T

    if len(outs) > (ins > 0):
        @pl.when(pl.program_id(0) >= ins)
        def _():
            outs[-1][0, :, 0] = value


def place(at, layer, found, parts, outs, shapes, layout):
    rows = layout.rows
    sources, in_tiles, out_tiles = [], [], []
    ins = sum(count for inside, _, count, _ in parts if inside)
    for inside, source, count, target in parts:
        sources += range(source, source + count)
        (in_tiles if inside else out_tiles).extend(range(target, target + count))
    steps = len(sources)
    in_tiles = in_tiles + (in_tiles[-1:] or [0]) * (steps - len(in_tiles))
    out_tiles = (out_tiles[:1] or [0]) * (steps - len(out_tiles)) + out_tiles
    table = jnp.array([sources, in_tiles, out_tiles], jnp.int32)
    across = shapes[1][-1] // WIDE
    both = [
        pl.BlockSpec((1, WIDE, shapes[0][2]), lambda s, at_ref, t: (layer, t[1, s], 0)),
        pl.BlockSpec(
            (1, layout.places, 1, rows, WIDE),
            lambda s, at_ref, t: (layer, 0, t[2, s] // across, 0, t[2, s] % across),
        ),
    ]
    used = [i for i, needed in enumerate((ins > 0, ins < steps)) if needed]
    given = [outs[i] for i in used if outs[i] is not None]
    source = pl.BlockSpec((found[0].shape[0], rows, WIDE), lambda s, at_ref, t: (0, 0, t[0, s]))
    made = pl.pallas_call(
        functools.partial(place_kernel, ins, len(found), len(given)),
        grid_spec=pltpu.PrefetchScalarGridSpec(
            num_scalar_prefetch=2,
            grid=(steps,),
            in_specs=[source] * len(found) + [pl.BlockSpec(memory_space=pl.ANY)] * len(given),
            out_specs=[both[i] for i in used],
            scratch_shapes=[pltpu.VMEM((layout.places, rows, WIDE), bf16)],
        ),
        out_shape=[jax.ShapeDtypeStruct(shapes[i], f32) for i in used],
        input_output_aliases={2 + len(found) + i: i for i in range(len(given))},
        compiler_params=pltpu.CompilerParams(vmem_limit_bytes=VMEM),
        cost_estimate=NO_COST,
        name="place",
    )(at, table, *found, *given)
    outs = list(outs)
    for i, a in zip(used, made):
        outs[i] = a
    return outs


def lanes(row):
    return jnp.pad(row, (0, STATE - row.shape[0]))[None]


def local(
    tokens,
    in_weight,
    out_weight,
    conv_weight,
    conv_bias,
    a_log,
    dt_bias,
    skip_d,
    norm_gain,
    gated_gain,
    doc_start,
    cotangent,
):
    layers = in_weight.shape[0]
    length, width = tokens.shape[1:]
    taps, channels = conv_weight.shape[1:]
    owners = lax.axis_size("wa")
    heads = a_log.shape[1] * owners
    inner = heads * HEADDIM
    starts = (doc_start[0] - lax.axis_index("seq") * length)[:, None]

    devices = lax.axis_size("seq")
    rows = in_weight.shape[1] // devices
    here = jnp.stack([lax.axis_index("wa"), lax.axis_index("seq")]).astype(jnp.int32)
    fold = inner // width
    dealing = devices == 2 * Y and owners > 1 and owners & (owners - 1) == 0 and rows % RIM == 0
    weights = []
    if dealing:
        layout = Layout(owners, devices, rows)
        at = here
        in_turned = in_weight.swapaxes(1, 2)
        pieces = cut(at, layout, in_turned, out_weight)
        first_column = over_wa(pieces[0], layout)
        early = straight(here, first_column)
        column = over_wa(pieces[1], layout)
        late = straight(here, column, early.arrays[1:])
        weights.append((near_by(early), 0, late))
        next_own = lax.all_gather(tie(pieces[2], column[1:]), "wa")[None]
        straight_place = jnp.stack([jnp.zeros_like(here[0]), here[1]])
        assert layers == 2
    else:
        layout = Layout(owners, 1, in_weight.shape[1])
        at = jnp.zeros((2,), jnp.int32)
        for layer in range(layers):
            out = out_weight[layer].reshape(fold, layout.rows, width).swapaxes(0, 1)
            out = out.reshape(layout.rows, fold * width)
            gate, rest = in_weight[layer][:, :inner], in_weight[layer][:, inner:]
            found = [
                Slots(at, [lax.all_gather(part, "wa")[None]], [((0,), 0)])
                for part in (rest, jnp.concatenate([gate, out], axis=1))
            ]
            weights.append((found[0], 0, found[1]))
    own_small = [
        conv_weight.reshape(layers, taps * channels), conv_bias, a_log, dt_bias, skip_d,
        norm_gain, gated_gain,
    ]
    small = jnp.concatenate(own_small, axis=1)
    if dealing:
        small = tie(small, weights[0][0].arrays[:1])
    if owners & (owners - 1) == 0:
        small = jnp.stack([small] + [swap(small, "wa", q) for q in range(1, owners)])
        small = jnp.take(small, jnp.arange(owners) ^ lax.axis_index("wa"), axis=0).astype(f32)
    else:
        small = lax.all_gather(small, "wa", axis=0).astype(f32)
    sizes = [a.shape[1] for a in own_small]
    params = []
    for layer in range(layers):
        found, col = [], 0
        for i, size in enumerate(sizes):
            part = small[:, layer, col : col + size]
            col += size
            if i == 0:
                part = part.reshape(owners, taps, channels).swapaxes(0, 1)
                found.append(part.reshape(taps, owners * channels))
            else:
                found.append(part.reshape(owners * size))
        params.append(found)

    resid = tokens[0]
    start = resid.astype(f32)
    normed = (
        start
        * lax.rsqrt(jnp.mean(start * start, axis=1, keepdims=True) + EPSILON)
        * params[0][5]
    ).astype(bf16)
    records = []
    for layer in range(layers):
        cw, cb, alog, dtb, skip, ngain, ggain = params[layer]
        rate = lanes(-jnp.exp(alog))
        skip_row = jnp.repeat(skip, HEADDIM)[None]
        if dealing and layer > 0:
            split = inner + fold * width
            found = across(straight_place, tie(next_own[..., split:], [beside_out]))
            late = across(straight_place, tie(next_own[..., :split], found.arrays[1:]))
            weights.append((near_by(found, [normed]), 0, late))
        early, rest_at, late = weights[layer]
        rim = passed_along(normed[length - RIM :], "seq", 1)
        nrm = normed
        cin, cv, dt, lam, sig, lamt, state, fresh, dec, nrmt = first(
            layout, rim, nrm, early, rest_at, cw, cb[None], lanes(dtb), rate, starts, heads
        )
        y = within(cv, dt, lam, lamt, starts, skip_row)
        if dealing:
            state = tie(state, [*late.arrays[1:], y])
        s0, _, entered = carried_over(here, state, False, lambda sent: [sent])
        if dealing:
            late = near_by(late, [entered] if layer else ())
            weights[layer] = (early, 0, late)
        beside_out = s0 if not dealing else entered
        gain_next = params[min(layer + 1, layers - 1)][5][None]
        gate, y, gated, scale, resid_next, low, normed = join(
            layout, late, 0, 1, nrm, y, cv, lam, starts, s0, fresh, dec, ggain[None], resid, gain_next
        )
        records.append(
            (resid, cin, cv, dt, lam, sig, lamt, fresh, dec, nrmt, s0, gate, y, gated, scale,
             rate, skip_row, rim, nrm)
        )
        resid = resid_next
    result = low[None]
    grad_low = cotangent[0]
    grad = grad_low
    big = [None] * layers
    little = [None] * layers
    for layer in reversed(range(layers)):
        cw, cb, alog, dtb, skip, ngain, ggain = params[layer]
        early, rest_at, late = weights[layer]
        (resid, cin, cv, dt, lam, sig, lamt, fresh, dec, nrmt, s0, gate, y, gated, scale,
         rate, skip_row, first_rim, nrm) = records[layer]
        top = layer == layers - 1
        to = at
        if dealing and top:
            to = jnp.stack([jnp.zeros_like(at[0]), at[1] % 2])
        gy, ggate, gggain, gskip, later, total, *dwo = gate_back(
            [upper.pairs] if dealing and not top else (), to, layout, late, 1, grad_low, y, gate, gated, scale, ggain[None], cv, lam, starts,
            dec,
        )
        if dealing and top:
            upper = Collect(here, layout)
            upper.add(1, *dwo)
        elif dealing:
            under = Collect(here, layout)
            under.add(1, *dwo)

        def beside(sent):
            return within_back(
                (), to, layout, late, 0, gy, cv, dt, lam, lamt, starts, s0, fresh, dec, ggate, nrmt
            )

        gend, (gxd, glam, gbc, gnrm_gate, *dw_gate), entered = carried_over(
            here, total, True, beside
        )
        if dealing and top:
            upper.add(0, *dw_gate, [entered])
        elif dealing:
            under.add(0, *dw_gate, [entered, under.parts[1][1]])
            under.pack()
        edge, gnrm, gcw, gcb, gsmall, gngain, *dw_rest = last(
            under.now[:1] if dealing and not top else (), to, layout, early, rest_at, gxd, cv, cin, gy, dt, lam, sig, starts, gend, later, s0,
            fresh, dec, nrmt, glam, gbc, gnrm_gate, skip_row, rate, cw, first_rim, nrm,
            ngain[None],
        )
        if dealing and top:
            upper.add(2, *dw_rest, [upper.parts[0][1], upper.parts[1][1]])
        elif dealing:
            under.halve(gsmall)
            tail = Collect(here, layout)
            tail.add(0, *dw_rest, [under.now[0]])
            edge = tie(edge, [under.now[0]])
        rim = passed_along(edge, "seq", -1)
        if layer > 0 or not dealing:
            grad, grad_low = norm_back(grad, gnrm, rim, resid, ngain[None])
        if dealing and top:
            upper.at_once(grad_low)
        big[layer] = (dw_gate, dwo, dw_rest)
        little[layer] = (gcw, gcb, gsmall[:2], gngain, gggain, gskip)

    in_width, rest = in_weight.shape[2], in_weight.shape[2] - inner
    if dealing:
        assert layers == 2
        values = [a for layer in range(layers) for a in little[layer]]
        tail.add(1, *deal_small(here, values, layout))
        tail.pack()
        under.apart(tail.now[0])
        tail.halve(under.now[0])
        upper.gathered(tail.now[0])
        grad, _ = norm_back(grad, gnrm, rim, resid, ngain[None], tail.now[:1])
        both = [(layers, in_width, in_weight.shape[1]), (layers, layout.places, fold, layout.rows, width)]
        tiles = inner // WIDE
        more = -(-rest // WIDE)
        under.whole(grad)
        tail.apart(under.now[0])
        under.spread(tail.now[0])
        made = place(
            at, 1, upper.now,
            ((True, 0, tiles, 0), (True, 2 * tiles, more, tiles), (False, tiles, tiles, 0)),
            [None, None], both, layout,
        )
        tail.whole(made[0])
        tail.spread()
        made = place(
            at, 0, under.now, ((True, 0, tiles, 0), (False, tiles, tiles, 0)), made, both, layout
        )
        made = place(at, 0, tail.now, ((True, 0, more, tiles),), made, both, layout)
        in_grad = made[0].swapaxes(1, 2)
        out_grad = made[1].reshape(out_weight.shape)
        found = place_small(
            here, *tail.now, values, [a.shape for a in (conv_weight, conv_bias, a_log, dt_bias, skip_d, norm_gain, gated_gain)], layout
        )
    else:

        def owned(part):
            part = part.reshape(owners, -1, part.shape[-1])
            part = lax.psum_scatter(part, "wa", scatter_dimension=0)
            return lax.psum(part, "seq").astype(f32)

        in_grad = jnp.stack(
            [
                jnp.concatenate([owned(big[layer][0][0]), owned(big[layer][2][0])], axis=1)
                for layer in range(layers)
            ]
        )
        out_grad = jnp.stack([owned(big[layer][1][0]) for layer in range(layers)])
        rows = []
        for gcw, gcb, two, gngain, gggain, gskip in little:
            gcw = gcw.reshape(taps, owners, channels).swapaxes(0, 1).reshape(owners, -1)
            flat = (gcb[0], two[1, :heads], two[0, :heads], gskip[0, :heads], gngain[0], gggain[0])
            rows.append(jnp.concatenate([gcw] + [a.reshape(owners, -1) for a in flat], axis=1))
        mine = lax.dynamic_index_in_dim(
            lax.psum(jnp.stack(rows, axis=1), ("wa", "seq")), lax.axis_index("wa"), 0, keepdims=False
        )
        found, col = [], 0
        for i, size in enumerate(sizes):
            part = mine[:, col : col + size]
            col += size
            found.append(part.reshape(layers, taps, channels) if i == 0 else part)
    return (result, grad[None], in_grad, out_grad, *found)


def solution(mesh):
    in_specs = (
        P("wa", "seq", None),
        P(None, "wa", None),
        P(None, "wa", None),
        P(None, None, "wa"),
        P(None, "wa"),
        P(None, "wa"),
        P(None, "wa"),
        P(None, "wa"),
        P(None, "wa"),
        P(None, "wa"),
        P("wa", "seq"),
        P("wa", "seq", None),
    )
    out_specs = (
        P("wa", "seq", None),
        P("wa", "seq", None),
        P(None, "wa", None),
        P(None, "wa", None),
        P(None, None, "wa"),
        P(None, "wa"),
        P(None, "wa"),
        P(None, "wa"),
        P(None, "wa"),
        P(None, "wa"),
        P(None, "wa"),
    )
    return jax.shard_map(local, mesh=mesh, in_specs=in_specs, out_specs=out_specs, check_vma=False)
```

```python
import functools

import jax
import jax.numpy as jnp
from jax import lax
from jax.experimental import pallas as pl
from jax.experimental.pallas import tpu as pltpu
from jax.sharding import PartitionSpec as P

HEADDIM = 64
STATE = 128
BLOCK = 256
TILE = 256
PER = TILE // HEADDIM
RIM = 16
EPSILON = 1e-05
PRECISE = lax.Precision.HIGHEST
f32 = jnp.float32
bf16 = jnp.bfloat16
FAR = -1e30
VMEM = 64 * 2**20
NO_COST = pl.CostEstimate(flops=0, bytes_accessed=0, transcendentals=0)


def dot(a, b, ca=1, cb=0, precision=None):
    return lax.dot_general(
        a, b, (((ca,), (cb,)), ((), ())), precision=precision, preferred_element_type=f32
    )


def iota(shape, axis):
    return lax.broadcasted_iota(jnp.int32, shape, axis)


def logistic(v):
    return 0.5 + 0.5 * jnp.tanh(0.5 * v)


def silu(v):
    return v * logistic(v)


def dsilu(v):
    s = logistic(v)
    return s * (1.0 + v * (1.0 - s))


def split(q):
    high = q.astype(bf16)
    return jnp.concatenate([high, (q - high.astype(f32)).astype(bf16)], axis=1)


def spread(pair, group):
    rows = iota((2 * STATE, TILE), 0) % STATE
    cols = PER * group + iota((2 * STATE, TILE), 1) // HEADDIM
    return dot(pair, (rows == cols).astype(f32).astype(bf16))


def chooser(group):
    return iota((TILE, STATE), 1) == PER * group + iota((TILE, STATE), 0) // HEADDIM


def gather_heads(z, group):
    pick = chooser(group).astype(f32).astype(bf16)
    high = z.astype(bf16)
    low = (z - high.astype(f32)).astype(bf16)
    return dot(high, pick) + dot(low, pick)


def head_rows(row, group):
    return jnp.sum(jnp.where(chooser(group), row, 0.0), axis=1, keepdims=True)


def lower(n):
    return iota((n, n), 0) >= iota((n, n), 1)


def decay_rows(decay):
    high = decay.astype(bf16).astype(f32)
    zeros = jnp.zeros((RIM - 2, STATE), f32)
    return jnp.concatenate([high, decay - high, zeros], axis=0).astype(bf16)


def block_of(b):
    return slice(b * BLOCK, (b + 1) * BLOCK)


def end_weights(starts, lam, b):
    s = block_of(b)
    last = (b + 1) * BLOCK - 1
    place = b * BLOCK + iota((BLOCK, 1), 0)
    keep = place >= starts[last : last + 1]
    return jnp.where(keep, jnp.exp(lam[last : last + 1] - lam[s]), 0.0)


def reach_weights(starts, lam, b):
    s = block_of(b)
    return jnp.where(starts[s] < b * BLOCK, jnp.exp(lam[s]), 0.0)


def fill_mask(mask_ref, starts, blocks):
    for b in range(blocks):
        t = b * BLOCK + iota((BLOCK, BLOCK), 0)
        s = b * BLOCK + iota((BLOCK, BLOCK), 1)
        mask_ref[b] = jnp.where((s <= t) & (s >= starts[block_of(b)]), 0.0, FAR)


def assemble(w_refs, w_sc, at_ref, plan):
    for w_ref, (places, first_owner) in zip(w_refs, plan):
        for i, r in enumerate(places):
            for q in range(w_ref.shape[1]):
                w_sc[at_ref[0] ^ (first_owner + q), at_ref[1] ^ r] = w_ref[i, q]
    return w_sc[...].reshape(-1, w_sc.shape[-1])


def deal(value, keep_ref, send_ref, d_sc, at_ref):
    owners, places = d_sc.shape[:2]
    d_sc[...] = value.astype(bf16).reshape(d_sc.shape)
    for r in range(places):
        target = send_ref if r % 2 else keep_ref
        for q in range(owners):
            target[r // 2, q] = d_sc[at_ref[2] ^ q, at_ref[3] ^ r]


class Layout:
    def __init__(self, owners, places, rows):
        self.owners, self.places, self.rows = owners, places, rows

    def scratch(self, width):
        return pltpu.VMEM((self.owners, self.places, self.rows, width), bf16)

    def dealt(self, col):
        block = (max(self.places // 2, 1), self.owners, self.rows, TILE)
        return [pl.BlockSpec(block, lambda *s: (0, 0, 0, col(*s)))] * (1 if self.places == 1 else 2)

    def dealt_shape(self, rows, width):
        shape = (max(self.places // 2, 1), self.owners, rows, width)
        return [jax.ShapeDtypeStruct(shape, bf16)] * (1 if self.places == 1 else 2)


class Slots:
    def __init__(self, near, arrays, plan):
        self.near, self.arrays, self.plan = near, tuple(arrays), tuple(plan)

    def tiles(self, col):
        return [
            pl.BlockSpec((*a.shape[:3], TILE), lambda *s: (0, 0, 0, col(*s))) for a in self.arrays
        ]

    def whole(self, width, at):
        return [pl.BlockSpec((*a.shape[:3], width), lambda *s: (0, 0, 0, at)) for a in self.arrays]


SMEM = pl.BlockSpec(memory_space=pltpu.SMEM)


def first_kernel(
    plan, at_ref, rim_ref, normed_ref, *refs
):
    w_refs, rest = refs[: len(plan)], refs[len(plan) :]
    first_body(plan, at_ref, rim_ref, normed_ref, w_refs, *rest)


def first_body(
    plan, at_ref, rim_ref, normed_ref, w_refs, cw_ref, cb_ref, dtb_ref, rate_ref, starts_ref,
    cin_ref, cv_ref, dt_ref, lam_ref, sig_ref, lamt_ref, state_ref, fresh_ref, dec_ref, nrmt_ref,
    b_sc, e_sc, w_sc, nrm_ref,
):
    step = pl.program_id(0)
    length = starts_ref.shape[0]
    blocks = length // BLOCK
    heads = lamt_ref.shape[0] * PER
    starts = starts_ref[...]
    w = assemble(w_refs, w_sc, at_ref, plan)

    @pl.when(step == 0)
    def _():
        nrm_ref[:length] = normed_ref[...]
        nrm_ref[length:] = rim_ref[...]

    def conv():
        pe = dot(nrm_ref[...], w)
        cin_ref[...] = pe.astype(bf16)
        place = iota((length, 1), 0)
        taps = cw_ref.shape[0]
        acc = cb_ref[...] + cw_ref[taps - 1 : taps] * pe[:length]
        for k in range(taps - 1):
            back = taps - 1 - k
            keep = place - back >= starts
            acc = acc + jnp.where(keep, cw_ref[k : k + 1] * pltpu.roll(pe, back, 0)[:length], 0.0)
        cv = acc.astype(bf16)
        cv_ref[...] = cv
        return silu(cv.astype(f32))

    @pl.when(step == 0)
    def _():
        act = conv()
        b_sc[...] = act[:, :STATE].astype(bf16)
        nrmt_ref[...] = nrm_ref[...].T

    @pl.when(step == 1)
    def _():
        z = dot(nrm_ref[:length], w[:, :STATE]) + dtb_ref[...]
        live = iota(z.shape, 1) < heads
        dt = jnp.where(live, jnp.maximum(z, 0.0) + jnp.log1p(jnp.exp(-jnp.abs(z))), 0.0)
        dt_ref[...] = dt
        sig_ref[...] = jnp.where(live, 1.0 / (1.0 + jnp.exp(-z)), 0.0)
        change = dt * rate_ref[...]
        tri = lower(BLOCK).astype(f32)
        lam = jnp.concatenate(
            [dot(tri, change[block_of(b)], precision=PRECISE) for b in range(blocks)], axis=0
        )
        lam_ref[...] = lam
        across = lam.T
        for g in range(lamt_ref.shape[0]):
            lamt_ref[g] = across[PER * g : PER * (g + 1)]
        total = None
        rows = []
        for b in range(blocks):
            e_sc[block_of(b)] = split(end_weights(starts, lam, b) * dt[block_of(b)])
            last = (b + 1) * BLOCK - 1
            decay = jnp.where(
                starts[last : last + 1] < b * BLOCK, jnp.exp(lam[last : last + 1]), 0.0
            )
            decay = jnp.where(iota(decay.shape, 1) < heads, decay, 0.0)
            rows.append(decay)
            total = decay if total is None else total * decay
        rows.append(total)
        rows.append(jnp.zeros((8 - len(rows), STATE), f32))
        dec_ref[...] = jnp.concatenate(rows, axis=0)
        state_ref[:RIM] = decay_rows(total)

    @pl.when(step >= 2)
    def _():
        group = step - 2
        xe = (conv() * spread(e_sc[...], group)).astype(bf16)
        total = None
        for b in range(blocks):
            fresh = dot(xe[block_of(b)], b_sc[block_of(b)], 0, 0)
            if b + 1 < blocks:
                fresh_ref[b] = fresh
            if total is None:
                total = fresh
            else:
                total = head_rows(dec_ref[b : b + 1], group) * total + fresh
        state_ref[...] = total.astype(state_ref.dtype)


def first(layout, rim, normed, slots, rest_at, cw, cb, dtb, rate, starts, heads):
    d = normed.shape[1]
    length = starts.shape[0]
    ext = length + RIM
    blocks = length // BLOCK
    inner = heads * HEADDIM
    groups = inner // TILE
    col = lambda s: jnp.where(s == 0, groups, jnp.maximum(s - 2, 0))
    wcol = lambda s: rest_at + jnp.where(s < 2, groups + s, s - 2)
    tile = lambda s: jnp.maximum(s - 2, 0)
    full = lambda *shape: pl.BlockSpec(shape, lambda s: (0,) * len(shape))
    state = lambda s: jnp.where(s < 2, groups, s - 2)
    return pl.pallas_call(
        functools.partial(first_kernel, slots.plan),
        grid=(groups + 2,),
        in_specs=[
            SMEM,
            full(RIM, d),
            full(length, d),
            *slots.tiles(wcol),
            pl.BlockSpec((cw.shape[0], TILE), lambda s: (0, col(s))),
            pl.BlockSpec((1, TILE), lambda s: (0, col(s))),
            full(1, STATE),
            full(1, STATE),
            full(length, 1),
        ],
        out_specs=[
            pl.BlockSpec((ext, TILE), lambda s: (0, col(s))),
            pl.BlockSpec((length, TILE), lambda s: (0, col(s))),
            full(length, STATE),
            full(length, STATE),
            full(length, STATE),
            full(groups, PER, length),
            pl.BlockSpec((TILE, STATE), lambda s: (state(s), 0)),
            pl.BlockSpec((blocks - 1, TILE, STATE), lambda s: (0, tile(s), 0)),
            full(8, STATE),
            full(d, ext),
        ],
        out_shape=[
            jax.ShapeDtypeStruct((ext, inner + 2 * STATE), bf16),
            jax.ShapeDtypeStruct((length, inner + 2 * STATE), bf16),
            jax.ShapeDtypeStruct((length, STATE), f32),
            jax.ShapeDtypeStruct((length, STATE), f32),
            jax.ShapeDtypeStruct((length, STATE), f32),
            jax.ShapeDtypeStruct((groups, PER, length), f32),
            jax.ShapeDtypeStruct((inner + RIM, STATE), bf16),
            jax.ShapeDtypeStruct((blocks - 1, inner, STATE), f32),
            jax.ShapeDtypeStruct((8, STATE), f32),
            jax.ShapeDtypeStruct((d, ext), bf16),
        ],
        scratch_shapes=[
            pltpu.VMEM((length, STATE), bf16),
            pltpu.VMEM((length, 2 * STATE), bf16),
            layout.scratch(TILE),
            pltpu.VMEM((ext, d), bf16),
        ],
        compiler_params=pltpu.CompilerParams(vmem_limit_bytes=VMEM),
        cost_estimate=NO_COST,
        name="project",
    )(slots.near, rim, normed, *slots.arrays, cw, cb, dtb, rate, starts)


def pair_of(width):
    return iota((1, width), 1) < HEADDIM


def within_kernel(
    x_ref, bc_ref, dt_ref, lam_ref, lamt_ref, starts_ref, skip_ref,
    y_ref,
    cross_sc, mask_sc, dt_sc,
):
    group = pl.program_id(0)
    length = starts_ref.shape[0]
    blocks = length // BLOCK

    @pl.when(group == 0)
    def _():
        act = silu(bc_ref[...].astype(f32)).astype(bf16)
        for b in range(blocks):
            s = block_of(b)
            cross_sc[b] = dot(act[s, STATE:], act[s, :STATE], 1, 1)
        fill_mask(mask_sc, starts_ref[...], blocks)
        dt_sc[...] = split(dt_ref[...])

    x = silu(x_ref[...].astype(f32))
    xd = (x * spread(dt_sc[...], group)).astype(bf16)
    lam = pltpu.roll(lam_ref[...], lax.rem(STATE - PER * group, STATE), 1)
    lamt = lamt_ref[group]
    left = pair_of(2 * HEADDIM)
    for b in range(blocks):
        s = block_of(b)
        parts = []
        for p in range(PER // 2):
            c = slice(2 * HEADDIM * p, 2 * HEADDIM * (p + 1))
            two = []
            for h in (2 * p, 2 * p + 1):
                gap = (lam[s, h : h + 1] - lamt[h : h + 1, s]) + mask_sc[b]
                two.append(dot((jnp.exp(gap) * cross_sc[b]).astype(bf16), xd[s, c]))
            parts.append(jnp.where(left, two[0], two[1]))
        y = jnp.concatenate(parts, axis=1) + skip_ref[...] * x[s]
        y_ref[s] = y.astype(bf16)


def within(cv, dt, lam, lamt, starts, skip):
    length = starts.shape[0]
    blocks = length // BLOCK
    groups = lamt.shape[0]
    inner = groups * TILE
    full = lambda *shape: pl.BlockSpec(shape, lambda s: (0,) * len(shape))
    tile = pl.BlockSpec((length, TILE), lambda s: (0, s))
    return pl.pallas_call(
        within_kernel,
        grid=(groups,),
        in_specs=[
            tile,
            pl.BlockSpec((length, TILE), lambda s: (0, groups)),
            full(length, STATE),
            full(length, STATE),
            full(groups, PER, length),
            full(length, 1),
            pl.BlockSpec((1, TILE), lambda s: (0, s)),
        ],
        out_specs=tile,
        out_shape=jax.ShapeDtypeStruct((length, inner), bf16),
        scratch_shapes=[
            pltpu.VMEM((blocks, BLOCK, BLOCK), f32),
            pltpu.VMEM((blocks, BLOCK, BLOCK), f32),
            pltpu.VMEM((length, 2 * STATE), bf16),
        ],
        compiler_params=pltpu.CompilerParams(vmem_limit_bytes=VMEM),
        cost_estimate=NO_COST,
        name="within",
    )(cv, cv, dt, lam, lamt, starts, skip)


def states_of(s0, fresh_ref, dec_ref, group, blocks):
    found = [s0]
    for b in range(blocks - 1):
        found.append(head_rows(dec_ref[b : b + 1], group) * found[-1] + fresh_ref[b])
    return found


def unfold(wo_refs, wo_sc, at_ref, plan):
    rows, width = wo_sc.shape[-2:]
    short = wo_refs[0].shape[2]
    for wo_ref, (places, first_owner) in zip(wo_refs, plan):
        for i, r in enumerate(places):
            for q in range(wo_ref.shape[1]):
                for f in range(rows // short):
                    part = wo_ref[i, q, :, f * width : (f + 1) * width]
                    owner = at_ref[0] ^ (first_owner + q)
                    wo_sc[owner, at_ref[1] ^ r, f * short : (f + 1) * short] = part


def pieces_of(shape, group):
    share = shape[1] * shape[2]
    parts = share // TILE
    if parts == 1:
        return group, slice(None)
    many = TILE // shape[2]
    return group // parts, pl.ds(many * (group % parts), many)


def join_kernel(
    plan, at_ref, *refs
):
    many = len(plan)
    join_body(plan, at_ref, refs[:many], refs[many : 2 * many], *refs[2 * many :])


def join_body(
    plan, at_ref, w_refs, wo_refs, nrm_ref, y_ref, bc_ref, lam_ref, starts_ref, s0_ref, fresh_ref, dec_ref, gain_ref,
    resid_ref, gain_next_ref,
    gate_ref, y_out_ref, gated_ref, scale_ref, next_ref, low_ref, normed_ref,
    u_sc, c_sc, v_sc, sq_sc, wo_sc, w_sc,
):
    group = pl.program_id(0)
    length = starts_ref.shape[0]
    blocks = length // BLOCK
    groups = v_sc.shape[0]
    inner = groups * TILE

    @pl.when(group == 0)
    def _():
        c_sc[...] = silu(bc_ref[:, STATE:].astype(f32)).astype(bf16)
        for b in range(blocks):
            u_sc[block_of(b)] = split(reach_weights(starts_ref[...], lam_ref[...], b))
        sq_sc[...] = jnp.zeros_like(sq_sc)

    u = spread(u_sc[...], group)
    before = states_of(s0_ref[...].astype(f32), fresh_ref, dec_ref, group, blocks)
    carried = jnp.concatenate(
        [dot(c_sc[block_of(b)], before[b].astype(bf16), 1, 1) for b in range(blocks)], axis=0
    )
    y = (y_ref[...].astype(f32) + u * carried).astype(bf16)
    y_out_ref[...] = y
    gate = dot(nrm_ref[...], assemble(w_refs, w_sc, at_ref, plan)).astype(bf16)
    gate_ref[...] = gate
    v = y.astype(f32) * silu(gate.astype(f32))
    v_sc[group] = v
    sq = v * v
    sq_sc[...] += sq[:, :STATE] + sq[:, STATE:]

    @pl.when(group == groups - 1)
    def _():
        mean = jnp.sum(sq_sc[...], axis=1, keepdims=True) / inner
        scale = lax.rsqrt(mean + EPSILON)
        scale_ref[...] = scale
        acc = resid_ref[...].astype(f32)
        unfold(wo_refs, wo_sc, at_ref, plan)
        for g in range(groups):
            c = slice(g * TILE, (g + 1) * TILE)
            low = (v_sc[g] * scale * gain_ref[:, c]).astype(bf16)
            gated_ref[:, c] = low
            owner, piece = pieces_of(wo_sc.shape, g)
            acc = acc + dot(low, wo_sc[owner, piece].reshape(TILE, -1))
        next_ref[...] = acc
        low_ref[...] = acc.astype(bf16)
        norm = lax.rsqrt(jnp.mean(acc * acc, axis=1, keepdims=True) + EPSILON)
        normed_ref[...] = (acc * norm * gain_next_ref[...]).astype(bf16)


def join(layout, slots, gate_at, out_at, nrm, y, cv, lam, starts, s0, fresh, dec, gain, resid, gain_next):
    length, inner = y.shape
    d = resid.shape[1]
    fold = inner // d
    blocks = length // BLOCK
    groups = inner // TILE
    full = lambda *shape: pl.BlockSpec(shape, lambda s: (0,) * len(shape))
    tile = pl.BlockSpec((length, TILE), lambda s: (0, s))
    return pl.pallas_call(
        functools.partial(join_kernel, slots.plan),
        grid=(groups,),
        in_specs=[
            SMEM,
            *slots.tiles(lambda s: gate_at + s),
            *slots.whole(inner, out_at),
            full(length, d),
            tile,
            pl.BlockSpec((length, TILE), lambda s: (0, groups)),
            full(length, STATE),
            full(length, 1),
            pl.BlockSpec((TILE, STATE), lambda s: (s, 0)),
            pl.BlockSpec((blocks - 1, TILE, STATE), lambda s: (0, s, 0)),
            full(8, STATE),
            full(1, inner),
            full(length, d),
            full(1, d),
        ],
        out_specs=[
            tile,
            tile,
            full(length, inner),
            full(length, 1),
            full(length, d),
            full(length, d),
            full(length, d),
        ],
        out_shape=[
            jax.ShapeDtypeStruct((length, inner), bf16),
            jax.ShapeDtypeStruct((length, inner), bf16),
            jax.ShapeDtypeStruct((length, inner), bf16),
            jax.ShapeDtypeStruct((length, 1), f32),
            jax.ShapeDtypeStruct((length, d), f32),
            jax.ShapeDtypeStruct((length, d), bf16),
            jax.ShapeDtypeStruct((length, d), bf16),
        ],
        scratch_shapes=[
            pltpu.VMEM((length, 2 * STATE), bf16),
            pltpu.VMEM((length, STATE), bf16),
            pltpu.VMEM((groups, length, TILE), f32),
            pltpu.VMEM((length, STATE), f32),
            pltpu.VMEM((layout.owners, layout.places, fold * layout.rows, d), bf16),
            layout.scratch(TILE),
        ],
        compiler_params=pltpu.CompilerParams(vmem_limit_bytes=VMEM),
        cost_estimate=NO_COST,
        name="join",
    )(
        slots.near, *slots.arrays, *slots.arrays, nrm, y, cv, lam, starts, s0, fresh, dec, gain, resid,
        gain_next,
    )


def gate_back_kernel(
    plan, skip, at_ref, *refs
):
    refs = refs[skip:]
    wo_refs, rest = refs[: len(plan)], refs[len(plan) :]
    gate_back_body(plan, at_ref, wo_refs, *rest)


def gate_back_body(
    plan, at_ref, wo_refs, grad_ref, y_ref, gate_ref, gated_ref, scale_ref, gain_ref, x_ref, bc_ref, lam_ref,
    starts_ref, dec_ref,
    gy_ref, ggate_ref, ggain_ref, gskip_ref, later_ref, total_ref, *more
):
    gg_sc, u_sc, c_sc, dot_sc, wo_sc, dwo_sc = more[-6:]
    keep_ref, send_ref = more[0], more[-7]
    phase, group = pl.program_id(0), pl.program_id(1)
    length = starts_ref.shape[0]
    blocks = length // BLOCK
    groups = gg_sc.shape[0]
    inner = groups * TILE

    @pl.when((phase == 0) & (group == 0))
    def _():
        c_sc[...] = silu(bc_ref[:, STATE:].astype(f32)).astype(bf16)
        for b in range(blocks):
            u_sc[block_of(b)] = split(reach_weights(starts_ref[...], lam_ref[...], b))
        dot_sc[...] = jnp.zeros_like(dot_sc)
        unfold(wo_refs, wo_sc, at_ref, plan)

    y = y_ref[...].astype(f32)
    gate = gate_ref[...].astype(f32)
    sig = logistic(gate)
    act = gate * sig
    v = y * act
    scale = scale_ref[...]

    @pl.when(phase == 0)
    def _():
        owners, places, rows, width = wo_sc.shape
        owner, piece = pieces_of(wo_sc.shape, group)
        gg = dot(grad_ref[...], wo_sc[owner, piece].reshape(TILE, width), 1, 1)
        gv = gg * v
        ggain_ref[...] = jnp.sum(gv * scale, axis=0, keepdims=True)
        total_ref[:RIM] = decay_rows(dec_ref[blocks : blocks + 1])
        gv = gv * gain_ref[...]
        dot_sc[...] += gv[:, :STATE] + gv[:, STATE:]
        gg_sc[group] = gg * gain_ref[...]
        dwo = dot(gated_ref[...], grad_ref[...], 0, 0).astype(bf16)
        dwo_sc[owner, piece] = dwo.reshape(-1, rows, width)

        @pl.when(group == groups - 1)
        def _():
            for r in range(places):
                target = send_ref if r % 2 else keep_ref
                for q in range(owners):
                    target[r // 2, q] = dwo_sc[at_ref[2] ^ q, at_ref[3] ^ r]

    @pl.when(phase == 1)
    def _():
        @pl.when(group == 0)
        def _():
            total = jnp.sum(dot_sc[...], axis=1, keepdims=True)
            dot_sc[...] = jnp.broadcast_to(
                total * scale * scale * scale * (1.0 / inner), dot_sc.shape
            )

        gv = scale * gg_sc[group] - v * dot_sc[:, :1]
        gy = gv * act
        ggate_ref[...] = (gv * y * (sig + act * (1.0 - sig))).astype(bf16)
        low = gy.astype(bf16)
        gy_ref[...] = low
        x = silu(x_ref[...].astype(f32))
        skip = jnp.sum(low.astype(f32) * x, axis=0, keepdims=True)
        skip = gather_heads(jnp.broadcast_to(skip, (8, TILE)), group)[:1]

        @pl.when(group == 0)
        def _():
            gskip_ref[...] = jnp.zeros_like(gskip_ref)

        gskip_ref[...] += skip
        ug = (gy * spread(u_sc[...], group)).astype(bf16)
        total = None
        for b in reversed(range(blocks)):
            direct = dot(ug[block_of(b)], c_sc[block_of(b)], 0, 0)
            if total is None:
                total = direct
            else:
                total = head_rows(dec_ref[b : b + 1], group) * total + direct
            if b > 0:
                later_ref[b - 1] = direct
        total_ref[...] = total.astype(total_ref.dtype)


def gate_back(after, at, layout, slots, out_at, grad_low, y, gate, gated, scale, gain, cv, lam, starts, dec):
    length, inner = y.shape
    d = grad_low.shape[1]
    rows = inner // d * layout.rows
    blocks = length // BLOCK
    groups = inner // TILE
    full = lambda *shape: pl.BlockSpec(shape, lambda p, s: (0,) * len(shape))
    early = lambda p, s: jnp.where(p == 0, s, groups - 1)
    late = lambda p, s: s * p
    tile = pl.BlockSpec((length, TILE), lambda p, s: (0, s))
    late_tile = pl.BlockSpec((length, TILE), lambda p, s: (0, late(p, s)))
    return pl.pallas_call(
        functools.partial(gate_back_kernel, slots.plan, len(after)),
        grid=(2, groups),
        in_specs=[
            SMEM,
            *[pl.BlockSpec(memory_space=pl.ANY)] * len(after),
            *slots.whole(inner, out_at),
            full(length, d),
            tile,
            tile,
            pl.BlockSpec((length, TILE), lambda p, s: (0, early(p, s))),
            full(length, 1),
            pl.BlockSpec((1, TILE), lambda p, s: (0, s)),
            late_tile,
            pl.BlockSpec((length, TILE), lambda p, s: (0, groups)),
            full(length, STATE),
            full(length, 1),
            full(8, STATE),
        ],
        out_specs=[
            late_tile,
            late_tile,
            pl.BlockSpec((1, TILE), lambda p, s: (0, early(p, s))),
            full(1, STATE),
            pl.BlockSpec((blocks - 1, TILE, STATE), lambda p, s: (0, late(p, s), 0)),
            pl.BlockSpec((TILE, STATE), lambda p, s: (jnp.where(p == 0, groups, s), 0)),
            *[full(*a.shape) for a in layout.dealt_shape(rows, d)],
        ],
        out_shape=[
            jax.ShapeDtypeStruct((length, inner), bf16),
            jax.ShapeDtypeStruct((length, inner), bf16),
            jax.ShapeDtypeStruct((1, inner), f32),
            jax.ShapeDtypeStruct((1, STATE), f32),
            jax.ShapeDtypeStruct((blocks - 1, inner, STATE), f32),
            jax.ShapeDtypeStruct((inner + RIM, STATE), bf16),
            *layout.dealt_shape(rows, d),
        ],
        scratch_shapes=[
            pltpu.VMEM((groups, length, TILE), f32),
            pltpu.VMEM((length, 2 * STATE), bf16),
            pltpu.VMEM((length, STATE), bf16),
            pltpu.VMEM((length, STATE), f32),
            pltpu.VMEM((layout.owners, layout.places, rows, d), bf16),
            pltpu.VMEM((layout.owners, layout.places, rows, d), bf16),
        ],
        compiler_params=pltpu.CompilerParams(vmem_limit_bytes=VMEM),
        cost_estimate=NO_COST,
        name="gate_back",
    )(jnp.concatenate([slots.near, at]), *after, *slots.arrays, grad_low, y, gate, gated, scale, gain, cv, cv, lam, starts, dec)


def within_back_kernel(
    plan, skip, at_ref, *refs
):
    refs = refs[skip:]
    w_refs, rest = refs[: len(plan)], refs[len(plan) :]
    within_back_body(plan, at_ref, w_refs, *rest)


def within_back_body(
    plan, at_ref, w_refs, gy_ref, x_ref, bc_ref, dt_ref, lam_ref, lamt_ref, starts_ref, s0_ref, fresh_ref, dec_ref,
    ggate_ref, nrmt_ref,
    gxd_ref, glam_ref, gbc_ref, gnrm_ref, *more
):
    cross_sc, gcross_sc, mask_sc, dt_sc, u_sc, act_sc, w_sc, d_sc = more[-8:]
    keep_ref, send_ref = more[0], more[-9]
    group = pl.program_id(0)
    length = starts_ref.shape[0]
    blocks = length // BLOCK
    groups = lamt_ref.shape[0]

    @pl.when(group == 0)
    def _():
        act = silu(bc_ref[...].astype(f32)).astype(bf16)
        act_sc[...] = act
        for b in range(blocks):
            s = block_of(b)
            cross_sc[b] = dot(act[s, STATE:], act[s, :STATE], 1, 1)
            u_sc[s] = split(reach_weights(starts_ref[...], lam_ref[...], b))
        fill_mask(mask_sc, starts_ref[...], blocks)
        dt_sc[...] = split(dt_ref[...])
        gcross_sc[...] = jnp.zeros_like(gcross_sc)
        glam_ref[...] = jnp.zeros_like(glam_ref)
        gbc_ref[...] = jnp.zeros_like(gbc_ref)
        gnrm_ref[...] = jnp.zeros_like(gnrm_ref)

    ggate = ggate_ref[...]
    gnrm_ref[...] += dot(ggate, assemble(w_refs, w_sc, at_ref, plan), 1, 1)
    deal(dot(nrmt_ref[:, :length], ggate), keep_ref, send_ref, d_sc, at_ref)

    x = silu(x_ref[...].astype(f32))
    xd = (x * spread(dt_sc[...], group)).astype(bf16)
    gy = gy_ref[...]
    u = spread(u_sc[...], group)
    before = states_of(s0_ref[...].astype(f32), fresh_ref, dec_ref, group, blocks)
    lam = pltpu.roll(lam_ref[...], lax.rem(STATE - PER * group, STATE), 1)
    lamt = lamt_ref[group]
    left = pair_of(2 * HEADDIM)
    for b in range(blocks):
        s = block_of(b)
        gcross = gcross_sc[b]
        ys, gxds = [], []
        for p in range(PER // 2):
            c = slice(2 * HEADDIM * p, 2 * HEADDIM * (p + 1))
            y2, g2 = [], []
            for h in (2 * p, 2 * p + 1):
                decay = jnp.exp((lam[s, h : h + 1] - lamt[h : h + 1, s]) + mask_sc[b])
                weight = (decay * cross_sc[b]).astype(bf16)
                y2.append(dot(weight, xd[s, c]))
                g2.append(dot(weight, gy[s, c], 0, 0))
                own = left if h % 2 == 0 else ~left
                mine = jnp.where(own, gy[s, c], jnp.zeros((), bf16))
                gcross = gcross + dot(mine, xd[s, c], 1, 1) * decay
            ys.append(jnp.where(left, y2[0], y2[1]))
            gxds.append(jnp.where(left, g2[0], g2[1]))
        gcross_sc[b] = gcross
        state = before[b].astype(bf16)
        y = jnp.concatenate(ys, axis=1) + u[s] * dot(act_sc[s, STATE:], state, 1, 1)
        gxd = jnp.concatenate(gxds, axis=1)
        gxd_ref[s] = gxd
        gyf = gy[s].astype(f32)
        glam_ref[s] += gather_heads(gyf * y - xd[s].astype(f32) * gxd, group)
        gbc_ref[s, STATE:] += dot((u[s] * gyf).astype(bf16), state)

    @pl.when(group == groups - 1)
    def _():
        for b in range(blocks):
            s = block_of(b)
            low = gcross_sc[b].astype(bf16)
            gbc_ref[s, :STATE] += dot(low, act_sc[s, STATE:], 0, 0)
            gbc_ref[s, STATE:] += dot(low, act_sc[s, :STATE])


def within_back(after, at, layout, slots, gate_at, gy, cv, dt, lam, lamt, starts, s0, fresh, dec, ggate, nrmt):
    length, inner = gy.shape
    d, ext = nrmt.shape
    blocks = length // BLOCK
    groups = inner // TILE
    full = lambda *shape: pl.BlockSpec(shape, lambda s: (0,) * len(shape))
    tile = pl.BlockSpec((length, TILE), lambda s: (0, s))
    return pl.pallas_call(
        functools.partial(within_back_kernel, slots.plan, len(after)),
        grid=(groups,),
        in_specs=[
            SMEM,
            *[pl.BlockSpec(memory_space=pl.ANY)] * len(after),
            *slots.tiles(lambda s: gate_at + s),
            tile,
            tile,
            pl.BlockSpec((length, TILE), lambda s: (0, groups)),
            full(length, STATE),
            full(length, STATE),
            full(groups, PER, length),
            full(length, 1),
            pl.BlockSpec((TILE, STATE), lambda s: (s, 0)),
            pl.BlockSpec((blocks - 1, TILE, STATE), lambda s: (0, s, 0)),
            full(8, STATE),
            tile,
            full(d, ext),
        ],
        out_specs=[
            tile, full(length, STATE), full(length, 2 * STATE), full(length, d),
            *layout.dealt(lambda s: s),
        ],
        out_shape=[
            jax.ShapeDtypeStruct((length, inner), f32),
            jax.ShapeDtypeStruct((length, STATE), f32),
            jax.ShapeDtypeStruct((length, 2 * STATE), f32),
            jax.ShapeDtypeStruct((length, d), f32),
            *layout.dealt_shape(layout.rows, inner),
        ],
        scratch_shapes=[
            pltpu.VMEM((blocks, BLOCK, BLOCK), f32),
            pltpu.VMEM((blocks, BLOCK, BLOCK), f32),
            pltpu.VMEM((blocks, BLOCK, BLOCK), f32),
            pltpu.VMEM((length, 2 * STATE), bf16),
            pltpu.VMEM((length, 2 * STATE), bf16),
            pltpu.VMEM((length, 2 * STATE), bf16),
            layout.scratch(TILE),
            layout.scratch(TILE),
        ],
        compiler_params=pltpu.CompilerParams(vmem_limit_bytes=VMEM),
        cost_estimate=NO_COST,
        name="within_back",
    )(jnp.concatenate([slots.near, at]), *after, *slots.arrays, gy, cv, cv, dt, lam, lamt, starts, s0, fresh, dec, ggate, nrmt)


def last_kernel(
    plan, skip, at_ref, *refs
):
    refs = refs[skip:]
    w_refs, rest = refs[: len(plan)], refs[len(plan) :]
    last_body(plan, at_ref, w_refs, *rest)


def last_body(
    plan, at_ref, w_refs, gxd_ref, cv_ref, cin_ref, gy_ref, bc_ref, dt_ref, lam_ref, sig_ref, starts_ref, gend_ref,
    later_ref, s0_ref, fresh_ref, dec_ref, nrmt_ref, glam_ref, gbc_ref, gin_ref, skip_ref,
    rate_ref, cw_ref, rim_ref, nrm_ref, gain_ref,
    edge_ref, out_ref, gcw_ref, gcb_ref, gsmall_ref, ngain_ref, *more
):
    b_sc, gb_sc, dt_sc, e_sc, gdt_sc, zs_sc, over_sc, gp_sc, w_sc, d_sc, gnrm_ref = more[-11:]
    keep_ref, send_ref = more[0], more[-12]
    step = pl.program_id(0)
    length = starts_ref.shape[0]
    blocks = length // BLOCK
    groups = pl.num_programs(0) - 2
    starts = starts_ref[...]
    ext = gnrm_ref.shape[0]

    @pl.when(step == 0)
    def _():
        b_sc[...] = silu(bc_ref[:, :STATE].astype(f32)).astype(bf16)
        gb_sc[...] = gbc_ref[:, :STATE]
        dt_sc[...] = split(dt_ref[...])
        for b in range(blocks):
            e_sc[block_of(b)] = split(end_weights(starts, lam_ref[...], b))
        gdt_sc[...] = jnp.zeros_like(gdt_sc)
        zs_sc[...] = jnp.zeros_like(zs_sc)
        over_sc[...] = jnp.zeros_like(over_sc)
        gnrm_ref[length:] = jnp.zeros((RIM, gnrm_ref.shape[1]), f32)
        gnrm_ref[:length] = gin_ref[...]

    def conv_back(gact):
        gcv = gact * dsilu(cv_ref[...].astype(f32))
        gcb_ref[...] = jnp.sum(gcv, axis=0, keepdims=True)
        place = iota((length, 1), 0)
        taps = cw_ref.shape[0]
        cin = cin_ref[...].astype(f32)
        zeros = jnp.zeros((RIM, TILE), f32)
        acc = None
        rows = []
        for k in range(taps):
            back = taps - 1 - k
            term = gcv if back == 0 else jnp.where(place - back >= starts, gcv, 0.0)
            moved = jnp.concatenate([term, zeros], axis=0)
            if back:
                moved = pltpu.roll(moved, ext - back, 0)
            rows.append(jnp.sum(moved * cin, axis=0, keepdims=True))
            part = cw_ref[k : k + 1] * moved
            acc = part if acc is None else acc + part
        gcw_ref[...] = jnp.concatenate(rows, axis=0)
        gp_sc[...] = acc.astype(bf16)

    @pl.when(step < groups)
    def _():
        group = step
        x = silu(cv_ref[...].astype(f32))
        dt = spread(dt_sc[...], group)
        e = spread(e_sc[...], group)
        xd = x * dt
        gend = gend_ref[...].astype(f32)
        grads = [None] * blocks
        for b in reversed(range(blocks)):
            grads[b] = gend
            if b > 0:
                gend = head_rows(dec_ref[b : b + 1], group) * gend + later_ref[b - 1]
        before = states_of(s0_ref[...].astype(f32), fresh_ref, dec_ref, group, blocks)
        parts = []
        for b in range(blocks):
            s = block_of(b)
            low = grads[b].astype(bf16)
            parts.append(e[s] * dot(b_sc[s], low, 1, 1))
            gb_sc[s] += dot((e[s] * xd[s]).astype(bf16), low)
            over = jnp.sum(grads[b] * before[b], axis=1, keepdims=True)
            over_sc[b : b + 1] += dec_ref[b : b + 1] * jnp.sum(
                jnp.where(chooser(group), over, 0.0), axis=0, keepdims=True
            )
        more = jnp.concatenate(parts, axis=0)
        gxd = gxd_ref[...] + more
        zs_sc[...] += gather_heads(xd * more, group)
        gdt_sc[...] += gather_heads(x * gxd, group)
        conv_back(dt * gxd + skip_ref[...] * gy_ref[...].astype(f32))

    @pl.when(step == groups)
    def _():
        conv_back(jnp.concatenate([gb_sc[...], gbc_ref[:, STATE:]], axis=1))

    @pl.when(step <= groups)
    def _():
        gp = gp_sc[...]
        gnrm_ref[...] += dot(gp, assemble(w_refs, w_sc, at_ref, plan), 1, 1)
        deal(dot(nrmt_ref[...], gp), keep_ref, send_ref, d_sc, at_ref)

    @pl.when(step == groups + 1)
    def _():
        tri = lower(BLOCK).astype(f32)
        glam = glam_ref[...] - zs_sc[...]
        rows = []
        for b in range(blocks):
            s = block_of(b)
            end = jnp.sum(zs_sc[s], axis=0, keepdims=True) + over_sc[b : b + 1]
            rows.append(dot(tri, glam[s], 0, 0, precision=PRECISE) + end)
        back = jnp.concatenate(rows, axis=0)
        dt = dt_ref[...]
        gz = (gdt_sc[...] + rate_ref[...] * back) * sig_ref[...]
        gsmall_ref[0:1] = jnp.sum(gz, axis=0, keepdims=True)
        gsmall_ref[1:2] = rate_ref[...] * jnp.sum(dt * back, axis=0, keepdims=True)
        gsmall_ref[2:8] = jnp.zeros((6, STATE), f32)
        low = gz.astype(bf16)
        heads = groups * PER
        w = assemble(w_refs, w_sc, at_ref, plan)[:, :STATE]
        w = jnp.where(iota(w.shape, 1) < heads, w, jnp.zeros((), bf16))
        gnrm_ref[:length] += dot(low, w, 1, 1)
        dw = dot(nrmt_ref[:, :length], low)
        deal(jnp.concatenate([dw, jnp.zeros_like(dw)], axis=1), keep_ref, send_ref, d_sc, at_ref)
        gnrm = gnrm_ref[...]
        edge_ref[...] = gnrm[length:]
        out_ref[...] = gnrm[:length]
        ngain = jnp.sum(gnrm[length:] * rim_ref[...].astype(f32), axis=0, keepdims=True)
        ngain = ngain + jnp.sum(gnrm[:length] * nrm_ref[...].astype(f32), axis=0, keepdims=True)
        ngain_ref[...] = ngain / gain_ref[...]


def last(
    after, at, layout, slots, rest_at, gxd, cv, cin, gy, dt, lam, sig, starts, gend, later, s0, fresh, dec, nrmt, glam, gbc,
    gin, skip, rate, cw, rim, nrm, gain,
):
    length, inner = gy.shape
    d, ext = nrmt.shape
    blocks = length // BLOCK
    groups = inner // TILE
    heads = inner // HEADDIM
    taps = cw.shape[0]
    full = lambda *shape: pl.BlockSpec(shape, lambda s: (0,) * len(shape))
    own = lambda s: jnp.minimum(s, groups - 1)
    col = lambda s: jnp.minimum(s, groups)
    tile = pl.BlockSpec((length, TILE), lambda s: (0, own(s)))
    state = pl.BlockSpec((TILE, STATE), lambda s: (own(s), 0))
    states = pl.BlockSpec((blocks - 1, TILE, STATE), lambda s: (0, own(s), 0))
    return pl.pallas_call(
        functools.partial(last_kernel, slots.plan, len(after)),
        grid=(groups + 2,),
        in_specs=[
            SMEM,
            *[pl.BlockSpec(memory_space=pl.ANY)] * len(after),
            *slots.tiles(lambda s: rest_at + s),
            tile,
            pl.BlockSpec((length, TILE), lambda s: (0, col(s))),
            pl.BlockSpec((ext, TILE), lambda s: (0, col(s))),
            tile,
            pl.BlockSpec((length, TILE), lambda s: (0, groups)),
            full(length, STATE),
            full(length, STATE),
            full(length, STATE),
            full(length, 1),
            state,
            states,
            state,
            states,
            full(8, STATE),
            full(d, ext),
            full(length, STATE),
            full(length, 2 * STATE),
            full(length, d),
            pl.BlockSpec((1, TILE), lambda s: (0, own(s))),
            full(1, STATE),
            pl.BlockSpec((taps, TILE), lambda s: (0, col(s))),
            full(RIM, d),
            full(length, d),
            full(1, d),
        ],
        out_specs=[
            full(RIM, d),
            full(length, d),
            pl.BlockSpec((taps, TILE), lambda s: (0, col(s))),
            pl.BlockSpec((1, TILE), lambda s: (0, col(s))),
            full(8, STATE),
            full(1, d),
            *layout.dealt(lambda s: s),
        ],
        out_shape=[
            jax.ShapeDtypeStruct((RIM, d), f32),
            jax.ShapeDtypeStruct((length, d), f32),
            jax.ShapeDtypeStruct((taps, inner + 2 * STATE), f32),
            jax.ShapeDtypeStruct((1, inner + 2 * STATE), f32),
            jax.ShapeDtypeStruct((8, STATE), f32),
            jax.ShapeDtypeStruct((1, d), f32),
            *layout.dealt_shape(layout.rows, inner + 2 * STATE + heads),
        ],
        scratch_shapes=[
            pltpu.VMEM((length, STATE), bf16),
            pltpu.VMEM((length, STATE), f32),
            pltpu.VMEM((length, 2 * STATE), bf16),
            pltpu.VMEM((length, 2 * STATE), bf16),
            pltpu.VMEM((length, STATE), f32),
            pltpu.VMEM((length, STATE), f32),
            pltpu.VMEM((8, STATE), f32),
            pltpu.VMEM((ext, TILE), bf16),
            layout.scratch(TILE),
            layout.scratch(TILE),
            pltpu.VMEM((ext, d), f32),
        ],
        compiler_params=pltpu.CompilerParams(vmem_limit_bytes=VMEM),
        cost_estimate=NO_COST,
        name="last",
    )(
        jnp.concatenate([slots.near, at]), *after, *slots.arrays, gxd, cv, cin, gy, cv, dt, lam, sig, starts, gend, later, s0, fresh, dec, nrmt,
        glam, gbc, gin, skip, rate, cw, rim, nrm, gain,
    )


def norm_back_kernel(grad_ref, gnrm_ref, rim_ref, resid_ref, gain_ref, *refs):
    out_ref, low_ref = refs[-2:]
    rows, width = out_ref.shape
    gnrm = gnrm_ref[...]
    last = pl.program_id(0) == pl.num_programs(0) - 1
    more = jnp.where(last, rim_ref[...], 0.0)
    gnrm = jnp.concatenate([gnrm[: rows - RIM], gnrm[rows - RIM :] + more], axis=0)
    resid = resid_ref[...].astype(f32)
    scale = lax.rsqrt(jnp.mean(resid * resid, axis=1, keepdims=True) + EPSILON)
    scaled = gnrm * gain_ref[...]
    inner = jnp.sum(scaled * resid, axis=1, keepdims=True)
    total = grad_ref[...].astype(f32) + scale * scaled - resid * (inner * scale * scale * scale / width)
    out_ref[...] = total
    low_ref[...] = total.astype(bf16)


def norm_back(grad, gnrm, rim, resid, gain, after=()):
    length, width = grad.shape
    rows = 128
    block = pl.BlockSpec((rows, width), lambda s: (s, 0))
    fixed = lambda n: pl.BlockSpec((n, width), lambda s: (0, 0))
    return pl.pallas_call(
        norm_back_kernel,
        grid=(length // rows,),
        in_specs=[block, block, fixed(RIM), block, fixed(1)]
        + [pl.BlockSpec(memory_space=pl.ANY)] * len(after),
        out_specs=[block, block],
        out_shape=[
            jax.ShapeDtypeStruct((length, width), f32),
            jax.ShapeDtypeStruct((length, width), bf16),
        ],
        compiler_params=pltpu.CompilerParams(vmem_limit_bytes=VMEM),
        cost_estimate=NO_COST,
        name="norm_back",
    )(grad, gnrm, rim, resid, gain, *after)


def passed_along(shard, axis, by):
    devices = lax.axis_size(axis)
    pairs = [(i, i + by) for i in range(devices) if 0 <= i + by < devices]
    return lax.ppermute(shard, axis, pairs)


def swap(value, axis, by):
    return lax.ppermute(value, axis, [(i, i ^ by) for i in range(lax.axis_size(axis))])


def decay_of(ref, at):
    return ref[at : at + 1].astype(f32) + ref[at + 1 : at + 2].astype(f32)


def joint_kernel(reverse, at_ref, mine_ref, other_ref, *refs):
    sent_ref = refs[-1]
    half = sent_ref.shape[0] - RIM
    odd = at_ref[1] % 2
    mine, other = decay_of(mine_ref, 2 * half), decay_of(other_ref, 2 * half)
    by = jnp.where((odd == 1) == reverse, other, mine)
    for g in range(half // TILE):
        rows = pl.ds(pl.multiple_of(odd * half + g * TILE, TILE), TILE)
        here, there = mine_ref[rows].astype(f32), other_ref[rows].astype(f32)
        first = jnp.where((odd == 1) == reverse, here, there)
        second = jnp.where((odd == 1) == reverse, there, here)
        scale = head_rows(by, odd * (half // TILE) + g)
        sent_ref[g * TILE : (g + 1) * TILE] = (scale * first + second).astype(bf16)
    sent_ref[half:] = decay_rows(mine * other)


def entering_kernel(reverse, pairs, at_ref, *refs):
    got, out_ref = refs[: pairs - 1], refs[-1]
    half = out_ref.shape[0]
    odd, chip = at_ref[1] % 2, at_ref[1] // 2
    decays = [decay_of(a, half) for a in got]
    shares = []
    for i in range(1, pairs):
        source = chip ^ i
        counts = source > chip if reverse else source < chip
        share = jnp.where(counts, jnp.ones((1, STATE), f32), 0.0)
        for j in range(1, pairs):
            if j != i:
                by = chip ^ j
                inside = (by < source) & (by > chip) if reverse else (by > source) & (by < chip)
                share = jnp.where(inside, share * decays[j - 1], share)
        shares.append(share)
    for g in range(half // TILE):
        rows = slice(g * TILE, (g + 1) * TILE)
        total = None
        for share, a in zip(shares, got):
            part = head_rows(share, odd * (half // TILE) + g) * a[rows].astype(f32)
            total = part if total is None else total + part
        out_ref[rows] = total.astype(bf16)


def behind_kernel(reverse, at_ref, half_ref, rest_ref, other_ref, out_ref):
    half = half_ref.shape[0]
    odd = at_ref[1] % 2
    decay = decay_of(other_ref, 2 * half)
    for g in range(2 * half // TILE):
        rows = slice(g * TILE, (g + 1) * TILE)
        upper = g * TILE >= half
        short = slice(rows.start % half, rows.start % half + TILE)
        own = (odd == 1) == upper
        value = jnp.where(own, half_ref[short].astype(f32), rest_ref[short].astype(f32))
        later = head_rows(decay, g) * value + other_ref[rows].astype(f32)
        out_ref[rows] = jnp.where((odd == 1) != reverse, later, value)


def small_call(kernel, at, args, shapes, after=(), name=None):
    args = list(args) + list(after)
    count = len(args) - len(after)
    vmem = pl.BlockSpec(memory_space=pltpu.VMEM)
    return pl.pallas_call(
        kernel,
        in_specs=[SMEM] + [vmem] * count + [pl.BlockSpec(memory_space=pl.ANY)] * len(after),
        out_specs=[vmem] * len(shapes),
        out_shape=shapes,
        compiler_params=pltpu.CompilerParams(vmem_limit_bytes=VMEM),
        cost_estimate=NO_COST,
        name=name,
    )(at, *args)


def carried_over(here, state, reverse, meanwhile):
    pairs = lax.axis_size("seq") // 2
    rows = state.shape[0] - RIM
    other = swap(state, "seq", 1)
    sent_shape = jax.ShapeDtypeStruct((rows // 2 + RIM, STATE), bf16)
    (sent,) = small_call(
        functools.partial(joint_kernel, reverse), here, [state, other], [sent_shape], name="joint"
    )
    got = [swap(sent, "seq", 2 * i) for i in range(1, pairs)]
    beside = meanwhile(sent)
    half_shape = jax.ShapeDtypeStruct((rows // 2, STATE), bf16)
    (half,) = small_call(
        functools.partial(entering_kernel, reverse, pairs), here, got, [half_shape],
        after=[beside[0]], name="entering",
    )
    rest = swap(half, "seq", 1)
    (whole,) = small_call(
        functools.partial(behind_kernel, reverse), here, [half, rest, other],
        [jax.ShapeDtypeStruct((rows, STATE), f32)], name="behind",
    )
    return whole, beside, half


def cut_kernel(inner, at_ref, in_ref, out_ref, rest_ref, *targets):
    rows, share, width = rest_ref.shape[0], in_ref.shape[2], out_ref.shape[2]
    for layer, target in enumerate(targets):

        @pl.when(pl.program_id(0) == layer)
        def _():
            pick = iota((rows, share), 1) == rows * at_ref[1] + iota((rows, share), 0)
            pick = pick.astype(f32).astype(bf16)
            rest = dot(pick, in_ref[0, inner:], 1, 1).astype(bf16)
            if layer == 0:
                rest_ref[...] = rest
            else:
                target[:, 2 * inner :] = rest
            target[:, :inner] = dot(pick, in_ref[0, :inner], 1, 1).astype(bf16)
            for f in range(inner // width):
                part = out_ref[0, f * rows : (f + 1) * rows]
                target[:, inner + f * width : inner + (f + 1) * width] = part


def cut(at, layout, in_turned, out_weight):
    layers, wide, share = in_turned.shape
    width = out_weight.shape[2]
    rows = layout.rows
    fold = out_weight.shape[1] // share
    inner = fold * width
    shapes = [
        jax.ShapeDtypeStruct((rows, n), bf16)
        for n in (wide - inner, 2 * inner, *[wide + inner] * (layers - 1))
    ]
    return pl.pallas_call(
        functools.partial(cut_kernel, inner),
        grid_spec=pltpu.PrefetchScalarGridSpec(
            num_scalar_prefetch=1,
            grid=(layers,),
            in_specs=[
                pl.BlockSpec((1, wide, share), lambda s, at_ref: (s, 0, 0)),
                pl.BlockSpec((1, fold * rows, width), lambda s, at_ref: (s, at_ref[1], 0)),
            ],
            out_specs=[pl.BlockSpec(a.shape, lambda s, at_ref: (0, 0)) for a in shapes],
        ),
        out_shape=shapes,
        compiler_params=pltpu.CompilerParams(vmem_limit_bytes=VMEM),
        cost_estimate=NO_COST,
        name="cut",
    )(at, in_turned, out_weight)


X, Y = 2, 4


def over_wa(piece, layout):
    return [piece] + [swap(piece, "wa", q) for q in range(1, layout.owners)]


def stack_kernel(count, *refs):
    for i in range(count):
        refs[-1][0, i] = refs[i][...]


def stack(pieces, after=()):
    vmem = pl.BlockSpec(memory_space=pltpu.VMEM)
    return pl.pallas_call(
        functools.partial(stack_kernel, len(pieces)),
        in_specs=[vmem] * len(pieces) + [pl.BlockSpec(memory_space=pl.ANY)] * len(after),
        out_specs=vmem,
        out_shape=jax.ShapeDtypeStruct((1, len(pieces), *pieces[0].shape), pieces[0].dtype),
        compiler_params=pltpu.CompilerParams(vmem_limit_bytes=VMEM),
        cost_estimate=NO_COST,
        name="stack",
    )(*pieces, *after)


def straight(here, pieces, after=()):
    return across(here, stack(pieces, after))


def across(near, own):
    arrays = [own] + [swap(own, "seq", by) for by in (X, Y, X + Y)]
    return Slots(near, arrays, [((r,), 0) for r in (0, X, Y, X + Y)])


def near_by(slots, after=()):
    arrays = [tie(a, after) if after else a for a in slots.arrays]
    return Slots(
        slots.near, arrays + [swap(a, "seq", 1) for a in arrays],
        slots.plan + tuple((tuple(r + 1 for r in places), owner) for places, owner in slots.plan),
    )


def like_cores(layout):
    places, owners = layout.places, layout.owners
    return [
        [p * owners + w for p in range(near, places, 2) for w in range(owners)] for near in (0, 1)
    ]


def tie(value, after):
    def kernel(*refs):
        pass

    return pl.pallas_call(
        kernel,
        in_specs=[pl.BlockSpec(memory_space=pl.ANY)] * (1 + len(after)),
        out_specs=pl.BlockSpec(memory_space=pl.ANY),
        out_shape=jax.ShapeDtypeStruct(value.shape, value.dtype),
        input_output_aliases={0: 0},
        cost_estimate=NO_COST,
        name="tie",
    )(value, *after)


def pack_kernel(count, rows, *refs):
    outs = refs[-4:]
    at = 0
    for k in range(count):
        keeps, gots = refs[4 * k : 4 * k + 2], refs[4 * k + 2 : 4 * k + 4]
        width = keeps[0].shape[-1]
        for f in range(keeps[0].shape[2] // rows):
            s = slice(f * rows, (f + 1) * rows)
            for part, pairs in ((0, ((0, 2), (1, 3))), (1, ((0, 1), (2, 3)))):
                for place, target in zip(pairs, outs[2 * part : 2 * part + 2]):
                    for n, i in enumerate(place):
                        total = keeps[part][i, 0, s].astype(f32) + gots[part][i, 0, s].astype(f32)
                        target[n, 0, :, at : at + width] = total.astype(bf16)
            at += -(-width // STATE) * STATE


def pack(parts, layout, after=()):
    half = layout.owners // 2
    flat, specs = [], []
    for pair in parts:
        for a in pair:
            block = (a.shape[0], 1, *a.shape[2:])
            flat += [a, a]
            specs += [
                pl.BlockSpec(block, lambda q: (0, q, 0, 0)),
                pl.BlockSpec(block, lambda q: (0, half + q, 0, 0)),
            ]
    width = 0
    for keep, _ in parts:
        width = -(-width // STATE) * STATE + keep.shape[2] // layout.rows * keep.shape[3]
    out = jax.ShapeDtypeStruct((2, half, layout.rows, width), bf16)
    return pl.pallas_call(
        functools.partial(pack_kernel, len(parts), layout.rows),
        grid=(half,),
        in_specs=specs + [pl.BlockSpec(memory_space=pl.ANY)] * len(after),
        out_specs=[pl.BlockSpec((2, 1, layout.rows, width), lambda q: (0, q, 0, 0))] * 4,
        out_shape=[out] * 4,
        compiler_params=pltpu.CompilerParams(vmem_limit_bytes=VMEM),
        cost_estimate=NO_COST,
        name="pack",
    )(*flat, *after)


def small_rows(layer_shapes):
    table = []
    for k, shape in enumerate(layer_shapes):
        for at in range(0, shape[1], STATE):
            table.append((k, shape[0], at))
    return sorted(table, key=lambda entry: -entry[1])


def deal_small_kernel(table, arrays, at_ref, *refs):
    keep_ref, send_ref, all_sc = refs[arrays : arrays + 3]
    places, rows, width = all_sc.shape
    all_sc[...] = jnp.zeros_like(all_sc)
    row = 0
    for k, count, at in table:
        all_sc[row // rows, row % rows : row % rows + count] = refs[k][:count, at : at + width]
        row += count
    for r in range(places):
        target = send_ref if r % 2 else keep_ref
        part = all_sc[at_ref[1] ^ r].astype(bf16)
        for q in range(target.shape[1]):
            target[r // 2, q] = part


def deal_small(here, values, layout):
    shapes = [(min(a.shape[0], 4), a.shape[1]) for a in values]
    table = small_rows(shapes)
    assert sum(entry[1] for entry in table) <= layout.places * layout.rows
    shape = jax.ShapeDtypeStruct((layout.places // 2, layout.owners, layout.rows, STATE), bf16)
    vmem = pl.BlockSpec(memory_space=pltpu.VMEM)
    return pl.pallas_call(
        functools.partial(deal_small_kernel, table, len(values)),
        in_specs=[SMEM] + [vmem] * len(values),
        out_specs=[vmem, vmem],
        out_shape=[shape, shape],
        scratch_shapes=[pltpu.VMEM((layout.places, layout.rows, STATE), f32)],
        compiler_params=pltpu.CompilerParams(vmem_limit_bytes=VMEM),
        cost_estimate=NO_COST,
        name="deal_small",
    )(here, *values)


def place_small_kernel(table, shapes, at_ref, even_ref, odd_ref, *refs):
    count = len(shapes)
    outs, all_sc, row_scs = refs[:-1 - count], refs[-1 - count], refs[-count:]
    pairs, rows = even_ref.shape[:2]
    for i in range(pairs):
        all_sc[(2 * i) ^ at_ref[1]] = even_ref[i].astype(f32)
        all_sc[(2 * i + 1) ^ at_ref[1]] = odd_ref[i].astype(f32)
    row = 0
    for k, n, at in table:
        row_scs[k][:n, at : at + STATE] = all_sc[row // rows, row % rows : row % rows + n]
        row += n
    each = len(shapes) // outs[0].shape[0]

    def share(k, width):
        whole = row_scs[k][...]
        return pltpu.roll(whole, lax.rem(whole.shape[1] - width * at_ref[0], whole.shape[1]), 1)

    for layer in range(outs[0].shape[0]):
        cw, cb, heads, gain_in, gain_gated, skip = range(each * layer, each * layer + each)
        outs[0][layer] = share(cw, outs[0].shape[2])[:4, : outs[0].shape[2]]
        one = slice(layer, layer + 1)
        outs[1][one] = share(cb, outs[1].shape[1])[:1, : outs[1].shape[1]]
        per = outs[2].shape[1]
        two = share(heads, per)
        outs[2][one] = two[1:2, :per]
        outs[3][one] = two[:1, :per]
        outs[4][one] = share(skip, per)[:1, :per]
        outs[5][one] = share(gain_in, outs[5].shape[1])[:1, : outs[5].shape[1]]
        outs[6][one] = share(gain_gated, outs[6].shape[1])[:1, : outs[6].shape[1]]


def place_small(here, even, odd, values, shapes, layout):
    sizes = [(min(a.shape[0], 4), a.shape[1]) for a in values]
    table = small_rows(sizes)
    vmem = pl.BlockSpec(memory_space=pltpu.VMEM)
    block = (layout.places // 2, layout.rows, STATE)
    last = even.shape[2] // STATE - 1
    return pl.pallas_call(
        functools.partial(place_small_kernel, table, sizes),
        grid=(1,),
        in_specs=[SMEM] + [pl.BlockSpec(block, lambda s: (0, 0, last))] * 2,
        out_specs=[vmem] * len(shapes),
        out_shape=[jax.ShapeDtypeStruct(shape, f32) for shape in shapes],
        scratch_shapes=[pltpu.VMEM((layout.places, layout.rows, STATE), f32)]
        + [pltpu.VMEM((8, width), f32) for _, width in sizes],
        compiler_params=pltpu.CompilerParams(vmem_limit_bytes=VMEM),
        cost_estimate=NO_COST,
        name="place_small",
    )(here, even, odd)


def pair_kernel(count, rows, *refs):
    target = refs[-1]
    at = 0
    for k in range(count):
        keep, got = refs[2 * k : 2 * k + 2]
        width = keep.shape[-1]
        for f in range(keep.shape[2] // rows):
            s = slice(f * rows, (f + 1) * rows)
            total = keep[:, 0, s].astype(f32) + got[:, 0, s].astype(f32)
            target[:, 0, :, at : at + width] = total.astype(bf16)
            at += width


def pair_sums(parts, layout, after=()):
    flat = [a for pair in parts for a in pair]
    width = sum(keep.shape[2] // layout.rows * keep.shape[3] for keep, _ in parts)
    pairs = layout.places // 2
    return pl.pallas_call(
        functools.partial(pair_kernel, len(parts), layout.rows),
        grid=(layout.owners,),
        in_specs=[pl.BlockSpec((pairs, 1, *a.shape[2:]), lambda q: (0, q, 0, 0)) for a in flat]
        + [pl.BlockSpec(memory_space=pl.ANY)] * len(after),
        out_specs=pl.BlockSpec((pairs, 1, layout.rows, width), lambda q: (0, q, 0, 0)),
        out_shape=jax.ShapeDtypeStruct((pairs, layout.owners, layout.rows, width), bf16),
        compiler_params=pltpu.CompilerParams(vmem_limit_bytes=VMEM),
        cost_estimate=NO_COST,
        name="pair_sums",
    )(*flat, *after)


def halve_kernel(*refs):
    outs = refs[-4:]
    for part in (0, 1):
        keep, got = refs[2 * part : 2 * part + 2]
        for n in (0, 1):
            total = keep[n].astype(f32) + got[n].astype(f32)
            outs[2 * part + n][...] = total.astype(bf16)


def halve(arrays, after=()):
    two, half, rows, width = arrays[0].shape
    return pl.pallas_call(
        halve_kernel,
        grid=(half,),
        in_specs=[pl.BlockSpec((2, 1, rows, width), lambda q: (0, q, 0, 0))] * 4
        + [pl.BlockSpec(memory_space=pl.ANY)] * len(after),
        out_specs=[pl.BlockSpec((1, rows, width), lambda q: (q, 0, 0))] * 4,
        out_shape=[jax.ShapeDtypeStruct((half, rows, width), bf16)] * 4,
        compiler_params=pltpu.CompilerParams(vmem_limit_bytes=VMEM),
        cost_estimate=NO_COST,
        name="halve",
    )(*arrays, *after)


def apart_kernel(owners, at_ref, *refs):
    outs = refs[-owners:]
    half = owners // 2
    for q in range(owners):
        keep, got = refs[:2] if q < half else refs[2:4]
        outs[q][...] = (keep[q % half].astype(f32) + got[q % half].astype(f32)).astype(bf16)


def sum_kernel(count, at_ref, *refs):
    total = refs[0][...].astype(f32)
    for a in refs[1:count]:
        total = total + a[...].astype(f32)
    refs[-1][...] = total.astype(bf16)


class Collect:
    def __init__(self, here, layout):
        self.here, self.layout, self.parts = here, layout, {}

    def add(self, order, keep, send, after=()):
        if after:
            send = tie(send, after)
        self.parts[order] = (keep, swap(send, "seq", 1))
        return self.parts[order][1]

    def pack(self, *after):
        parts = [self.parts[k] for k in sorted(self.parts)]
        keep_a, send_a, keep_b, send_b = pack(parts, self.layout, after)
        self.now = [keep_a, swap(send_a, "seq", X), keep_b, swap(send_b, "seq", Y)]

    def halve(self, *after):
        keep_a, send_a, keep_b, send_b = halve(self.now, after)
        self.now = [keep_a, swap(send_a, "seq", Y), keep_b, swap(send_b, "seq", X)]

    def apart(self, *after):
        owners = self.layout.owners
        shape = jax.ShapeDtypeStruct(self.now[0].shape[1:], bf16)
        out = small_call(
            functools.partial(apart_kernel, owners), self.here, self.now, [shape] * owners, after,
            name="apart",
        )
        self.now = [out[0]] + [swap(out[q], "wa", q) for q in range(1, owners)]

    def whole(self, *after):
        shape = jax.ShapeDtypeStruct(self.now[0].shape, bf16)
        (own,) = small_call(
            functools.partial(sum_kernel, len(self.now)), self.here, self.now, [shape], after,
            name="whole",
        )
        self.now = [own]

    def at_once(self, *after):
        places, owners = self.layout.places, self.layout.owners
        parts = [self.parts[k] for k in sorted(self.parts)]
        self.pairs = pair_sums(parts, self.layout, after)
        total = self.pairs
        total = total.reshape(places // 2 * owners, *total.shape[2:])
        like = like_cores(self.layout)
        self.now = [lax.psum_scatter(total, ("seq", "wa"), axis_index_groups=like)]

    def gathered(self, *after):
        self.now = [lax.all_gather(tie(self.now[0], after), "seq")]

    def spread(self, *after):
        own = tie(self.now[0], after) if after else self.now[0]
        even = jnp.stack([own] + [swap(own, "seq", by) for by in (X, Y, X + Y)])
        self.now = [even, swap(even, "seq", 1)]


WIDE = 1024


def place_kernel(ins, sources, given, at_ref, steps_ref, *refs):
    found, outs, own_sc = refs[:sources], refs[sources + given : -1], refs[-1]
    if sources == 1:
        value = found[0][...].astype(f32)
    else:
        for i in range(found[0].shape[0]):
            own_sc[(2 * i) ^ at_ref[1]] = found[0][i]
            own_sc[(2 * i + 1) ^ at_ref[1]] = found[1][i]
        value = own_sc[...].astype(f32)
    if ins:
        @pl.when(pl.program_id(0) < ins)
        def _():
            outs[0][0] = value.reshape(-1, WIDE).T

    if len(outs) > (ins > 0):
        @pl.when(pl.program_id(0) >= ins)
        def _():
            outs[-1][0, :, 0] = value


def place(at, layer, found, parts, outs, shapes, layout):
    rows = layout.rows
    sources, in_tiles, out_tiles = [], [], []
    ins = sum(count for inside, _, count, _ in parts if inside)
    for inside, source, count, target in parts:
        sources += range(source, source + count)
        (in_tiles if inside else out_tiles).extend(range(target, target + count))
    steps = len(sources)
    in_tiles = in_tiles + (in_tiles[-1:] or [0]) * (steps - len(in_tiles))
    out_tiles = (out_tiles[:1] or [0]) * (steps - len(out_tiles)) + out_tiles
    table = jnp.array([sources, in_tiles, out_tiles], jnp.int32)
    across = shapes[1][-1] // WIDE
    both = [
        pl.BlockSpec((1, WIDE, shapes[0][2]), lambda s, at_ref, t: (layer, t[1, s], 0)),
        pl.BlockSpec(
            (1, layout.places, 1, rows, WIDE),
            lambda s, at_ref, t: (layer, 0, t[2, s] // across, 0, t[2, s] % across),
        ),
    ]
    used = [i for i, needed in enumerate((ins > 0, ins < steps)) if needed]
    given = [outs[i] for i in used if outs[i] is not None]
    source = pl.BlockSpec((found[0].shape[0], rows, WIDE), lambda s, at_ref, t: (0, 0, t[0, s]))
    made = pl.pallas_call(
        functools.partial(place_kernel, ins, len(found), len(given)),
        grid_spec=pltpu.PrefetchScalarGridSpec(
            num_scalar_prefetch=2,
            grid=(steps,),
            in_specs=[source] * len(found) + [pl.BlockSpec(memory_space=pl.ANY)] * len(given),
            out_specs=[both[i] for i in used],
            scratch_shapes=[pltpu.VMEM((layout.places, rows, WIDE), bf16)],
        ),
        out_shape=[jax.ShapeDtypeStruct(shapes[i], f32) for i in used],
        input_output_aliases={2 + len(found) + i: i for i in range(len(given))},
        compiler_params=pltpu.CompilerParams(vmem_limit_bytes=VMEM),
        cost_estimate=NO_COST,
        name="place",
    )(at, table, *found, *given)
    outs = list(outs)
    for i, a in zip(used, made):
        outs[i] = a
    return outs


def lanes(row):
    return jnp.pad(row, (0, STATE - row.shape[0]))[None]


def local(
    tokens,
    in_weight,
    out_weight,
    conv_weight,
    conv_bias,
    a_log,
    dt_bias,
    skip_d,
    norm_gain,
    gated_gain,
    doc_start,
    cotangent,
):
    layers = in_weight.shape[0]
    length, width = tokens.shape[1:]
    taps, channels = conv_weight.shape[1:]
    owners = lax.axis_size("wa")
    heads = a_log.shape[1] * owners
    inner = heads * HEADDIM
    starts = (doc_start[0] - lax.axis_index("seq") * length)[:, None]

    devices = lax.axis_size("seq")
    rows = in_weight.shape[1] // devices
    here = jnp.stack([lax.axis_index("wa"), lax.axis_index("seq")]).astype(jnp.int32)
    fold = inner // width
    dealing = devices == 2 * Y and owners > 1 and owners & (owners - 1) == 0 and rows % RIM == 0
    weights = []
    if dealing:
        layout = Layout(owners, devices, rows)
        at = here
        in_turned = in_weight.swapaxes(1, 2)
        pieces = cut(at, layout, in_turned, out_weight)
        first_column = over_wa(pieces[0], layout)
        early = straight(here, first_column)
        column = over_wa(pieces[1], layout)
        late = straight(here, column, early.arrays[1:])
        weights.append((near_by(early), 0, late))
        next_own = lax.all_gather(tie(pieces[2], column[1:]), "wa")[None]
        straight_place = jnp.stack([jnp.zeros_like(here[0]), here[1]])
        assert layers == 2
    else:
        layout = Layout(owners, 1, in_weight.shape[1])
        at = jnp.zeros((2,), jnp.int32)
        for layer in range(layers):
            out = out_weight[layer].reshape(fold, layout.rows, width).swapaxes(0, 1)
            out = out.reshape(layout.rows, fold * width)
            gate, rest = in_weight[layer][:, :inner], in_weight[layer][:, inner:]
            found = [
                Slots(at, [lax.all_gather(part, "wa")[None]], [((0,), 0)])
                for part in (rest, jnp.concatenate([gate, out], axis=1))
            ]
            weights.append((found[0], 0, found[1]))
    own_small = [
        conv_weight.reshape(layers, taps * channels), conv_bias, a_log, dt_bias, skip_d,
        norm_gain, gated_gain,
    ]
    small = jnp.concatenate(own_small, axis=1)
    if dealing:
        small = tie(small, weights[0][0].arrays[:1])
    if owners & (owners - 1) == 0:
        small = jnp.stack([small] + [swap(small, "wa", q) for q in range(1, owners)])
        small = jnp.take(small, jnp.arange(owners) ^ lax.axis_index("wa"), axis=0).astype(f32)
    else:
        small = lax.all_gather(small, "wa", axis=0).astype(f32)
    sizes = [a.shape[1] for a in own_small]
    params = []
    for layer in range(layers):
        found, col = [], 0
        for i, size in enumerate(sizes):
            part = small[:, layer, col : col + size]
            col += size
            if i == 0:
                part = part.reshape(owners, taps, channels).swapaxes(0, 1)
                found.append(part.reshape(taps, owners * channels))
            else:
                found.append(part.reshape(owners * size))
        params.append(found)

    resid = tokens[0]
    start = resid.astype(f32)
    normed = (
        start
        * lax.rsqrt(jnp.mean(start * start, axis=1, keepdims=True) + EPSILON)
        * params[0][5]
    ).astype(bf16)
    records = []
    for layer in range(layers):
        cw, cb, alog, dtb, skip, ngain, ggain = params[layer]
        rate = lanes(-jnp.exp(alog))
        skip_row = jnp.repeat(skip, HEADDIM)[None]
        if dealing and layer > 0:
            split = inner + fold * width
            found = across(straight_place, tie(next_own[..., split:], [beside_out]))
            late = across(straight_place, tie(next_own[..., :split], found.arrays[1:]))
            weights.append((near_by(found, [normed]), 0, late))
        early, rest_at, late = weights[layer]
        rim = passed_along(normed[length - RIM :], "seq", 1)
        nrm = normed
        cin, cv, dt, lam, sig, lamt, state, fresh, dec, nrmt = first(
            layout, rim, nrm, early, rest_at, cw, cb[None], lanes(dtb), rate, starts, heads
        )
        y = within(cv, dt, lam, lamt, starts, skip_row)
        if dealing:
            state = tie(state, [*late.arrays[1:], y])
        s0, _, entered = carried_over(here, state, False, lambda sent: [sent])
        if dealing:
            late = near_by(late, [entered] if layer else ())
            weights[layer] = (early, 0, late)
        beside_out = s0 if not dealing else entered
        gain_next = params[min(layer + 1, layers - 1)][5][None]
        gate, y, gated, scale, resid_next, low, normed = join(
            layout, late, 0, 1, nrm, y, cv, lam, starts, s0, fresh, dec, ggain[None], resid, gain_next
        )
        records.append(
            (resid, cin, cv, dt, lam, sig, lamt, fresh, dec, nrmt, s0, gate, y, gated, scale,
             rate, skip_row, rim, nrm)
        )
        resid = resid_next
    result = low[None]
    grad_low = cotangent[0]
    grad = grad_low
    big = [None] * layers
    little = [None] * layers
    for layer in reversed(range(layers)):
        cw, cb, alog, dtb, skip, ngain, ggain = params[layer]
        early, rest_at, late = weights[layer]
        (resid, cin, cv, dt, lam, sig, lamt, fresh, dec, nrmt, s0, gate, y, gated, scale,
         rate, skip_row, first_rim, nrm) = records[layer]
        top = layer == layers - 1
        to = at
        if dealing and top:
            to = jnp.stack([jnp.zeros_like(at[0]), at[1] % 2])
        gy, ggate, gggain, gskip, later, total, *dwo = gate_back(
            [upper.pairs] if dealing and not top else (), to, layout, late, 1, grad_low, y, gate, gated, scale, ggain[None], cv, lam, starts,
            dec,
        )
        if dealing and top:
            upper = Collect(here, layout)
            upper.add(1, *dwo)
        elif dealing:
            under = Collect(here, layout)
            under.add(1, *dwo)

        def beside(sent):
            return within_back(
                (), to, layout, late, 0, gy, cv, dt, lam, lamt, starts, s0, fresh, dec, ggate, nrmt
            )

        gend, (gxd, glam, gbc, gnrm_gate, *dw_gate), entered = carried_over(
            here, total, True, beside
        )
        if dealing and top:
            upper.add(0, *dw_gate, [entered])
        elif dealing:
            under.add(0, *dw_gate, [entered, under.parts[1][1]])
            under.pack()
        edge, gnrm, gcw, gcb, gsmall, gngain, *dw_rest = last(
            under.now[:1] if dealing and not top else (), to, layout, early, rest_at, gxd, cv, cin, gy, dt, lam, sig, starts, gend, later, s0,
            fresh, dec, nrmt, glam, gbc, gnrm_gate, skip_row, rate, cw, first_rim, nrm,
            ngain[None],
        )
        if dealing and top:
            upper.add(2, *dw_rest, [upper.parts[0][1], upper.parts[1][1]])
        elif dealing:
            under.halve(gsmall)
            tail = Collect(here, layout)
            tail.add(0, *dw_rest, [under.now[0]])
            edge = tie(edge, [under.now[0]])
        rim = passed_along(edge, "seq", -1)
        if layer > 0 or not dealing:
            grad, grad_low = norm_back(grad, gnrm, rim, resid, ngain[None])
        if dealing and top:
            upper.at_once(grad_low)
        big[layer] = (dw_gate, dwo, dw_rest)
        little[layer] = (gcw, gcb, gsmall[:2], gngain, gggain, gskip)

    in_width, rest = in_weight.shape[2], in_weight.shape[2] - inner
    if dealing:
        assert layers == 2
        values = [a for layer in range(layers) for a in little[layer]]
        tail.add(1, *deal_small(here, values, layout))
        tail.pack()
        under.apart(tail.now[0])
        tail.halve(under.now[0])
        upper.gathered(tail.now[0])
        grad, _ = norm_back(grad, gnrm, rim, resid, ngain[None], tail.now[:1])
        both = [(layers, in_width, in_weight.shape[1]), (layers, layout.places, fold, layout.rows, width)]
        tiles = inner // WIDE
        more = -(-rest // WIDE)
        tail.apart(grad)
        under.whole(tail.now[0])
        under.spread()
        made = place(
            at, 1, upper.now,
            ((True, 0, tiles, 0), (True, 2 * tiles, more, tiles), (False, tiles, tiles, 0)),
            [None, None], both, layout,
        )
        tail.whole(made[0])
        tail.spread()
        made = place(
            at, 0, under.now, ((True, 0, tiles, 0), (False, tiles, tiles, 0)), made, both, layout
        )
        made = place(at, 0, tail.now, ((True, 0, more, tiles),), made, both, layout)
        in_grad = made[0].swapaxes(1, 2)
        out_grad = made[1].reshape(out_weight.shape)
        found = place_small(
            here, *tail.now, values, [a.shape for a in (conv_weight, conv_bias, a_log, dt_bias, skip_d, norm_gain, gated_gain)], layout
        )
    else:

        def owned(part):
            part = part.reshape(owners, -1, part.shape[-1])
            part = lax.psum_scatter(part, "wa", scatter_dimension=0)
            return lax.psum(part, "seq").astype(f32)

        in_grad = jnp.stack(
            [
                jnp.concatenate([owned(big[layer][0][0]), owned(big[layer][2][0])], axis=1)
                for layer in range(layers)
            ]
        )
        out_grad = jnp.stack([owned(big[layer][1][0]) for layer in range(layers)])
        rows = []
        for gcw, gcb, two, gngain, gggain, gskip in little:
            gcw = gcw.reshape(taps, owners, channels).swapaxes(0, 1).reshape(owners, -1)
            flat = (gcb[0], two[1, :heads], two[0, :heads], gskip[0, :heads], gngain[0], gggain[0])
            rows.append(jnp.concatenate([gcw] + [a.reshape(owners, -1) for a in flat], axis=1))
        mine = lax.dynamic_index_in_dim(
            lax.psum(jnp.stack(rows, axis=1), ("wa", "seq")), lax.axis_index("wa"), 0, keepdims=False
        )
        found, col = [], 0
        for i, size in enumerate(sizes):
            part = mine[:, col : col + size]
            col += size
            found.append(part.reshape(layers, taps, channels) if i == 0 else part)
    return (result, grad[None], in_grad, out_grad, *found)


def solution(mesh):
    in_specs = (
        P("wa", "seq", None),
        P(None, "wa", None),
        P(None, "wa", None),
        P(None, None, "wa"),
        P(None, "wa"),
        P(None, "wa"),
        P(None, "wa"),
        P(None, "wa"),
        P(None, "wa"),
        P(None, "wa"),
        P("wa", "seq"),
        P("wa", "seq", None),
    )
    out_specs = (
        P("wa", "seq", None),
        P("wa", "seq", None),
        P(None, "wa", None),
        P(None, "wa", None),
        P(None, None, "wa"),
        P(None, "wa"),
        P(None, "wa"),
        P(None, "wa"),
        P(None, "wa"),
        P(None, "wa"),
        P(None, "wa"),
    )
    return jax.shard_map(local, mesh=mesh, in_specs=in_specs, out_specs=out_specs, check_vma=False)
```
